32 devices in a mesh: seq: 8 (over y, x, core), req: 4 (over z).
Axes of the slice: x: 2, y: 2, z: 4, core: 2. Of those that a mesh axis runs over, the one named last changes fastest.
Arguments:
- x_in: bfloat16 [24, 4, 1536], P('req'), may hold values from -6 to 6
- attn_gain: float32 [1536], replicated, may hold values from 0.25 to 1.75
- moe_gain: float32 [1536], replicated, may hold values from 0.25 to 1.75
- w_qkv: bfloat16 [1536, 2560], P(None, 'seq'), may hold values from -0.15625 to 0.15625
- w_o: bfloat16 [1536, 1536], P(None, 'seq'), may hold values from -0.3125 to 0.3125
- cache_k: bfloat16 [24, 1024, 512], P('req', 'seq'), may hold values from -1024 to 1024
- cache_v: bfloat16 [24, 1024, 512], P('req', 'seq'), may hold values from -6 to 6
- page_map: int32 [24, 64], P('req', 'seq'), may hold values from 0 to 63, as said below
- lengths: int32 [24], P('req'), may hold values from 2 to 1024, as said below
- routes: int32 [24, 4, 8], P('req'), may hold values from 0 to 31, all different within a row; in each aligned block of 24 rows (0 to 23, 24 to 47, ..., all dimensions but the last counted through in order) at most 12 rows name the same one
- route_weights: float32 [24, 4, 8], P('req'), may hold values from 0.1 to 1
- w_gate_up: bfloat16 [32, 1536, 1024], P('seq', 'req'), may hold values from -0.15625 to 0.15625
- w_down: bfloat16 [32, 512, 1536], P('seq', None, 'req'), may hold values from -0.375 to 0.375
Outputs:
- layer_out: bfloat16 [24, 4, 1536], P('req', None, 'seq')
The draws below stay inside these ranges and needn't reach their ends.
Inputs may be any that keep to these rules, and one draw needn't show every extreme that they name: `lengths`: every index of req holds one request with exactly 1024 cached positions. `page_map`: each row is a permutation of the request's 64 logical pages. `routes`: A token names 8 different experts. Among the 24 tokens of one index of req no expert is named more than 12 times.
All inputs are finite; a program needn't handle non-finite values.
Results may differ from the reference program's by a relative error of at most 0.01.
Values may be sent and summed in bfloat16 or wider, within the bound.
No kernel may reach another device: no remote copies, remote signals or barrier semaphores. Data moves between devices by JAX's collectives and lax.ppermute only.
A program may use at most 64 MiB of HBM per device.

```python
import math
import jax
import jax.numpy as jnp
import numpy as np
from jax import lax

D = 1536
HEADS = 24
KVH = 8
HD = 64
FFE = 512
EXPERTS = 32
TOP = 8
NSTEP = 4
PAGE = 16
REQ_DEV = 6
R = 24
ROWS_G = 24
NPAGES = 64
MAXLEN = 1024
ATT = 1536
KVD = 512
QKV = 2560
GROUP = 3
CAP = 12
N_REQ = 4


def page_table(key):
    keys = jax.random.split(jax.random.fold_in(key, 11), R)
    return jax.vmap(lambda single: jax.random.permutation(single, NPAGES))(keys).astype(jnp.int32)


def draw_page_map(key, part):
    return page_table(key)


def draw_lengths(key, part):
    key_one, key_two, key_three, key_pick = jax.random.split(jax.random.fold_in(key, 21), 4)
    upper = MAXLEN - 2
    first = jax.random.randint(key_one, (R,), 0, upper)
    second = jax.random.randint(key_two, (R,), 0, upper)
    third = jax.random.randint(key_three, (R,), 0, upper)
    blended = first * second // MAXLEN
    blended = blended * third // MAXLEN
    picked = jax.random.randint(key_pick, (N_REQ,), 0, REQ_DEV)
    indices = jnp.arange(R, dtype=jnp.int32)
    full_length = indices % REQ_DEV == jnp.repeat(picked, REQ_DEV)
    return jnp.where(full_length, MAXLEN, 2 + blended).astype(jnp.int32)


def draw_cache_k(key, part):
    key_base = jax.random.fold_in(jax.random.fold_in(key, 31), 0)
    values = jnp.clip(jax.random.normal(key_base, (R, MAXLEN, KVD), jnp.float32), -6.0, 6.0)
    return values.astype(jnp.bfloat16)


def shard_levels(key, extent, shards, smallest, largest):
    def one(dim, parts):
        draws = jax.random.uniform(jax.random.fold_in(jax.random.fold_in(key, 6), dim), (parts,), jnp.float32, smallest / len(shards), largest / len(shards))
        return jnp.repeat(jnp.exp(draws), extent[dim] // parts).reshape((-1,) + (1,) * (len(extent) - dim - 1))

    loudness = one(*shards[0])
    for cut in shards[1:]:
        loudness = loudness * one(*cut)
    return loudness


def shared_out(rng, own, number, rows, amount, top, reach, skew):
    sequence = jax.random.permutation(rng, amount)
    crowded, common = portions_of(amount, rows * top, reach, skew, True), portions_of(amount, rows * top, reach, skew, False)
    places = jnp.arange(amount)

    def named(tallies, rotation):
        used = int((tallies > 0).sum())
        fixed = max(1, used // 4)
        shifted = fixed + (places - fixed + rotation * (used - fixed)) % max(1, amount - fixed)
        return jnp.zeros((amount,), jnp.int32).at[sequence[jnp.where(places < fixed, places, shifted)]].set(jnp.asarray(tallies, jnp.int32))

    tallies = jnp.where(number % 4 == 0, named(crowded, number // 4), named(common, number - number // 4 - 1))
    mixed = jax.random.permutation(jax.random.fold_in(own, 3), amount)
    giver, receiver = mixed[0:amount // 2 * 2:2], mixed[1:amount // 2 * 2:2]
    room = jnp.minimum(tallies[giver] - 1, reach - tallies[receiver]) // 2
    room = jnp.where((giver == sequence[0]) | (receiver == sequence[0]) | (tallies[receiver] == 0), 0, jnp.maximum(room, 0))
    shifted = jax.random.randint(jax.random.fold_in(own, 4), (amount // 2,), 0, 1 << 20) % (room + 1)
    tallies = tallies.at[giver].add(-shifted).at[receiver].add(shifted)
    labels = jnp.searchsorted(jnp.cumsum(tallies), jnp.arange(rows * top), side="right").astype(jnp.int32)
    listing = labels.reshape(top, rows).T
    listing = listing[jax.random.permutation(jax.random.fold_in(own, 1), rows)]
    rotation = jax.random.randint(jax.random.fold_in(own, 2), (rows, 1), 0, top)
    return jnp.take_along_axis(listing, (jnp.arange(top)[None, :] + rotation) % top, axis=1)


def portions_of(count, total, most, skew, full):
    portions = [(1 << 20) // math.isqrt(rank ** skew) + 1 for rank in range(1, count + 1)]
    largest = most if full else min(most, max(-(-total // count), total * portions[0] // sum(portions)))
    least = 1 if total - largest >= count - 1 else 0
    holding, surplus = [largest] + [least] * (count - 1), total - largest - least * (count - 1)
    while surplus > 0:
        free = [i for i in range(1, count) if holding[i] < largest] or [i for i in range(1, count) if holding[i] < most]
        pool, budget = sum([portions[i] for i in free]), surplus
        for i in free:
            extra = min(most - holding[i], max(1, budget * portions[i] // pool), surplus)
            holding[i] = holding[i] + extra
            surplus = surplus - extra
    return np.array(holding)


def bell_draw(own_key, dims, deviation, most, shards=(), kind=jnp.bfloat16):
    array = deviation * jax.random.normal(own_key, dims, jnp.float32)
    if shards:
        array = array * shard_levels(own_key, dims, shards, -0.22, 0.18)
    return jnp.clip(array, -most, most).astype(kind)


def setup_inputs(seed: int = 0) -> dict:
    seeds = jax.random.split(jax.random.key(seed), 14)
    x_in = bell_draw(seeds[0], (R, NSTEP, D), 1.0, 6.0, ((0, 4),))
    attn_gain = jnp.clip(1.0 + 0.15 * jax.random.normal(seeds[1], (D,), jnp.float32), 0.25, 1.75)
    moe_gain = jnp.clip(1.0 + 0.15 * jax.random.normal(seeds[2], (D,), jnp.float32), 0.25, 1.75)
    w_qkv = bell_draw(seeds[3], (D, QKV), D ** -0.5, 0.15625, ((1, 8),))
    w_o = bell_draw(seeds[4], (ATT, D), (ATT // 4) ** -0.5, 0.3125, ((1, 8),))
    cache_k = draw_cache_k(jax.random.fold_in(seeds[13], 71), 0)
    cache_v = bell_draw(seeds[6], (R, MAXLEN, KVD), 1.0, 6.0, ((0, 4), (1, 8)))
    page_map = draw_page_map(jax.random.fold_in(seeds[13], 71), 0)
    lengths = draw_lengths(jax.random.fold_in(seeds[13], 71), 0)
    routes_keys = jax.random.split(jax.random.fold_in(seeds[9], 1), R * NSTEP // ROWS_G)
    routes_turns = jax.random.permutation(jax.random.fold_in(seeds[9], 3), R * NSTEP // ROWS_G)
    routes = jax.vmap(lambda own, number: shared_out(jax.random.fold_in(seeds[9], 2), own, number, ROWS_G, EXPERTS, TOP, CAP, 1))(routes_keys, routes_turns).reshape((R, NSTEP, TOP))
    route_weights = jnp.clip(jnp.exp(math.log(1.0) - 2.3025851 * jax.random.uniform(seeds[10], (R, NSTEP, TOP), jnp.float32) ** shard_levels(seeds[10], (R, NSTEP, TOP), ((0, 4),), -0.2, 0.2)), 0.1, 1.0)
    w_gate_up = bell_draw(seeds[11], (EXPERTS, D, 2 * FFE), D ** -0.5, 0.15625, ((0, 8), (1, 4)))
    w_down = bell_draw(seeds[12], (EXPERTS, FFE, D), (FFE // 2) ** -0.5, 0.375, ((0, 8), (2, 4)))
    return {"x_in": x_in, "attn_gain": attn_gain, "moe_gain": moe_gain, "w_qkv": w_qkv, "w_o": w_o, "cache_k": cache_k, "cache_v": cache_v, "page_map": page_map, "lengths": lengths, "routes": routes, "route_weights": route_weights, "w_gate_up": w_gate_up, "w_down": w_down}


EPS = 1e-05
NEG = -1e+30

def normalize(values, gain):
    power = lax.optimization_barrier(jnp.mean(values * values, axis=-1, keepdims=True))
    return values * lax.rsqrt(power + EPS) * gain

def rotate(values, position):
    half = values.shape[-1] // 2
    rates = jnp.exp(jnp.arange(half, dtype=jnp.float32) * (-2.0 * math.log(10000.0) / values.shape[-1]))
    angle = position[..., None, None] * rates
    cosine = jnp.cos(angle)
    sine = jnp.sin(angle)
    first_half = values[..., :half]
    second_half = values[..., half:]
    return jnp.concatenate([first_half * cosine - second_half * sine, second_half * cosine + first_half * sine], axis=-1)

def reference(x_in, attn_gain, moe_gain, w_qkv, w_o, cache_k, cache_v, page_map, lengths, routes, route_weights, w_gate_up, w_down):
    requests = x_in.shape[0]
    row_count = requests * NSTEP
    inputs = x_in.astype(jnp.float32).reshape(row_count, D)
    normed = normalize(inputs, attn_gain).astype(jnp.bfloat16)
    projected = jnp.dot(normed, w_qkv, preferred_element_type=jnp.float32)
    queries = projected[:, :ATT].reshape(requests, NSTEP, HEADS, HD)
    keys_new = projected[:, ATT:ATT + KVD].reshape(requests, NSTEP, KVH, HD)
    values_new = projected[:, ATT + KVD:].reshape(requests, NSTEP, KVH, HD).astype(jnp.bfloat16)
    position = (lengths[:, None] + jnp.arange(NSTEP, dtype=jnp.int32)[None, :]).astype(jnp.float32)
    queries = rotate(queries, position).astype(jnp.bfloat16)
    keys_new = rotate(keys_new, position).astype(jnp.bfloat16)
    offsets = jnp.arange(PAGE, dtype=jnp.int32)
    causal = jnp.arange(NSTEP, dtype=jnp.int32)[:, None] >= jnp.arange(NSTEP, dtype=jnp.int32)[None, :]
    scale = HD ** (-0.5)

    def attend(items):
        query, key_fresh, value_fresh, keys, values, pages, length = items
        query = query.astype(jnp.float32).reshape(NSTEP, KVH, GROUP, HD)
        keys = keys.astype(jnp.float32).reshape(MAXLEN, KVH, HD)
        values = values.astype(jnp.float32).reshape(MAXLEN, KVH, HD)
        slot_position = (pages[:, None] * PAGE + offsets[None, :]).reshape(MAXLEN)
        live = slot_position < length
        cached = jnp.einsum('skgd,tkd->skgt', query, keys) * scale
        cached = jnp.where(live[None, None, None, :], cached, NEG)
        fresh = jnp.einsum('skgd,ukd->skgu', query, key_fresh.astype(jnp.float32)) * scale
        fresh = jnp.where(causal[:, None, None, :], fresh, NEG)
        highest = jnp.maximum(lax.optimization_barrier(jnp.max(cached, axis=-1)), lax.optimization_barrier(jnp.max(fresh, axis=-1)))
        cached_exp = jnp.exp(cached - highest[..., None])
        fresh_exp = jnp.exp(fresh - highest[..., None])
        denominator = lax.optimization_barrier(jnp.sum(cached_exp, axis=-1)) + lax.optimization_barrier(jnp.sum(fresh_exp, axis=-1))
        cached_probs = lax.optimization_barrier(cached_exp.astype(jnp.bfloat16)).astype(jnp.float32)
        fresh_probs = lax.optimization_barrier(fresh_exp.astype(jnp.bfloat16)).astype(jnp.float32)
        numerator = jnp.einsum('skgt,tkd->skgd', cached_probs, values)
        numerator = numerator + jnp.einsum('skgu,ukd->skgd', fresh_probs, value_fresh.astype(jnp.float32))
        return (numerator / denominator[..., None]).reshape(NSTEP, ATT).astype(jnp.bfloat16)
    attended = lax.map(attend, (queries, keys_new, values_new, cache_k, cache_v, page_map, lengths))
    attended = attended.reshape(row_count, ATT)
    resid = inputs + jnp.dot(attended, w_o, preferred_element_type=jnp.float32)
    mixed_in = normalize(resid, moe_gain).astype(jnp.bfloat16)
    chosen = routes.reshape(row_count, TOP)
    gates = route_weights.reshape(row_count, TOP)
    expert_ids = jnp.arange(EXPERTS, dtype=jnp.int32)
    weight_table = lax.optimization_barrier(jnp.sum(jnp.where(chosen[:, :, None] == expert_ids[None, None, :], gates[:, :, None], 0.0), axis=1))

    def expert_step(carry, items):
        weight_in, weight_out, share = items
        gate_up = jnp.dot(mixed_in, weight_in, preferred_element_type=jnp.float32)
        hidden = (jax.nn.silu(gate_up[:, :FFE]) * gate_up[:, FFE:]).astype(jnp.bfloat16)
        produced = jnp.dot(hidden, weight_out, preferred_element_type=jnp.float32)
        return (carry + share[:, None] * produced, None)
    total_mix, unused = lax.scan(expert_step, jnp.zeros((row_count, D), jnp.float32), (w_gate_up, w_down, weight_table.T))
    return (resid + total_mix).astype(jnp.bfloat16).reshape(requests, NSTEP, D)
```

```python
import math

import jax
import jax.numpy as jnp
from jax import lax
from jax.experimental import pallas as pl
from jax.experimental.pallas import tpu as pltpu
from jax.sharding import PartitionSpec as P

D = 1536
HEADS = 24
KVH = 8
HD = 64
FFE = 512
TOP = 8
NSTEP = 4
PAGE = 16
ATT = 1536
KVD = 512
GROUP = 3
CAP = 12


EPS = 1e-05
NEG = -1e30


def combined_all(value, axis, join):
    pieces = jax.tree.map(lambda part: lax.all_gather(part, axis), value)
    head = jax.tree.map(lambda part: part[0], pieces)
    tail = jax.tree.map(lambda part: part[1:], pieces)
    so_far, _ = lax.scan(lambda so_far, piece: (join(so_far, piece), None), head, tail)
    return so_far


def normalize(values, gain):
    power = jnp.mean(values * values, axis=-1, keepdims=True)
    return values * lax.rsqrt(power + EPS) * gain


def rotate(values, position):
    half = values.shape[-1] // 2
    rates = jnp.exp(
        jnp.arange(half, dtype=jnp.float32) * (-2.0 * math.log(10000.0) / values.shape[-1])
    )
    angle = position[..., None, None] * rates
    cosine = jnp.cos(angle)
    sine = jnp.sin(angle)
    first_half = values[..., :half]
    second_half = values[..., half:]
    return jnp.concatenate(
        [first_half * cosine - second_half * sine, second_half * cosine + first_half * sine],
        axis=-1,
    )


def softmax_join(left, right):
    left_top, left_total, left_sums = left
    right_top, right_total, right_sums = right
    highest = jnp.maximum(left_top, right_top)
    left_factor = jnp.exp(left_top - highest)
    right_factor = jnp.exp(right_top - highest)
    row_count, head_count = highest.shape
    left_part = left_sums.reshape(row_count, head_count, -1) * left_factor[:, :, None]
    right_part = right_sums.reshape(row_count, head_count, -1) * right_factor[:, :, None]
    joined = (left_part + right_part).reshape(row_count, -1)
    return (highest, left_total * left_factor + right_total * right_factor, joined)


def project_with(left, piece):
    return jnp.dot(left, piece, preferred_element_type=jnp.float32)


def plain(
    x_in,
    attn_gain,
    moe_gain,
    w_qkv,
    w_o,
    cache_k,
    cache_v,
    page_map,
    lengths,
    routes,
    route_weights,
    w_gate_up,
    w_down,
):
    local_requests = x_in.shape[0]
    row_count = local_requests * NSTEP
    inputs = x_in.astype(jnp.float32).reshape(row_count, D)
    normed = normalize(inputs, attn_gain).astype(jnp.bfloat16)
    projected = project_with(normed, lax.all_gather(w_qkv, "seq", axis=1, tiled=True))
    queries = projected[:, :ATT].reshape(local_requests, NSTEP, HEADS, HD)
    keys_new = projected[:, ATT : ATT + KVD].reshape(local_requests, NSTEP, KVH, HD)
    values_new = (
        projected[:, ATT + KVD :].reshape(local_requests, NSTEP, KVH, HD).astype(jnp.bfloat16)
    )
    position = (lengths[:, None] + jnp.arange(NSTEP, dtype=jnp.int32)[None, :]).astype(jnp.float32)
    queries = (
        rotate(queries, position)
        .astype(jnp.bfloat16)
        .reshape(local_requests, NSTEP, KVH, GROUP, HD)
    )
    keys_new = rotate(keys_new, position).astype(jnp.bfloat16)
    scale = HD ** (-0.5)
    slot_count = cache_k.shape[1]
    cached_keys = cache_k.reshape(local_requests, slot_count, KVH, HD)
    cached_values = cache_v.reshape(local_requests, slot_count, KVH, HD)
    slot_position = (
        page_map[:, :, None] * PAGE + jnp.arange(PAGE, dtype=jnp.int32)[None, None, :]
    ).reshape(local_requests, slot_count)
    live = (slot_position < lengths[:, None])[:, None, None, None, :]
    scores = (
        jnp.einsum("rskgd,rtkd->rskgt", queries, cached_keys, preferred_element_type=jnp.float32)
        * scale
    )
    scores = jnp.where(live, scores, NEG)
    local_top = jnp.max(scores, axis=-1)
    exp_scores = jnp.where(live, jnp.exp(scores - local_top[..., None]), 0.0)
    local_total = jnp.sum(exp_scores, axis=-1).reshape(row_count, HEADS)
    local_sums = jnp.einsum(
        "rskgt,rtkd->rskgd",
        exp_scores.astype(jnp.bfloat16),
        cached_values,
        preferred_element_type=jnp.float32,
    ).reshape(row_count, ATT)
    local_top = local_top.reshape(row_count, HEADS)
    cache_top, cache_total, cache_sums = combined_all(
        (local_top, local_total, local_sums), "seq", softmax_join
    )
    causal = (
        jnp.arange(NSTEP, dtype=jnp.int32)[:, None] >= jnp.arange(NSTEP, dtype=jnp.int32)[None, :]
    )[None, :, None, None, :]
    fresh = (
        jnp.einsum("rskgd,rukd->rskgu", queries, keys_new, preferred_element_type=jnp.float32)
        * scale
    )
    fresh = jnp.where(causal, fresh, NEG).reshape(row_count, HEADS, NSTEP)
    highest = jnp.maximum(cache_top, jnp.max(fresh, axis=-1))
    fresh_exp = jnp.exp(fresh - highest[:, :, None])
    carried = jnp.exp(cache_top - highest)
    denominator = cache_total * carried + jnp.sum(fresh_exp, axis=-1)
    fresh_probs = fresh_exp.reshape(local_requests, NSTEP, KVH, GROUP, NSTEP).astype(jnp.bfloat16)
    fresh_sums = jnp.einsum(
        "rskgu,rukd->rskgd", fresh_probs, values_new, preferred_element_type=jnp.float32
    ).reshape(row_count, HEADS, HD)
    numerator = cache_sums.reshape(row_count, HEADS, HD) * carried[:, :, None] + fresh_sums
    attended = (numerator / denominator[:, :, None]).reshape(row_count, ATT).astype(jnp.bfloat16)
    attn_mixed = project_with(attended, lax.all_gather(w_o, "seq", axis=1, tiled=True))
    resid = inputs + attn_mixed
    mixed_in = normalize(resid, moe_gain).astype(jnp.bfloat16)
    local_experts = w_gate_up.shape[0]
    groups = lax.axis_size("req")
    owned = lax.axis_index("seq") * local_experts + jnp.arange(local_experts, dtype=jnp.int32)
    chosen = routes.reshape(row_count, TOP)
    gates = route_weights.reshape(row_count, TOP)
    matches = chosen[None, :, :] == owned[:, None, None]
    routed = jnp.any(matches, axis=-1)
    route_scale = jnp.sum(jnp.where(matches, gates[None, :, :], 0.0), axis=-1)
    ordinal = jnp.cumsum(routed.astype(jnp.int32), axis=1) - 1
    placed = routed[:, :, None] & (
        ordinal[:, :, None] == jnp.arange(CAP, dtype=jnp.int32)[None, None, :]
    )
    outgoing = jnp.einsum(
        "erc,rd->ecd", placed.astype(jnp.bfloat16), mixed_in, preferred_element_type=jnp.float32
    ).astype(jnp.bfloat16)
    arrived = lax.all_to_all(outgoing[:, None], "req", split_axis=3, concat_axis=1, tiled=True)
    slice_width = arrived.shape[3]
    arrived = arrived.reshape(local_experts, groups * CAP, slice_width)
    partial_values = jnp.einsum(
        "end,edf->enf", arrived, w_gate_up, preferred_element_type=jnp.float32
    )
    gate_up = lax.psum(partial_values, "req")
    hidden = (jax.nn.silu(gate_up[..., :FFE]) * gate_up[..., FFE:]).astype(jnp.bfloat16)
    produced = jnp.einsum("enf,efd->end", hidden, w_down, preferred_element_type=jnp.float32)
    returned = lax.all_to_all(
        produced.reshape(local_experts, groups, CAP, slice_width),
        "req",
        split_axis=1,
        concat_axis=3,
        tiled=True,
    )[:, 0]
    weighted = placed.astype(jnp.float32) * route_scale[:, :, None]
    expert_total = jnp.einsum("erc,ecd->rd", weighted, returned, precision=lax.Precision.HIGHEST)
    own_share = lax.psum_scatter(expert_total, "seq", scatter_dimension=1, tiled=True)
    share_width = own_share.shape[1]
    resid_share = lax.dynamic_slice_in_dim(
        resid, lax.axis_index("seq") * share_width, share_width, 1
    )
    return (
        (resid_share + own_share).astype(jnp.bfloat16).reshape(local_requests, NSTEP, share_width)
    )


F32 = jnp.float32
BF16 = jnp.bfloat16
STAT = 128
WIDE = KVD + STAT
VMEM = pl.BlockSpec(memory_space=pltpu.VMEM)
SMEM = pl.BlockSpec(memory_space=pltpu.SMEM)


def kernel_call(body, out_shape, in_specs, scratch=(), vmem_mib=24):
    many = isinstance(out_shape, (list, tuple))
    return pl.pallas_call(
        body,
        out_shape=out_shape,
        in_specs=in_specs,
        out_specs=[VMEM] * len(out_shape) if many else VMEM,
        scratch_shapes=list(scratch),
        compiler_params=pltpu.CompilerParams(vmem_limit_bytes=vmem_mib * 2**20),
    )


def iota(shape, dim):
    return lax.broadcasted_iota(jnp.int32, shape, dim)


def split3(value):
    high = value.astype(BF16).astype(F32)
    rest = value - high
    middle = rest.astype(BF16).astype(F32)
    return high, middle, rest - middle


def rows_of(ref):
    return jnp.concatenate([ref[r].astype(F32) for r in range(ref.shape[0])], axis=0)


def xor_pairs(size, mask):
    return [(i, i ^ mask) for i in range(size)]


def swap(value, axis, mask):
    return lax.ppermute(value, axis, xor_pairs(lax.axis_size(axis), mask))


def project_kernel(
    x_ref, gain_ref, w_ref, cos_ref, sin_ref, routes_ref, weights_ref, me_ref, heads_ref, *pack_refs
):
    x = rows_of(x_ref)
    row_count = x.shape[0]
    power = jnp.mean(x * x, axis=-1, keepdims=True)
    normed = (x * lax.rsqrt(power + EPS) * gain_ref[...]).astype(BF16)
    projected = jnp.dot(normed, w_ref[...], preferred_element_type=F32)
    heads = w_ref.shape[1] // HD
    cosine, sine = cos_ref[...], sin_ref[...]
    for i in range(heads):
        one = projected[:, i * HD : (i + 1) * HD]
        both = jnp.concatenate([one, one], axis=1)
        turned = both * cosine + pltpu.roll(both, HD // 2, 1) * sine
        rotated = me_ref[0] * heads + i < HEADS + KVH
        heads_ref[i] = jnp.where(rotated, turned, both).astype(BF16)
    high, middle, low = split3(rows_of(weights_ref))
    routing = jnp.concatenate(
        [
            rows_of(routes_ref),
            high,
            middle,
            low,
            jnp.zeros((row_count, STAT - 4 * TOP), F32),
        ],
        axis=1,
    )
    groups = len(pack_refs)
    width = D // groups
    for k in range(groups):
        start = pl.multiple_of((me_ref[1] ^ k) * width, STAT)
        part = jnp.concatenate(
            [x_ref[r, :, pl.ds(start, width)].astype(F32) for r in range(x_ref.shape[0])], axis=0
        )
        pack_refs[k][...] = jnp.concatenate([part, routing], axis=1).astype(BF16)


def gathered_heads(me_ref, near_refs, far_refs, all_ref):
    chips = len(near_refs)
    heads = all_ref.shape[2]
    core = me_ref[0] % 2
    chip = me_ref[0] // 2
    for k in range(chips):
        all_ref[core, k] = near_refs[k][...]
        all_ref[1 - core, k] = far_refs[k][...]

    def head(h):
        owner = h // heads
        return all_ref[owner % 2, chip ^ (owner // 2), h % heads].astype(F32)

    return head


def paired(head, left, right):
    a = head(left)
    return jnp.where(iota(a.shape, 1) < HD, a, head(right))


def query_rows(head, q_ref):
    for g in range(GROUP):
        for m in range(KVH // 2):
            q_ref[g, :, m * STAT : (m + 1) * STAT] = paired(
                head, GROUP * 2 * m + g, GROUP * (2 * m + 1) + g
            )


def expanded(q_ref, r):
    rows = [q_ref[g, r * NSTEP : (r + 1) * NSTEP, :] for g in range(GROUP)]
    base = jnp.concatenate(rows + [jnp.zeros((NSTEP, KVD), F32)], axis=0)
    owner = iota(base.shape, 1) // HD
    return jnp.concatenate(
        [jnp.where(owner == k, base, 0.0) for k in range(KVH)], axis=0
    ).astype(BF16)


def attend_part(query, keys, values, live):
    scores = lax.dot_general(
        query, keys, (((1,), (1,)), ((), ())), preferred_element_type=F32
    ) * (HD ** (-0.5))
    scores = jnp.where(live, scores, NEG)
    top = jnp.max(scores, axis=1, keepdims=True)
    exp_scores = jnp.where(live, jnp.exp(scores - top), 0.0)
    total = jnp.sum(exp_scores, axis=1, keepdims=True)
    sums = jnp.dot(exp_scores.astype(BF16), values, preferred_element_type=F32)
    block = (GROUP + 1) * NSTEP
    owner = iota((block, KVD), 1) // HD
    lane = iota((block, STAT), 1)
    own_sums = jnp.zeros((block, KVD), F32)
    stats = jnp.zeros((block, STAT), F32)
    for k in range(KVH):
        rows = slice(k * block, (k + 1) * block)
        own_sums = jnp.where(owner == k, sums[rows], own_sums)
        value = jnp.where(lane < 3 * KVH, top[rows], total[rows])
        stats = jnp.where(lane % KVH == k, value, stats)
    high, middle, low = split3(stats)
    part = (lane // KVH) % 3
    return own_sums, jnp.where(part == 0, high, jnp.where(part == 1, middle, low))


def place_rows(part_ref, r, row_count, own_sums, stats):
    for g in range(GROUP):
        rows = slice(g * row_count + r * NSTEP, g * row_count + (r + 1) * NSTEP)
        part_ref[rows, :KVD] = own_sums[g * NSTEP : (g + 1) * NSTEP]
        part_ref[rows, KVD:] = stats[g * NSTEP : (g + 1) * NSTEP]


def attend_kernel(chips, *refs):
    near_refs, far_refs = refs[:chips], refs[chips : 2 * chips]
    me_ref, pages_ref, lengths_ref, k_ref, v_ref, out_ref, all_ref, q_ref, part_ref = refs[
        2 * chips :
    ]
    head = gathered_heads(me_ref, near_refs, far_refs, all_ref)
    query_rows(head, q_ref)
    requests, slots = k_ref.shape[0], k_ref.shape[1]
    lane = iota((1, slots), 1)
    for r in range(requests):
        page = jnp.zeros((1, slots), jnp.int32)
        for j in range(slots // PAGE):
            page = jnp.where(lane // PAGE == j, pages_ref[r, j], page)
        live = page * PAGE + lane % PAGE < lengths_ref[r]
        own_sums, stats = attend_part(expanded(q_ref, r), k_ref[r], v_ref[r], live)
        place_rows(part_ref, r, requests * NSTEP, own_sums, stats)
    out_ref[...] = part_ref[...].astype(BF16)


def fresh_kernel(chips, *refs):
    near_refs, far_refs = refs[:chips], refs[chips : 2 * chips]
    me_ref, out_ref, all_ref, q_ref, part_ref = refs[2 * chips :]
    head = gathered_heads(me_ref, near_refs, far_refs, all_ref)
    query_rows(head, q_ref)
    row_count = q_ref.shape[1]
    pad = jnp.zeros((STAT - row_count, KVD), F32)

    def new_rows(first):
        pieces = [paired(head, first + 2 * m, first + 2 * m + 1) for m in range(KVH // 2)]
        return jnp.concatenate([jnp.concatenate(pieces, axis=1), pad], axis=0).astype(BF16)

    keys, values = new_rows(HEADS), new_rows(HEADS + KVH)
    shape = ((GROUP + 1) * NSTEP * KVH, STAT)
    slot, step = iota(shape, 1), iota(shape, 0) % NSTEP
    for r in range(row_count // NSTEP):
        live = (slot // NSTEP == r) & (slot % NSTEP <= step)
        own_sums, stats = attend_part(expanded(q_ref, r), keys, values, live)
        place_rows(part_ref, r, row_count, own_sums, stats)
    out_ref[...] = part_ref[...]


def merge_kernel(count, *refs):
    part_refs = refs[:count]
    fresh_ref, x_ref, w_ref, me_ref, out_ref, share_ref = refs[count:]
    parts = [ref[...].astype(F32) for ref in part_refs] + [fresh_ref[...]]
    tops, totals = [], []
    for part in parts:
        stats = part[:, KVD:]
        full = stats + (
            pltpu.roll(stats, STAT - KVH, 1) + pltpu.roll(stats, STAT - 2 * KVH, 1)
        )
        tops.append(full)
        totals.append(pltpu.roll(full, STAT - 3 * KVH, 1))
    highest = tops[0]
    for top in tops[1:]:
        highest = jnp.maximum(highest, top)
    factors = [jnp.exp(top - highest) for top in tops]
    denominator = factors[0] * totals[0]
    for factor, total in zip(factors[1:], totals[1:]):
        denominator = denominator + factor * total
    inverse = 1.0 / denominator
    row_total = parts[0].shape[0]
    left = iota((row_total, STAT), 1) < HD
    columns = []
    for m in range(KVH // 2):
        value = jnp.zeros((row_total, STAT), F32)
        for part, factor in zip(parts, factors):
            spread = jnp.where(left, factor[:, 2 * m : 2 * m + 1], factor[:, 2 * m + 1 : 2 * m + 2])
            value = value + spread * part[:, m * STAT : (m + 1) * STAT]
        spread = jnp.where(left, inverse[:, 2 * m : 2 * m + 1], inverse[:, 2 * m + 1 : 2 * m + 2])
        columns.append(value * spread)
    attended = jnp.concatenate(columns, axis=1)
    out_ref[...] = attended.astype(BF16)
    row_count = row_total // GROUP
    width = w_ref.shape[1]
    share = jnp.zeros((row_count, width), F32)
    for g in range(GROUP):
        share = share + jnp.dot(
            attended[g * row_count : (g + 1) * row_count].astype(BF16),
            group_weight(w_ref, g),
            preferred_element_type=F32,
        )
    start = pl.multiple_of((me_ref[0] // 2) * (2 * width), STAT)
    chunk = jnp.concatenate(
        [x_ref[r, :, pl.ds(start, 2 * width)].astype(F32) for r in range(x_ref.shape[0])], axis=0
    )
    share_ref[...] = share + jnp.where(me_ref[0] % 2 == 0, chunk[:, :width], chunk[:, width:])


def group_weight(w_ref, g):
    return jnp.concatenate(
        [w_ref[(k * GROUP + g) * HD : (k * GROUP + g + 1) * HD, :] for k in range(KVH)], axis=0
    )


def across(column, eye):
    return jnp.sum(jnp.where(eye, column, 0.0), axis=0, keepdims=True)


def gate_kernel(groups, *refs):
    attended_refs, pack_refs = refs[:groups], refs[groups : 2 * groups]
    near_ref, far_ref, gain_ref, w_ref, me_ref = refs[2 * groups : 2 * groups + 5]
    message_refs = refs[2 * groups + 5 : 3 * groups + 5]
    placed_ref, scale_ref, full_ref = refs[3 * groups + 5 :]
    pieces = [ref[...].astype(F32) for ref in attended_refs]
    packs = [ref[...].astype(F32) for ref in pack_refs]
    row_count = packs[0].shape[0]
    tokens = groups * row_count
    width = near_ref.shape[1]
    near = jnp.zeros((tokens, width), F32)
    far = jnp.zeros((tokens, width), F32)
    for g in range(GROUP):
        rows = jnp.concatenate(
            [piece[g * row_count : (g + 1) * row_count] for piece in pieces], axis=0
        ).astype(BF16)
        near = near + jnp.dot(rows, group_weight(near_ref, g), preferred_element_type=F32)
        far = far + jnp.dot(rows, group_weight(far_ref, g), preferred_element_type=F32)
    first = me_ref[0] % 2 == 0
    mixed = jnp.concatenate([jnp.where(first, near, far), jnp.where(first, far, near)], axis=1)
    resid = jnp.concatenate([pack[:, : 2 * width] for pack in packs], axis=0) + mixed
    power = jnp.sum(resid * resid, axis=1, keepdims=True)
    start = pl.multiple_of(me_ref[1] * (2 * width), STAT)
    scaled = (resid * gain_ref[:, pl.ds(start, 2 * width)]).astype(BF16)

    routing = jnp.concatenate([pack[:, 2 * width :] for pack in packs], axis=0)
    chosen = routing[:, :TOP]
    gates = routing[:, TOP : 2 * TOP] + (
        routing[:, 2 * TOP : 3 * TOP] + routing[:, 3 * TOP : 4 * TOP]
    )
    experts = w_ref.shape[0]
    eye = iota((tokens, tokens), 0) == iota((tokens, tokens), 1)
    earlier = (iota((tokens, tokens), 0) < iota((tokens, tokens), 1)) & (
        iota((tokens, tokens), 0) // row_count == iota((tokens, tokens), 1) // row_count
    )
    slots = groups * CAP
    shape = (slots, tokens)
    home = (iota(shape, 1) // row_count) ^ me_ref[1]
    slot = iota(shape, 0)
    same_group = slot // CAP == home
    ordinal_of_slot = (slot % CAP).astype(F32)
    placed, scales = [], []
    for e in range(experts):
        match = chosen == (me_ref[0] * experts + e).astype(F32)
        routed = jnp.max(jnp.where(match, 1.0, 0.0), axis=1, keepdims=True)
        scale = jnp.sum(jnp.where(match, gates, 0.0), axis=1, keepdims=True)
        ordinal = across(routed, earlier)
        here = same_group & (across(routed, eye) > 0.5) & (ordinal_of_slot == ordinal)
        placed.append(jnp.where(here, 1.0, 0.0))
        scales.append(jnp.sum(jnp.where(here, across(scale, eye), 0.0), axis=1, keepdims=True))
    placed = jnp.concatenate(placed, axis=0).astype(BF16)
    placed_ref[...] = placed
    scale_ref[...] = jnp.broadcast_to(jnp.concatenate(scales, axis=0), scale_ref.shape)
    taken = jnp.dot(placed, scaled, preferred_element_type=F32).astype(BF16)
    for e in range(experts):
        full_ref[e * slots : (e + 1) * slots, :] = jnp.dot(
            taken[e * slots : (e + 1) * slots], w_ref[e], preferred_element_type=F32
        )
    parts = split3(across(power, eye))
    row = iota((16, tokens), 0)
    power_rows = jnp.where(
        row == 0, parts[0], jnp.where(row == 1, parts[1], jnp.where(row == 2, parts[2], 0.0))
    ).astype(BF16)
    slot_power = lax.dot_general(
        power_rows, placed, (((1,), (1,)), ((), ())), preferred_element_type=F32
    ).astype(BF16)
    total_slots = experts * slots
    piece = FFE // groups
    for k in range(groups):
        begin = pl.multiple_of((me_ref[1] ^ k) * piece, STAT)
        message_refs[k][:total_slots, :piece] = full_ref[:, pl.ds(begin, piece)].astype(BF16)
        message_refs[k][:total_slots, piece:] = full_ref[:, pl.ds(begin + FFE, piece)].astype(BF16)
        message_refs[k][total_slots:, :total_slots] = slot_power
        message_refs[k][total_slots:, total_slots:] = jnp.zeros(
            (16, 2 * piece - total_slots), BF16
        )


def down_kernel(groups, *refs):
    message_refs = refs[:groups]
    own_ref = refs[groups]
    down_refs = refs[groups + 1 : 2 * groups]
    placed_ref, scale_ref, me_ref = refs[2 * groups : 2 * groups + 3]
    out_refs = refs[2 * groups + 3 :]
    total_slots = placed_ref.shape[0]
    piece = message_refs[0].shape[1] // 2
    summed = message_refs[0][...].astype(F32)
    for ref in message_refs[1:]:
        summed = summed + ref[...].astype(F32)
    stats = summed[total_slots:, :total_slots]
    power = stats[0:1] + (stats[1:2] + stats[2:3])
    eye = iota((total_slots, total_slots), 0) == iota((total_slots, total_slots), 1)
    power = jnp.sum(jnp.where(eye, power, 0.0), axis=1, keepdims=True)
    gate_up = summed[:total_slots] * lax.rsqrt(power / D + EPS)
    gate, up = gate_up[:, :piece], gate_up[:, piece:]
    hidden = (gate / (1.0 + jnp.exp(-gate)) * up).astype(BF16)
    experts = own_ref.shape[0]
    slots = total_slots // experts
    placed = placed_ref[...]
    scale = scale_ref[...][:, :1]
    begin = pl.multiple_of(me_ref[1] * piece, STAT)
    width = own_ref.shape[2]
    row_count = out_refs[0].shape[0]
    for k in range(groups):
        produced = []
        for e in range(experts):
            weight = own_ref[e, pl.ds(begin, piece), :] if k == 0 else down_refs[k - 1][e]
            produced.append(
                jnp.dot(
                    hidden[e * slots : (e + 1) * slots], weight, preferred_element_type=F32
                )
            )
        produced = (jnp.concatenate(produced, axis=0) * scale).astype(BF16)
        total = lax.dot_general(
            placed, produced, (((0,), (0,)), ((), ())), preferred_element_type=F32
        )
        column = pl.multiple_of((me_ref[1] ^ k) * width, STAT)
        for j in range(groups):
            out_refs[j][:, pl.ds(column, width)] = total[
                j * row_count : (j + 1) * row_count
            ].astype(BF16)


def spread_kernel(groups, *refs):
    total = refs[0][...].astype(F32)
    for ref in refs[1:groups]:
        total = total + ref[...].astype(F32)
    out_ref = refs[groups]
    width = out_ref.shape[2]
    for s in range(out_ref.shape[0]):
        out_ref[s] = total[:, s * width : (s + 1) * width].astype(BF16)


def final_kernel(share_ref, arrived_ref, out_ref):
    total = share_ref[...]
    for s in range(arrived_ref.shape[0]):
        total = total + arrived_ref[s].astype(F32)
    for r in range(out_ref.shape[0]):
        out_ref[r] = total[r * NSTEP : (r + 1) * NSTEP].astype(BF16)


def staged(
    x_in,
    attn_gain,
    moe_gain,
    w_qkv,
    w_o,
    cache_k,
    cache_v,
    page_map,
    lengths,
    routes,
    route_weights,
    w_gate_up,
    w_down,
):
    requests = x_in.shape[0]
    row_count = requests * NSTEP
    members, groups = lax.axis_size("seq"), lax.axis_size("req")
    chips = members // 2
    me = jnp.stack([lax.axis_index("seq"), lax.axis_index("req")]).astype(jnp.int32)
    heads = w_qkv.shape[1] // HD
    width = w_o.shape[1]

    position = (lengths[:, None] + jnp.arange(NSTEP, dtype=jnp.int32)[None, :]).astype(F32)
    half = HD // 2
    rates = jnp.exp(jnp.arange(half, dtype=F32) * (-2.0 * math.log(10000.0) / HD))
    angle = position.reshape(row_count, 1) * jnp.tile(rates, STAT // half)[None, :]
    sign = jnp.where(jnp.arange(STAT) % HD < half, -1.0, 1.0).astype(F32)
    cosine, sine = jnp.cos(angle), jnp.sin(angle) * sign[None, :]

    own_heads, *packs = kernel_call(
        project_kernel,
        [jax.ShapeDtypeStruct((heads, row_count, 2 * HD), BF16)]
        + [jax.ShapeDtypeStruct((row_count, 2 * width + STAT), BF16)] * groups,
        [VMEM] * 7 + [SMEM],
    )(x_in, attn_gain[None], w_qkv, cosine, sine, routes, route_weights, me)
    near = [own_heads] + [swap(own_heads, "seq", 2 * k) for k in range(1, chips)]
    far = [swap(piece, "seq", 1) for piece in near]

    packs = [packs[0]] + [swap(packs[k], "req", k) for k in range(1, groups)]
    moved = w_o
    place = ("seq", "req")
    arriving = [
        lax.ppermute(
            w_o,
            place,
            [
                ((2 * z + c) * groups + z, (2 * (z ^ k) + c) * groups + z)
                for z in range(groups)
                for c in range(2)
            ],
        )
        for k in range(1, chips)
    ]
    total = arriving[0]
    for piece in arriving[1:]:
        total = total + piece
    near_w_o = jnp.where(me[0] // 2 == me[1], w_o, total)
    far_w_o = swap(near_w_o, "seq", 1)
    depth = w_down.shape[1] // groups
    downs = [
        swap(lax.dynamic_slice_in_dim(w_down, (me[1] ^ k) * depth, depth, 1), "req", k)
        for k in range(1, groups)
    ]

    head_scratch = [
        pltpu.VMEM((2, chips, heads, row_count, 2 * HD), BF16),
        pltpu.VMEM((GROUP, row_count, KVD), F32),
        pltpu.VMEM((GROUP * row_count, WIDE), F32),
    ]
    part = kernel_call(
        lambda *refs: attend_kernel(chips, *refs),
        jax.ShapeDtypeStruct((GROUP * row_count, WIDE), BF16),
        [VMEM] * (2 * chips) + [SMEM] * 3 + [VMEM] * 2,
        head_scratch,
    )(*near, *far, me, page_map, lengths, cache_k, cache_v)
    fresh = kernel_call(
        lambda *refs: fresh_kernel(chips, *refs),
        jax.ShapeDtypeStruct((GROUP * row_count, WIDE), F32),
        [VMEM] * (2 * chips) + [SMEM],
        head_scratch,
    )(*near, *far, me)
    parts = [part] + [swap(part, "seq", 2 * k) for k in range(1, chips)]
    parts = parts + [swap(piece, "seq", 1) for piece in parts]
    attended, share = kernel_call(
        lambda *refs: merge_kernel(members, *refs),
        [
            jax.ShapeDtypeStruct((GROUP * row_count, KVD), BF16),
            jax.ShapeDtypeStruct((row_count, width), F32),
        ],
        [VMEM] * (members + 3) + [SMEM],
    )(*parts, fresh, x_in, w_o, me)
    everyone = [attended] + [swap(attended, "req", k) for k in range(1, groups)]

    experts = w_gate_up.shape[0]
    total_slots = experts * groups * CAP
    piece = FFE // groups
    *messages, placed, scale = kernel_call(
        lambda *refs: gate_kernel(groups, *refs),
        [jax.ShapeDtypeStruct((total_slots + 16, 2 * piece), BF16)] * groups
        + [
            jax.ShapeDtypeStruct((total_slots, groups * row_count), BF16),
            jax.ShapeDtypeStruct((total_slots, STAT), F32),
        ],
        [VMEM] * (2 * groups + 4) + [SMEM],
        [pltpu.VMEM((total_slots, 2 * FFE), F32)],
    )(*everyone, *packs, near_w_o, far_w_o, moe_gain[None], w_gate_up, me)
    messages = [messages[0]] + [swap(messages[k], "req", k) for k in range(1, groups)]
    outs = kernel_call(
        lambda *refs: down_kernel(groups, *refs),
        [jax.ShapeDtypeStruct((row_count, D), BF16)] * groups,
        [VMEM] * (2 * groups + 2) + [SMEM],
    )(*messages, w_down, *downs, placed, scale, me)
    outs = [outs[0]] + [swap(outs[k], "req", k) for k in range(1, groups)]
    spread = kernel_call(
        lambda *refs: spread_kernel(groups, *refs),
        jax.ShapeDtypeStruct((members, row_count, width), BF16),
        [VMEM] * groups,
    )(*outs)
    arrived = lax.all_to_all(spread, "seq", 0, 0, tiled=True)
    return kernel_call(
        final_kernel, jax.ShapeDtypeStruct((requests, NSTEP, width), BF16), [VMEM] * 2
    )(share, arrived)


def local(*args):
    w_qkv, w_o, page_map, w_gate_up = args[3], args[4], args[7], args[11]
    members, groups = lax.axis_size("seq"), lax.axis_size("req")
    fits = (
        members == 2 * groups
        and groups & (groups - 1) == 0
        and w_qkv.shape[1] % HD == 0
        and (FFE // groups) % STAT == 0
        and (2 * w_o.shape[1]) % STAT == 0
        and w_gate_up.shape[0] * groups * CAP <= 2 * (FFE // groups)
    )
    return staged(*args) if fits else plain(*args)


def solution(mesh):
    in_specs = (
        P("req", None, None),
        P(),
        P(),
        P(None, "seq"),
        P(None, "seq"),
        P("req", "seq", None),
        P("req", "seq", None),
        P("req", "seq"),
        P("req"),
        P("req", None, None),
        P("req", None, None),
        P("seq", "req", None),
        P("seq", None, "req"),
    )
    out_specs = P("req", None, "seq")
    return jax.shard_map(local, mesh=mesh, in_specs=in_specs, out_specs=out_specs, check_vma=False)
```

```python
import math

import jax
import jax.numpy as jnp
from jax import lax
from jax.experimental import pallas as pl
from jax.experimental.pallas import tpu as pltpu
from jax.sharding import PartitionSpec as P

D = 1536
HEADS = 24
KVH = 8
HD = 64
FFE = 512
TOP = 8
NSTEP = 4
PAGE = 16
ATT = 1536
KVD = 512
GROUP = 3
CAP = 12


EPS = 1e-05
NEG = -1e30


def combined_all(value, axis, join):
    pieces = jax.tree.map(lambda part: lax.all_gather(part, axis), value)
    head = jax.tree.map(lambda part: part[0], pieces)
    tail = jax.tree.map(lambda part: part[1:], pieces)
    so_far, _ = lax.scan(lambda so_far, piece: (join(so_far, piece), None), head, tail)
    return so_far


def normalize(values, gain):
    power = jnp.mean(values * values, axis=-1, keepdims=True)
    return values * lax.rsqrt(power + EPS) * gain


def rotate(values, position):
    half = values.shape[-1] // 2
    rates = jnp.exp(
        jnp.arange(half, dtype=jnp.float32) * (-2.0 * math.log(10000.0) / values.shape[-1])
    )
    angle = position[..., None, None] * rates
    cosine = jnp.cos(angle)
    sine = jnp.sin(angle)
    first_half = values[..., :half]
    second_half = values[..., half:]
    return jnp.concatenate(
        [first_half * cosine - second_half * sine, second_half * cosine + first_half * sine],
        axis=-1,
    )


def softmax_join(left, right):
    left_top, left_total, left_sums = left
    right_top, right_total, right_sums = right
    highest = jnp.maximum(left_top, right_top)
    left_factor = jnp.exp(left_top - highest)
    right_factor = jnp.exp(right_top - highest)
    row_count, head_count = highest.shape
    left_part = left_sums.reshape(row_count, head_count, -1) * left_factor[:, :, None]
    right_part = right_sums.reshape(row_count, head_count, -1) * right_factor[:, :, None]
    joined = (left_part + right_part).reshape(row_count, -1)
    return (highest, left_total * left_factor + right_total * right_factor, joined)


def project_with(left, piece):
    return jnp.dot(left, piece, preferred_element_type=jnp.float32)


def plain(
    x_in,
    attn_gain,
    moe_gain,
    w_qkv,
    w_o,
    cache_k,
    cache_v,
    page_map,
    lengths,
    routes,
    route_weights,
    w_gate_up,
    w_down,
):
    local_requests = x_in.shape[0]
    row_count = local_requests * NSTEP
    inputs = x_in.astype(jnp.float32).reshape(row_count, D)
    normed = normalize(inputs, attn_gain).astype(jnp.bfloat16)
    projected = project_with(normed, lax.all_gather(w_qkv, "seq", axis=1, tiled=True))
    queries = projected[:, :ATT].reshape(local_requests, NSTEP, HEADS, HD)
    keys_new = projected[:, ATT : ATT + KVD].reshape(local_requests, NSTEP, KVH, HD)
    values_new = (
        projected[:, ATT + KVD :].reshape(local_requests, NSTEP, KVH, HD).astype(jnp.bfloat16)
    )
    position = (lengths[:, None] + jnp.arange(NSTEP, dtype=jnp.int32)[None, :]).astype(jnp.float32)
    queries = (
        rotate(queries, position)
        .astype(jnp.bfloat16)
        .reshape(local_requests, NSTEP, KVH, GROUP, HD)
    )
    keys_new = rotate(keys_new, position).astype(jnp.bfloat16)
    scale = HD ** (-0.5)
    slot_count = cache_k.shape[1]
    cached_keys = cache_k.reshape(local_requests, slot_count, KVH, HD)
    cached_values = cache_v.reshape(local_requests, slot_count, KVH, HD)
    slot_position = (
        page_map[:, :, None] * PAGE + jnp.arange(PAGE, dtype=jnp.int32)[None, None, :]
    ).reshape(local_requests, slot_count)
    live = (slot_position < lengths[:, None])[:, None, None, None, :]
    scores = (
        jnp.einsum("rskgd,rtkd->rskgt", queries, cached_keys, preferred_element_type=jnp.float32)
        * scale
    )
    scores = jnp.where(live, scores, NEG)
    local_top = jnp.max(scores, axis=-1)
    exp_scores = jnp.where(live, jnp.exp(scores - local_top[..., None]), 0.0)
    local_total = jnp.sum(exp_scores, axis=-1).reshape(row_count, HEADS)
    local_sums = jnp.einsum(
        "rskgt,rtkd->rskgd",
        exp_scores.astype(jnp.bfloat16),
        cached_values,
        preferred_element_type=jnp.float32,
    ).reshape(row_count, ATT)
    local_top = local_top.reshape(row_count, HEADS)
    cache_top, cache_total, cache_sums = combined_all(
        (local_top, local_total, local_sums), "seq", softmax_join
    )
    causal = (
        jnp.arange(NSTEP, dtype=jnp.int32)[:, None] >= jnp.arange(NSTEP, dtype=jnp.int32)[None, :]
    )[None, :, None, None, :]
    fresh = (
        jnp.einsum("rskgd,rukd->rskgu", queries, keys_new, preferred_element_type=jnp.float32)
        * scale
    )
    fresh = jnp.where(causal, fresh, NEG).reshape(row_count, HEADS, NSTEP)
    highest = jnp.maximum(cache_top, jnp.max(fresh, axis=-1))
    fresh_exp = jnp.exp(fresh - highest[:, :, None])
    carried = jnp.exp(cache_top - highest)
    denominator = cache_total * carried + jnp.sum(fresh_exp, axis=-1)
    fresh_probs = fresh_exp.reshape(local_requests, NSTEP, KVH, GROUP, NSTEP).astype(jnp.bfloat16)
    fresh_sums = jnp.einsum(
        "rskgu,rukd->rskgd", fresh_probs, values_new, preferred_element_type=jnp.float32
    ).reshape(row_count, HEADS, HD)
    numerator = cache_sums.reshape(row_count, HEADS, HD) * carried[:, :, None] + fresh_sums
    attended = (numerator / denominator[:, :, None]).reshape(row_count, ATT).astype(jnp.bfloat16)
    attn_mixed = project_with(attended, lax.all_gather(w_o, "seq", axis=1, tiled=True))
    resid = inputs + attn_mixed
    mixed_in = normalize(resid, moe_gain).astype(jnp.bfloat16)
    local_experts = w_gate_up.shape[0]
    groups = lax.axis_size("req")
    owned = lax.axis_index("seq") * local_experts + jnp.arange(local_experts, dtype=jnp.int32)
    chosen = routes.reshape(row_count, TOP)
    gates = route_weights.reshape(row_count, TOP)
    matches = chosen[None, :, :] == owned[:, None, None]
    routed = jnp.any(matches, axis=-1)
    route_scale = jnp.sum(jnp.where(matches, gates[None, :, :], 0.0), axis=-1)
    ordinal = jnp.cumsum(routed.astype(jnp.int32), axis=1) - 1
    placed = routed[:, :, None] & (
        ordinal[:, :, None] == jnp.arange(CAP, dtype=jnp.int32)[None, None, :]
    )
    outgoing = jnp.einsum(
        "erc,rd->ecd", placed.astype(jnp.bfloat16), mixed_in, preferred_element_type=jnp.float32
    ).astype(jnp.bfloat16)
    arrived = lax.all_to_all(outgoing[:, None], "req", split_axis=3, concat_axis=1, tiled=True)
    slice_width = arrived.shape[3]
    arrived = arrived.reshape(local_experts, groups * CAP, slice_width)
    partial_values = jnp.einsum(
        "end,edf->enf", arrived, w_gate_up, preferred_element_type=jnp.float32
    )
    gate_up = lax.psum(partial_values, "req")
    hidden = (jax.nn.silu(gate_up[..., :FFE]) * gate_up[..., FFE:]).astype(jnp.bfloat16)
    produced = jnp.einsum("enf,efd->end", hidden, w_down, preferred_element_type=jnp.float32)
    returned = lax.all_to_all(
        produced.reshape(local_experts, groups, CAP, slice_width),
        "req",
        split_axis=1,
        concat_axis=3,
        tiled=True,
    )[:, 0]
    weighted = placed.astype(jnp.float32) * route_scale[:, :, None]
    expert_total = jnp.einsum("erc,ecd->rd", weighted, returned, precision=lax.Precision.HIGHEST)
    own_share = lax.psum_scatter(expert_total, "seq", scatter_dimension=1, tiled=True)
    share_width = own_share.shape[1]
    resid_share = lax.dynamic_slice_in_dim(
        resid, lax.axis_index("seq") * share_width, share_width, 1
    )
    return (
        (resid_share + own_share).astype(jnp.bfloat16).reshape(local_requests, NSTEP, share_width)
    )


F32 = jnp.float32
BF16 = jnp.bfloat16
STAT = 128
WIDE = KVD + STAT
VMEM = pl.BlockSpec(memory_space=pltpu.VMEM)
HBM = pl.BlockSpec(memory_space=pltpu.HBM)


def kernel_call(body, out_shape, in_specs, scratch=(), out_specs=None, vmem_mib=8, cost=0.5):
    return pl.pallas_call(
        body,
        out_shape=out_shape,
        in_specs=in_specs,
        out_specs=out_specs or ([VMEM] * len(out_shape) if isinstance(out_shape, list) else VMEM),
        scratch_shapes=list(scratch),
        compiler_params=pltpu.CompilerParams(vmem_limit_bytes=vmem_mib * 2**20),
        cost_estimate=pl.CostEstimate(
            flops=int(cost * 1e9), bytes_accessed=int(cost * 3e6), transcendentals=0
        ),
    )


def iota(shape, dim):
    return lax.broadcasted_iota(jnp.int32, shape, dim)


def split3(value):
    high = value.astype(BF16).astype(F32)
    rest = value - high
    middle = rest.astype(BF16).astype(F32)
    return high, middle, rest - middle


def rows_of(ref):
    return jnp.concatenate([ref[r].astype(F32) for r in range(ref.shape[0])], axis=0)


def dot_nt(left, right):
    return lax.dot_general(left, right, (((1,), (1,)), ((), ())), preferred_element_type=F32)


def swap(value, axis, mask):
    pairs = [(i, i ^ mask) for i in range(lax.axis_size(axis))]
    return lax.ppermute(value, axis, pairs)


def after(value, *others):
    return lax.optimization_barrier((value, *others))[0]


def project_kernel(groups, *refs):
    x_hbm, attn_hbm, moe_hbm, w_hbm, lengths_hbm, pages_hbm, routes_hbm, weights_hbm = refs[:8]
    heads_ref, x_ref, live_ref, routing_ref, gain_ref = refs[8:13]
    x_in, attn_gain, moe_gain, w_in, lengths, pages, routes, weights, sem = refs[13:]
    loads = [
        pltpu.make_async_copy(source, target, sem.at[i])
        for i, (source, target) in enumerate(
            [
                (lengths_hbm, lengths),
                (x_hbm, x_in),
                (attn_hbm, attn_gain),
                (w_hbm, w_in),
                (pages_hbm, pages),
                (routes_hbm, routes),
                (weights_hbm, weights),
                (moe_hbm, moe_gain),
            ]
        )
    ]
    for load in loads:
        load.start()
    requests = x_in.shape[0]
    row_count = requests * NSTEP
    shape = (row_count, STAT)
    loads[0].wait()
    row, lane = iota(shape, 0), iota(shape, 1)
    position = row % NSTEP
    for r in range(requests):
        position = position + jnp.where(row // NSTEP == r, lengths[r], 0)
    rates = jnp.exp((lane % (HD // 2)).astype(F32) * (-2.0 * math.log(10000.0) / HD))
    angle = position.astype(F32) * rates
    cosine = jnp.cos(angle)
    sine = jnp.where(lane % HD < HD // 2, -jnp.sin(angle), jnp.sin(angle))
    loads[1].wait()
    x = rows_of(x_in)
    x_ref[...] = x
    power = jnp.mean(x * x, axis=-1, keepdims=True)
    loads[2].wait()
    normed = (x * lax.rsqrt(power + EPS) * attn_gain[...].reshape(1, D)).astype(BF16)
    loads[3].wait()
    projected = dot_nt(normed, w_in[...])
    heads = w_in.shape[0] // HD
    first = lax.axis_index("seq") * heads
    for i in range(heads):
        one = projected[:, i * HD : (i + 1) * HD]
        both = jnp.concatenate([one, one], axis=1)
        turned = both * cosine + pltpu.roll(both, HD // 2, 1) * sine
        heads_ref[i] = jnp.where(first + i < HEADS + KVH, turned, both).astype(BF16)
    for load in loads[4:]:
        load.wait()
    slots = live_ref.shape[1]
    slot = iota((1, slots), 1)
    for r in range(requests):
        page = jnp.zeros((1, slots), jnp.int32)
        for j in range(slots // PAGE):
            page = jnp.where(slot // PAGE == j, pages[r, j], page)
        live = page * PAGE + slot % PAGE < lengths[r]
        live_ref[r : r + 1, :] = jnp.where(live, 1.0, 0.0)
    high, middle, low = split3(rows_of(weights))
    routing_ref[...] = jnp.concatenate(
        [rows_of(routes), high, middle, low, jnp.zeros((row_count, STAT - 4 * TOP), F32)], axis=1
    )
    gain_ref[...] = moe_gain[...].reshape(1, D)


def cut_kernel(groups, down_ref, *refs):
    cut_refs, sem = refs[:-1], refs[-1]
    depth = cut_refs[0].shape[1]
    copies = []
    for k in range(1, groups):
        start = pl.multiple_of((lax.axis_index("req") ^ k) * depth, depth)
        source = down_ref.at[:, pl.ds(start, depth), :]
        copies.append(pltpu.make_async_copy(source, cut_refs[k - 1], sem.at[k - 1]))
        copies[-1].start()
    for copy in copies:
        copy.wait()


def gather_pieces(near_refs, far_refs, all_ref):
    core = lax.axis_index("seq") % 2
    for k in range(len(near_refs)):
        all_ref[core, k] = near_refs[k][...]
        all_ref[1 - core, k] = far_refs[k][...]


def paired(head, left, right):
    a = head(left)
    return jnp.where(iota(a.shape, 1) < HD, a, head(right))


def expanded(q_ref, r):
    rows = [q_ref[g, r * NSTEP : (r + 1) * NSTEP, :] for g in range(GROUP)]
    base = jnp.concatenate(rows + [jnp.zeros((NSTEP, KVD), F32)], axis=0)
    owner = iota(base.shape, 1) // HD
    return jnp.concatenate(
        [jnp.where(owner == k, base, 0.0) for k in range(KVH)], axis=0
    ).astype(BF16)


def attend_part(query, keys, values, live):
    scores = jnp.where(live, dot_nt(query, keys) * (HD ** (-0.5)), NEG)
    top = jnp.max(scores, axis=1, keepdims=True)
    exp_scores = jnp.where(live, jnp.exp(scores - top), 0.0)
    total = jnp.sum(exp_scores, axis=1, keepdims=True)
    return top, total, jnp.dot(exp_scores.astype(BF16), values, preferred_element_type=F32)


def place_rows(part_ref, r, row_count, top, total, sums):
    block = (GROUP + 1) * NSTEP
    owner = iota((block, KVD), 1) // HD
    lane = iota((block, STAT), 1)
    own_sums = jnp.zeros((block, KVD), F32)
    stats = jnp.zeros((block, STAT), F32)
    for k in range(KVH):
        rows = slice(k * block, (k + 1) * block)
        own_sums = jnp.where(owner == k, sums[rows], own_sums)
        value = jnp.where(lane < 3 * KVH, top[rows], total[rows])
        stats = jnp.where(lane % KVH == k, value, stats)
    high, middle, low = split3(stats)
    part = (lane // KVH) % 3
    stats = jnp.where(part == 0, high, jnp.where(part == 1, middle, low))
    for g in range(GROUP):
        rows = slice(g * row_count + r * NSTEP, g * row_count + (r + 1) * NSTEP)
        part_ref[rows, :KVD] = own_sums[g * NSTEP : (g + 1) * NSTEP]
        part_ref[rows, KVD:] = stats[g * NSTEP : (g + 1) * NSTEP]


def head_of(all_ref):
    chip = lax.axis_index("seq") // 2
    heads = all_ref.shape[2]

    def head(h):
        owner = h // heads
        return all_ref[owner % 2, chip ^ (owner // 2), h % heads].astype(F32)

    return head


def query_rows(head, q_ref):
    for g in range(GROUP):
        for m in range(KVH // 2):
            q_ref[g, :, m * STAT : (m + 1) * STAT] = paired(
                head, GROUP * 2 * m + g, GROUP * (2 * m + 1) + g
            )


def attend_kernel(chips, *refs):
    near_refs, far_refs = refs[:chips], refs[chips : 2 * chips]
    live_ref, k_ref, v_ref, out_ref, all_ref, q_ref, part_ref = refs[2 * chips :]
    requests = k_ref.shape[0]
    gather_pieces(near_refs, far_refs, all_ref)
    query_rows(head_of(all_ref), q_ref)
    for r in range(requests):
        live = live_ref[r : r + 1, :] > 0.5
        place_rows(
            part_ref,
            r,
            requests * NSTEP,
            *attend_part(expanded(q_ref, r), k_ref[r], v_ref[r], live),
        )
    out_ref[...] = part_ref[...].astype(BF16)


def fresh_kernel(chips, *refs):
    near_refs, far_refs = refs[:chips], refs[chips : 2 * chips]
    out_ref, all_ref, q_ref, part_ref = refs[2 * chips :]
    gather_pieces(near_refs, far_refs, all_ref)
    head = head_of(all_ref)
    query_rows(head, q_ref)
    row_count = q_ref.shape[1]
    pad = jnp.zeros((STAT - row_count, KVD), F32)

    def new_rows(first):
        pieces = [paired(head, first + 2 * m, first + 2 * m + 1) for m in range(KVH // 2)]
        return jnp.concatenate([jnp.concatenate(pieces, axis=1), pad], axis=0).astype(BF16)

    keys, values = new_rows(HEADS), new_rows(HEADS + KVH)
    shape = ((GROUP + 1) * NSTEP * KVH, STAT)
    slot, step = iota(shape, 1), iota(shape, 0) % NSTEP
    for r in range(row_count // NSTEP):
        live = (slot // NSTEP == r) & (slot % NSTEP <= step)
        place_rows(
            part_ref, r, row_count, *attend_part(expanded(q_ref, r), keys, values, live)
        )
    out_ref[...] = part_ref[...].astype(BF16)


def merge_kernel(count, *refs):
    part_refs = refs[:count]
    x_ref, w_ref, share_ref, resid_ref = refs[count:]
    parts = [ref[...].astype(F32) for ref in part_refs]
    tops, totals = [], []
    for part in parts:
        stats = part[:, KVD:]
        full = stats + (
            pltpu.roll(stats, STAT - KVH, 1) + pltpu.roll(stats, STAT - 2 * KVH, 1)
        )
        tops.append(full)
        totals.append(pltpu.roll(full, STAT - 3 * KVH, 1))
    highest = tops[0]
    for top in tops[1:]:
        highest = jnp.maximum(highest, top)
    factors = [jnp.exp(top - highest) for top in tops]
    denominator = factors[0] * totals[0]
    for factor, total in zip(factors[1:], totals[1:]):
        denominator = denominator + factor * total
    inverse = 1.0 / denominator
    row_total = parts[0].shape[0]
    row_count = row_total // GROUP
    left = iota((row_total, STAT), 1) < HD
    columns = []
    for m in range(KVH // 2):
        value = jnp.zeros((row_total, STAT), F32)
        for part, factor in zip(parts, factors):
            spread = jnp.where(left, factor[:, 2 * m : 2 * m + 1], factor[:, 2 * m + 1 : 2 * m + 2])
            value = value + spread * part[:, m * STAT : (m + 1) * STAT]
        spread = jnp.where(left, inverse[:, 2 * m : 2 * m + 1], inverse[:, 2 * m + 1 : 2 * m + 2])
        columns.append(value * spread)

    def head(h, side):
        k, g = h // GROUP, h % GROUP
        rows = columns[k // 2][g * row_count : (g + 1) * row_count]
        return rows if k % 2 == side else pltpu.roll(rows, HD, 1)

    left = iota((row_count, STAT), 1) < HD
    attended = jnp.concatenate(
        [jnp.where(left, head(2 * n, 0), head(2 * n + 1, 1)) for n in range(HEADS // 2)], axis=1
    ).astype(BF16)
    share = dot_nt(attended, w_ref[...])
    share_ref[...] = share
    width = w_ref.shape[0]
    member = lax.axis_index("seq")
    chunk = x_ref[:, pl.ds(pl.multiple_of((member // 2) * (2 * width), STAT), 2 * width)]
    resid_ref[...] = share + jnp.where(member % 2 == 0, chunk[:, :width], chunk[:, width:])


def mix_kernel(chips, groups, *refs):
    near_refs, far_refs = refs[:chips], refs[chips : 2 * chips]
    x_ref, gain_ref, routing_ref = refs[2 * chips : 2 * chips + 3]
    pack_refs, all_ref, mixed_ref = refs[2 * chips + 3 : -2], refs[-2], refs[-1]
    gather_pieces(near_refs, far_refs, all_ref)
    chip = lax.axis_index("seq") // 2
    attn = jnp.concatenate([all_ref[s % 2, chip ^ (s // 2)] for s in range(2 * chips)], axis=1)
    resid = x_ref[...] + attn
    power = jnp.mean(resid * resid, axis=-1, keepdims=True)
    mixed_ref[...] = resid * lax.rsqrt(power + EPS) * gain_ref[...]
    routing = routing_ref[...]
    width = D // groups
    for k in range(groups):
        start = pl.multiple_of((lax.axis_index("req") ^ k) * width, STAT)
        part = mixed_ref[:, pl.ds(start, width)]
        pack_refs[k][...] = jnp.concatenate([part, routing], axis=1).astype(BF16)


def across(column, eye):
    return jnp.sum(jnp.where(eye, column, 0.0), axis=0, keepdims=True)


def gate_kernel(groups, *refs):
    pack_refs = refs[:groups]
    w_ref = refs[groups]
    message_refs = refs[groups + 1 : 2 * groups + 1]
    placed_ref, scale_ref, full_ref = refs[2 * groups + 1 :]
    first = lax.axis_index("seq") * w_ref.shape[0]
    me = lax.axis_index("req")
    packs = [ref[...].astype(F32) for ref in pack_refs]
    row_count = packs[0].shape[0]
    tokens = groups * row_count
    width = w_ref.shape[1]
    mixed = jnp.concatenate([pack[:, :width] for pack in packs], axis=0).astype(BF16)
    routing = jnp.concatenate([pack[:, width:] for pack in packs], axis=0)
    chosen = routing[:, :TOP]
    gates = routing[:, TOP : 2 * TOP] + (
        routing[:, 2 * TOP : 3 * TOP] + routing[:, 3 * TOP : 4 * TOP]
    )
    experts = w_ref.shape[0]
    square = (tokens, tokens)
    eye = iota(square, 0) == iota(square, 1)
    earlier = (iota(square, 0) < iota(square, 1)) & (
        iota(square, 0) // row_count == iota(square, 1) // row_count
    )
    slots = groups * CAP
    shape = (slots, tokens)
    home = (iota(shape, 1) // row_count) ^ me
    slot = iota(shape, 0)
    same_group = slot // CAP == home
    ordinal_of_slot = (slot % CAP).astype(F32)
    placed, scales = [], []
    for e in range(experts):
        match = chosen == (first + e).astype(F32)
        routed = jnp.max(jnp.where(match, 1.0, 0.0), axis=1, keepdims=True)
        scale = jnp.sum(jnp.where(match, gates, 0.0), axis=1, keepdims=True)
        ordinal = across(routed, earlier)
        here = same_group & (across(routed, eye) > 0.5) & (ordinal_of_slot == ordinal)
        placed.append(jnp.where(here, 1.0, 0.0))
        scales.append(jnp.sum(jnp.where(here, across(scale, eye), 0.0), axis=1, keepdims=True))
    placed = jnp.concatenate(placed, axis=0).astype(BF16)
    placed_ref[...] = placed
    scale_ref[...] = jnp.broadcast_to(jnp.concatenate(scales, axis=0), scale_ref.shape)
    taken = jnp.dot(placed, mixed, preferred_element_type=F32).astype(BF16)
    for e in range(experts):
        full_ref[e * slots : (e + 1) * slots, :] = jnp.dot(
            taken[e * slots : (e + 1) * slots], w_ref[e], preferred_element_type=F32
        )
    piece = FFE // groups
    for k in range(groups):
        begin = pl.multiple_of((me ^ k) * piece, STAT)
        message_refs[k][:, :piece] = full_ref[:, pl.ds(begin, piece)].astype(BF16)
        message_refs[k][:, piece:] = full_ref[:, pl.ds(begin + FFE, piece)].astype(BF16)


def down_kernel(groups, *refs):
    message_refs = refs[:groups]
    own_ref = refs[groups]
    down_refs = refs[groups + 1 : 2 * groups]
    placed_ref, scale_ref = refs[2 * groups : 2 * groups + 2]
    out_refs = refs[2 * groups + 2 :]
    me = lax.axis_index("req")
    piece = message_refs[0].shape[1] // 2
    gate_up = message_refs[0][...].astype(F32)
    for ref in message_refs[1:]:
        gate_up = gate_up + ref[...].astype(F32)
    gate, up = gate_up[:, :piece], gate_up[:, piece:]
    hidden = (gate / (1.0 + jnp.exp(-gate)) * up).astype(BF16)
    experts = own_ref.shape[0]
    slots = placed_ref.shape[0] // experts
    placed = placed_ref[...]
    scale = scale_ref[...][:, :1]
    begin = pl.multiple_of(me * piece, STAT)
    width = own_ref.shape[2]
    row_count = out_refs[0].shape[0]
    for k in range(groups):
        produced = []
        for e in range(experts):
            weight = own_ref[e, pl.ds(begin, piece), :] if k == 0 else down_refs[k - 1][e]
            produced.append(
                jnp.dot(
                    hidden[e * slots : (e + 1) * slots], weight, preferred_element_type=F32
                )
            )
        produced = (jnp.concatenate(produced, axis=0) * scale).astype(BF16)
        total = lax.dot_general(
            placed, produced, (((0,), (0,)), ((), ())), preferred_element_type=F32
        )
        column = pl.multiple_of((me ^ k) * width, STAT)
        for j in range(groups):
            out_refs[j][:, pl.ds(column, width)] = total[
                j * row_count : (j + 1) * row_count
            ].astype(BF16)


def spread_kernel(groups, *refs):
    total = refs[0][...].astype(F32)
    for ref in refs[1:groups]:
        total = total + ref[...].astype(F32)
    out_ref = refs[groups]
    width = out_ref.shape[2]
    for s in range(out_ref.shape[0]):
        out_ref[s] = total[:, s * width : (s + 1) * width].astype(BF16)


def final_kernel(resid_ref, arrived_ref, out_ref):
    total = resid_ref[...]
    for s in range(arrived_ref.shape[0]):
        total = total + arrived_ref[s].astype(F32)
    for r in range(out_ref.shape[0]):
        out_ref[r] = total[r * NSTEP : (r + 1) * NSTEP].astype(BF16)


def staged(
    x_in,
    attn_gain,
    moe_gain,
    w_qkv,
    w_o,
    cache_k,
    cache_v,
    page_map,
    lengths,
    routes,
    route_weights,
    w_gate_up,
    w_down,
):
    requests = x_in.shape[0]
    row_count = requests * NSTEP
    members, groups = lax.axis_size("seq"), lax.axis_size("req")
    chips = members // 2
    heads = w_qkv.shape[1] // HD
    width = w_o.shape[1]
    depth = w_down.shape[1] // groups
    slots = cache_k.shape[1]

    own_heads, x, live, routing, gain = kernel_call(
        lambda *refs: project_kernel(groups, *refs),
        [
            jax.ShapeDtypeStruct((heads, row_count, 2 * HD), BF16),
            jax.ShapeDtypeStruct((row_count, D), F32),
            jax.ShapeDtypeStruct((requests, slots), F32),
            jax.ShapeDtypeStruct((row_count, STAT), F32),
            jax.ShapeDtypeStruct((1, D), F32),
        ],
        [HBM] * 8,
        [
            pltpu.VMEM(x_in.shape, BF16),
            pltpu.VMEM((D,), F32),
            pltpu.VMEM((D,), F32),
            pltpu.VMEM((w_qkv.shape[1], D), BF16),
            pltpu.SMEM(lengths.shape, jnp.int32),
            pltpu.SMEM(page_map.shape, jnp.int32),
            pltpu.VMEM(routes.shape, jnp.int32),
            pltpu.VMEM(route_weights.shape, F32),
            pltpu.SemaphoreType.DMA((8,)),
        ],
        vmem_mib=60,
    )(x_in, attn_gain, moe_gain, w_qkv.T, lengths, page_map, routes, route_weights)
    cuts = kernel_call(
        lambda *refs: cut_kernel(groups, *refs),
        [jax.ShapeDtypeStruct((w_down.shape[0], depth, w_down.shape[2]), BF16)] * (groups - 1),
        [HBM],
        [pltpu.SemaphoreType.DMA((groups - 1,))],
        [HBM] * (groups - 1),
    )(w_down)
    downs = [swap(cuts[k - 1], "req", k) for k in range(1, groups)]

    def gathered(own):
        near = [own] + [swap(own, "seq", 2 * k) for k in range(1, chips)]
        return near, [swap(piece, "seq", 1) for piece in near]

    near, far = gathered(own_heads)
    part_shape = jax.ShapeDtypeStruct((GROUP * row_count, WIDE), BF16)
    head_scratch = [
        pltpu.VMEM((2, chips, heads, row_count, 2 * HD), BF16),
        pltpu.VMEM((GROUP, row_count, KVD), F32),
        pltpu.VMEM((GROUP * row_count, WIDE), F32),
    ]
    part = kernel_call(
        lambda *refs: attend_kernel(chips, *refs),
        part_shape,
        [VMEM] * (2 * chips + 3),
        head_scratch,
    )(*near, *far, live, cache_k, cache_v)
    fresh = kernel_call(
        lambda *refs: fresh_kernel(chips, *refs),
        part_shape,
        [VMEM] * (2 * chips),
        head_scratch,
        cost=0.5,
    )(*near, *far)
    near, far = gathered(part)
    x = after(x, downs[2])
    share, resid = kernel_call(
        lambda *refs: merge_kernel(members + 1, *refs),
        [jax.ShapeDtypeStruct((row_count, width), F32)] * 2,
        [VMEM] * (members + 3),
    )(*near, *far, fresh, x, w_o.T)
    near, far = gathered(share)
    routing = after(routing, downs[1])
    packs = kernel_call(
        lambda *refs: mix_kernel(chips, groups, *refs),
        [jax.ShapeDtypeStruct((row_count, 2 * width + STAT), BF16)] * groups,
        [VMEM] * (2 * chips + 3),
        [pltpu.VMEM((2, chips, row_count, width), F32), pltpu.VMEM((row_count, D), F32)],
    )(*near, *far, x, gain, routing)

    def exchanged(pieces):
        return [pieces[0]] + [swap(pieces[k], "req", k) for k in range(1, groups)]

    experts = w_gate_up.shape[0]
    total_slots = experts * groups * CAP
    *messages, placed, scale = kernel_call(
        lambda *refs: gate_kernel(groups, *refs),
        [jax.ShapeDtypeStruct((total_slots, 2 * FFE // groups), BF16)] * groups
        + [
            jax.ShapeDtypeStruct((total_slots, groups * row_count), BF16),
            jax.ShapeDtypeStruct((total_slots, STAT), F32),
        ],
        [VMEM] * (groups + 1),
        [pltpu.VMEM((total_slots, 2 * FFE), F32)],
    )(*exchanged(packs), after(w_gate_up, downs[0]))
    outs = kernel_call(
        lambda *refs: down_kernel(groups, *refs),
        [jax.ShapeDtypeStruct((row_count, D), BF16)] * groups,
        [VMEM] * (2 * groups + 2),
    )(*exchanged(messages), w_down, *downs, placed, scale)
    spread = kernel_call(
        lambda *refs: spread_kernel(groups, *refs),
        jax.ShapeDtypeStruct((members, row_count, width), BF16),
        [VMEM] * groups,
    )(*exchanged(outs))
    arrived = lax.all_to_all(spread, "seq", 0, 0, tiled=True)
    return kernel_call(
        final_kernel, jax.ShapeDtypeStruct((requests, NSTEP, width), BF16), [VMEM] * 2
    )(resid, arrived)


def local(*args):
    w_qkv, w_o = args[3], args[4]
    members, groups = lax.axis_size("seq"), lax.axis_size("req")
    fits = (
        members == 2 * groups
        and groups & (groups - 1) == 0
        and w_qkv.shape[1] % HD == 0
        and (FFE // groups) % STAT == 0
        and (2 * w_o.shape[1]) % STAT == 0
    )
    return staged(*args) if fits else plain(*args)


def solution(mesh):
    in_specs = (
        P("req", None, None),
        P(),
        P(),
        P(None, "seq"),
        P(None, "seq"),
        P("req", "seq", None),
        P("req", "seq", None),
        P("req", "seq"),
        P("req"),
        P("req", None, None),
        P("req", None, None),
        P("seq", "req", None),
        P("seq", None, "req"),
    )
    out_specs = P("req", None, "seq")
    return jax.shard_map(local, mesh=mesh, in_specs=in_specs, out_specs=out_specs, check_vma=False)
```

```python
import math

import jax
import jax.numpy as jnp
from jax import lax
from jax.experimental import pallas as pl
from jax.experimental.pallas import tpu as pltpu
from jax.sharding import PartitionSpec as P

D = 1536
HEADS = 24
KVH = 8
HD = 64
FFE = 512
TOP = 8
NSTEP = 4
PAGE = 16
ATT = 1536
KVD = 512
GROUP = 3
CAP = 12


EPS = 1e-05
NEG = -1e30


def combined_all(value, axis, join):
    pieces = jax.tree.map(lambda part: lax.all_gather(part, axis), value)
    head = jax.tree.map(lambda part: part[0], pieces)
    tail = jax.tree.map(lambda part: part[1:], pieces)
    so_far, _ = lax.scan(lambda so_far, piece: (join(so_far, piece), None), head, tail)
    return so_far


def normalize(values, gain):
    power = jnp.mean(values * values, axis=-1, keepdims=True)
    return values * lax.rsqrt(power + EPS) * gain


def rotate(values, position):
    half = values.shape[-1] // 2
    rates = jnp.exp(
        jnp.arange(half, dtype=jnp.float32) * (-2.0 * math.log(10000.0) / values.shape[-1])
    )
    angle = position[..., None, None] * rates
    cosine = jnp.cos(angle)
    sine = jnp.sin(angle)
    first_half = values[..., :half]
    second_half = values[..., half:]
    return jnp.concatenate(
        [first_half * cosine - second_half * sine, second_half * cosine + first_half * sine],
        axis=-1,
    )


def softmax_join(left, right):
    left_top, left_total, left_sums = left
    right_top, right_total, right_sums = right
    highest = jnp.maximum(left_top, right_top)
    left_factor = jnp.exp(left_top - highest)
    right_factor = jnp.exp(right_top - highest)
    row_count, head_count = highest.shape
    left_part = left_sums.reshape(row_count, head_count, -1) * left_factor[:, :, None]
    right_part = right_sums.reshape(row_count, head_count, -1) * right_factor[:, :, None]
    joined = (left_part + right_part).reshape(row_count, -1)
    return (highest, left_total * left_factor + right_total * right_factor, joined)


def project_with(left, piece):
    return jnp.dot(left, piece, preferred_element_type=jnp.float32)


def plain(
    x_in,
    attn_gain,
    moe_gain,
    w_qkv,
    w_o,
    cache_k,
    cache_v,
    page_map,
    lengths,
    routes,
    route_weights,
    w_gate_up,
    w_down,
):
    local_requests = x_in.shape[0]
    row_count = local_requests * NSTEP
    inputs = x_in.astype(jnp.float32).reshape(row_count, D)
    normed = normalize(inputs, attn_gain).astype(jnp.bfloat16)
    projected = project_with(normed, lax.all_gather(w_qkv, "seq", axis=1, tiled=True))
    queries = projected[:, :ATT].reshape(local_requests, NSTEP, HEADS, HD)
    keys_new = projected[:, ATT : ATT + KVD].reshape(local_requests, NSTEP, KVH, HD)
    values_new = (
        projected[:, ATT + KVD :].reshape(local_requests, NSTEP, KVH, HD).astype(jnp.bfloat16)
    )
    position = (lengths[:, None] + jnp.arange(NSTEP, dtype=jnp.int32)[None, :]).astype(jnp.float32)
    queries = (
        rotate(queries, position)
        .astype(jnp.bfloat16)
        .reshape(local_requests, NSTEP, KVH, GROUP, HD)
    )
    keys_new = rotate(keys_new, position).astype(jnp.bfloat16)
    scale = HD ** (-0.5)
    slot_count = cache_k.shape[1]
    cached_keys = cache_k.reshape(local_requests, slot_count, KVH, HD)
    cached_values = cache_v.reshape(local_requests, slot_count, KVH, HD)
    slot_position = (
        page_map[:, :, None] * PAGE + jnp.arange(PAGE, dtype=jnp.int32)[None, None, :]
    ).reshape(local_requests, slot_count)
    live = (slot_position < lengths[:, None])[:, None, None, None, :]
    scores = (
        jnp.einsum("rskgd,rtkd->rskgt", queries, cached_keys, preferred_element_type=jnp.float32)
        * scale
    )
    scores = jnp.where(live, scores, NEG)
    local_top = jnp.max(scores, axis=-1)
    exp_scores = jnp.where(live, jnp.exp(scores - local_top[..., None]), 0.0)
    local_total = jnp.sum(exp_scores, axis=-1).reshape(row_count, HEADS)
    local_sums = jnp.einsum(
        "rskgt,rtkd->rskgd",
        exp_scores.astype(jnp.bfloat16),
        cached_values,
        preferred_element_type=jnp.float32,
    ).reshape(row_count, ATT)
    local_top = local_top.reshape(row_count, HEADS)
    cache_top, cache_total, cache_sums = combined_all(
        (local_top, local_total, local_sums), "seq", softmax_join
    )
    causal = (
        jnp.arange(NSTEP, dtype=jnp.int32)[:, None] >= jnp.arange(NSTEP, dtype=jnp.int32)[None, :]
    )[None, :, None, None, :]
    fresh = (
        jnp.einsum("rskgd,rukd->rskgu", queries, keys_new, preferred_element_type=jnp.float32)
        * scale
    )
    fresh = jnp.where(causal, fresh, NEG).reshape(row_count, HEADS, NSTEP)
    highest = jnp.maximum(cache_top, jnp.max(fresh, axis=-1))
    fresh_exp = jnp.exp(fresh - highest[:, :, None])
    carried = jnp.exp(cache_top - highest)
    denominator = cache_total * carried + jnp.sum(fresh_exp, axis=-1)
    fresh_probs = fresh_exp.reshape(local_requests, NSTEP, KVH, GROUP, NSTEP).astype(jnp.bfloat16)
    fresh_sums = jnp.einsum(
        "rskgu,rukd->rskgd", fresh_probs, values_new, preferred_element_type=jnp.float32
    ).reshape(row_count, HEADS, HD)
    numerator = cache_sums.reshape(row_count, HEADS, HD) * carried[:, :, None] + fresh_sums
    attended = (numerator / denominator[:, :, None]).reshape(row_count, ATT).astype(jnp.bfloat16)
    attn_mixed = project_with(attended, lax.all_gather(w_o, "seq", axis=1, tiled=True))
    resid = inputs + attn_mixed
    mixed_in = normalize(resid, moe_gain).astype(jnp.bfloat16)
    local_experts = w_gate_up.shape[0]
    groups = lax.axis_size("req")
    owned = lax.axis_index("seq") * local_experts + jnp.arange(local_experts, dtype=jnp.int32)
    chosen = routes.reshape(row_count, TOP)
    gates = route_weights.reshape(row_count, TOP)
    matches = chosen[None, :, :] == owned[:, None, None]
    routed = jnp.any(matches, axis=-1)
    route_scale = jnp.sum(jnp.where(matches, gates[None, :, :], 0.0), axis=-1)
    ordinal = jnp.cumsum(routed.astype(jnp.int32), axis=1) - 1
    placed = routed[:, :, None] & (
        ordinal[:, :, None] == jnp.arange(CAP, dtype=jnp.int32)[None, None, :]
    )
    outgoing = jnp.einsum(
        "erc,rd->ecd", placed.astype(jnp.bfloat16), mixed_in, preferred_element_type=jnp.float32
    ).astype(jnp.bfloat16)
    arrived = lax.all_to_all(outgoing[:, None], "req", split_axis=3, concat_axis=1, tiled=True)
    slice_width = arrived.shape[3]
    arrived = arrived.reshape(local_experts, groups * CAP, slice_width)
    partial_values = jnp.einsum(
        "end,edf->enf", arrived, w_gate_up, preferred_element_type=jnp.float32
    )
    gate_up = lax.psum(partial_values, "req")
    hidden = (jax.nn.silu(gate_up[..., :FFE]) * gate_up[..., FFE:]).astype(jnp.bfloat16)
    produced = jnp.einsum("enf,efd->end", hidden, w_down, preferred_element_type=jnp.float32)
    returned = lax.all_to_all(
        produced.reshape(local_experts, groups, CAP, slice_width),
        "req",
        split_axis=1,
        concat_axis=3,
        tiled=True,
    )[:, 0]
    weighted = placed.astype(jnp.float32) * route_scale[:, :, None]
    expert_total = jnp.einsum("erc,ecd->rd", weighted, returned, precision=lax.Precision.HIGHEST)
    own_share = lax.psum_scatter(expert_total, "seq", scatter_dimension=1, tiled=True)
    share_width = own_share.shape[1]
    resid_share = lax.dynamic_slice_in_dim(
        resid, lax.axis_index("seq") * share_width, share_width, 1
    )
    return (
        (resid_share + own_share).astype(jnp.bfloat16).reshape(local_requests, NSTEP, share_width)
    )


F32 = jnp.float32
BF16 = jnp.bfloat16
STAT = 128
WIDE = KVD + STAT
VMEM = pl.BlockSpec(memory_space=pltpu.VMEM)
SMEM = pl.BlockSpec(memory_space=pltpu.SMEM)


def kernel_call(body, out_shape, in_specs, scratch=(), out_specs=None, vmem_mib=8, cost=0.5):
    return pl.pallas_call(
        body,
        out_shape=out_shape,
        in_specs=in_specs,
        out_specs=out_specs or ([VMEM] * len(out_shape) if isinstance(out_shape, list) else VMEM),
        scratch_shapes=list(scratch),
        compiler_params=pltpu.CompilerParams(vmem_limit_bytes=vmem_mib * 2**20),
        cost_estimate=pl.CostEstimate(
            flops=int(cost * 1e9), bytes_accessed=int(cost * 3e6), transcendentals=0
        ),
    )


def iota(shape, dim):
    return lax.broadcasted_iota(jnp.int32, shape, dim)


def split3(value):
    high = value.astype(BF16).astype(F32)
    rest = value - high
    middle = rest.astype(BF16).astype(F32)
    return high, middle, rest - middle


def rows_of(ref):
    return jnp.concatenate([ref[r].astype(F32) for r in range(ref.shape[0])], axis=0)


def dot_nt(left, right):
    return lax.dot_general(left, right, (((1,), (1,)), ((), ())), preferred_element_type=F32)


def swap(value, axis, mask):
    pairs = [(i, i ^ mask) for i in range(lax.axis_size(axis))]
    return lax.ppermute(value, axis, pairs)


def after(value, *others):
    return lax.optimization_barrier((value, *others))[0]


def project_kernel(*refs):
    x_in, attn_gain, moe_gain, w_in, lengths, pages, routes, weights = refs[:8]
    heads_ref, x_ref, live_ref, routing_ref, gain_ref = refs[8:]
    requests = x_in.shape[0]
    row_count = requests * NSTEP
    shape = (row_count, STAT)
    row, lane = iota(shape, 0), iota(shape, 1)
    position = row % NSTEP
    for r in range(requests):
        position = position + jnp.where(row // NSTEP == r, lengths[r], 0)
    rates = jnp.exp((lane % (HD // 2)).astype(F32) * (-2.0 * math.log(10000.0) / HD))
    angle = position.astype(F32) * rates
    cosine = jnp.cos(angle)
    sine = jnp.where(lane % HD < HD // 2, -jnp.sin(angle), jnp.sin(angle))
    x = rows_of(x_in)
    x_ref[...] = x
    power = jnp.mean(x * x, axis=-1, keepdims=True)
    normed = (x * lax.rsqrt(power + EPS) * attn_gain[...].reshape(1, D)).astype(BF16)
    projected = dot_nt(normed, w_in[...])
    heads = w_in.shape[0] // HD
    first = lax.axis_index("seq") * heads
    for i in range(heads):
        one = projected[:, i * HD : (i + 1) * HD]
        both = jnp.concatenate([one, one], axis=1)
        turned = both * cosine + pltpu.roll(both, HD // 2, 1) * sine
        heads_ref[i] = jnp.where(first + i < HEADS + KVH, turned, both).astype(BF16)
    slots = live_ref.shape[1]
    slot = iota((1, slots), 1)
    for r in range(requests):
        page = jnp.zeros((1, slots), jnp.int32)
        for j in range(slots // PAGE):
            page = jnp.where(slot // PAGE == j, pages[r, j], page)
        live = page * PAGE + slot % PAGE < lengths[r]
        live_ref[r : r + 1, :] = jnp.where(live, 1.0, 0.0)
    high, middle, low = split3(rows_of(weights))
    routing_ref[...] = jnp.concatenate(
        [rows_of(routes), high, middle, low, jnp.zeros((row_count, STAT - 4 * TOP), F32)], axis=1
    )
    gain_ref[...] = moe_gain[...].reshape(1, D)


def gather_pieces(near_refs, far_refs, all_ref):
    core = lax.axis_index("seq") % 2
    for k in range(len(near_refs)):
        all_ref[core, k] = near_refs[k][...]
        all_ref[1 - core, k] = far_refs[k][...]


def paired(head, left, right):
    a = head(left)
    return jnp.where(iota(a.shape, 1) < HD, a, head(right))


def expanded(q_ref, r):
    rows = [q_ref[g, r * NSTEP : (r + 1) * NSTEP, :] for g in range(GROUP)]
    base = jnp.concatenate(rows + [jnp.zeros((NSTEP, KVD), F32)], axis=0)
    owner = iota(base.shape, 1) // HD
    return jnp.concatenate(
        [jnp.where(owner == k, base, 0.0) for k in range(KVH)], axis=0
    ).astype(BF16)


def attend_part(query, keys, values, live):
    scores = jnp.where(live, dot_nt(query, keys) * (HD ** (-0.5)), NEG)
    top = jnp.max(scores, axis=1, keepdims=True)
    exp_scores = jnp.where(live, jnp.exp(scores - top), 0.0)
    total = jnp.sum(exp_scores, axis=1, keepdims=True)
    return top, total, jnp.dot(exp_scores.astype(BF16), values, preferred_element_type=F32)


def place_rows(part_ref, r, row_count, top, total, sums):
    block = (GROUP + 1) * NSTEP
    owner = iota((block, KVD), 1) // HD
    lane = iota((block, STAT), 1)
    own_sums = jnp.zeros((block, KVD), F32)
    stats = jnp.zeros((block, STAT), F32)
    for k in range(KVH):
        rows = slice(k * block, (k + 1) * block)
        own_sums = jnp.where(owner == k, sums[rows], own_sums)
        value = jnp.where(lane < 3 * KVH, top[rows], total[rows])
        stats = jnp.where(lane % KVH == k, value, stats)
    high, middle, low = split3(stats)
    part = (lane // KVH) % 3
    stats = jnp.where(part == 0, high, jnp.where(part == 1, middle, low))
    for g in range(GROUP):
        rows = slice(g * row_count + r * NSTEP, g * row_count + (r + 1) * NSTEP)
        part_ref[rows, :KVD] = own_sums[g * NSTEP : (g + 1) * NSTEP]
        part_ref[rows, KVD:] = stats[g * NSTEP : (g + 1) * NSTEP]


def head_of(all_ref):
    chip = lax.axis_index("seq") // 2
    heads = all_ref.shape[2]

    def head(h):
        owner = h // heads
        return all_ref[owner % 2, chip ^ (owner // 2), h % heads].astype(F32)

    return head


def query_rows(head, q_ref):
    for g in range(GROUP):
        for m in range(KVH // 2):
            q_ref[g, :, m * STAT : (m + 1) * STAT] = paired(
                head, GROUP * 2 * m + g, GROUP * (2 * m + 1) + g
            )


def attend_kernel(chips, *refs):
    near_refs, far_refs = refs[:chips], refs[chips : 2 * chips]
    live_ref, k_ref, v_ref, out_ref, all_ref, q_ref, part_ref = refs[2 * chips :]
    requests = k_ref.shape[0]
    gather_pieces(near_refs, far_refs, all_ref)
    query_rows(head_of(all_ref), q_ref)
    for r in range(requests):
        live = live_ref[r : r + 1, :] > 0.5
        place_rows(
            part_ref,
            r,
            requests * NSTEP,
            *attend_part(expanded(q_ref, r), k_ref[r], v_ref[r], live),
        )
    out_ref[...] = part_ref[...].astype(BF16)


def fresh_kernel(chips, *refs):
    near_refs, far_refs = refs[:chips], refs[chips : 2 * chips]
    out_ref, all_ref, q_ref, part_ref = refs[2 * chips :]
    gather_pieces(near_refs, far_refs, all_ref)
    head = head_of(all_ref)
    query_rows(head, q_ref)
    row_count = q_ref.shape[1]
    pad = jnp.zeros((STAT - row_count, KVD), F32)

    def new_rows(first):
        pieces = [paired(head, first + 2 * m, first + 2 * m + 1) for m in range(KVH // 2)]
        return jnp.concatenate([jnp.concatenate(pieces, axis=1), pad], axis=0).astype(BF16)

    keys, values = new_rows(HEADS), new_rows(HEADS + KVH)
    shape = ((GROUP + 1) * NSTEP * KVH, STAT)
    slot, step = iota(shape, 1), iota(shape, 0) % NSTEP
    for r in range(row_count // NSTEP):
        live = (slot // NSTEP == r) & (slot % NSTEP <= step)
        place_rows(
            part_ref, r, row_count, *attend_part(expanded(q_ref, r), keys, values, live)
        )
    out_ref[...] = part_ref[...].astype(BF16)


def merge_kernel(count, *refs):
    part_refs = refs[:count]
    x_ref, w_ref, share_ref, resid_ref = refs[count:]
    parts = [ref[...].astype(F32) for ref in part_refs]
    tops, totals = [], []
    for part in parts:
        stats = part[:, KVD:]
        full = stats + (
            pltpu.roll(stats, STAT - KVH, 1) + pltpu.roll(stats, STAT - 2 * KVH, 1)
        )
        tops.append(full)
        totals.append(pltpu.roll(full, STAT - 3 * KVH, 1))
    highest = tops[0]
    for top in tops[1:]:
        highest = jnp.maximum(highest, top)
    factors = [jnp.exp(top - highest) for top in tops]
    denominator = factors[0] * totals[0]
    for factor, total in zip(factors[1:], totals[1:]):
        denominator = denominator + factor * total
    inverse = 1.0 / denominator
    row_total = parts[0].shape[0]
    row_count = row_total // GROUP
    left = iota((row_total, STAT), 1) < HD
    columns = []
    for m in range(KVH // 2):
        value = jnp.zeros((row_total, STAT), F32)
        for part, factor in zip(parts, factors):
            spread = jnp.where(left, factor[:, 2 * m : 2 * m + 1], factor[:, 2 * m + 1 : 2 * m + 2])
            value = value + spread * part[:, m * STAT : (m + 1) * STAT]
        spread = jnp.where(left, inverse[:, 2 * m : 2 * m + 1], inverse[:, 2 * m + 1 : 2 * m + 2])
        columns.append(value * spread)

    def head(h, side):
        k, g = h // GROUP, h % GROUP
        rows = columns[k // 2][g * row_count : (g + 1) * row_count]
        return rows if k % 2 == side else pltpu.roll(rows, HD, 1)

    left = iota((row_count, STAT), 1) < HD
    attended = jnp.concatenate(
        [jnp.where(left, head(2 * n, 0), head(2 * n + 1, 1)) for n in range(HEADS // 2)], axis=1
    ).astype(BF16)
    share = dot_nt(attended, w_ref[...])
    share_ref[...] = share
    width = w_ref.shape[0]
    member = lax.axis_index("seq")
    chunk = x_ref[:, pl.ds(pl.multiple_of((member // 2) * (2 * width), STAT), 2 * width)]
    resid_ref[...] = share + jnp.where(member % 2 == 0, chunk[:, :width], chunk[:, width:])


def mix_kernel(chips, groups, *refs):
    near_refs, far_refs = refs[:chips], refs[chips : 2 * chips]
    x_ref, gain_ref, routing_ref = refs[2 * chips : 2 * chips + 3]
    pack_refs, all_ref, mixed_ref = refs[2 * chips + 3 : -2], refs[-2], refs[-1]
    gather_pieces(near_refs, far_refs, all_ref)
    chip = lax.axis_index("seq") // 2
    attn = jnp.concatenate([all_ref[s % 2, chip ^ (s // 2)] for s in range(2 * chips)], axis=1)
    resid = x_ref[...] + attn
    power = jnp.mean(resid * resid, axis=-1, keepdims=True)
    mixed_ref[...] = resid * lax.rsqrt(power + EPS) * gain_ref[...]
    routing = routing_ref[...]
    width = D // groups
    for k in range(groups):
        start = pl.multiple_of((lax.axis_index("req") ^ k) * width, STAT)
        part = mixed_ref[:, pl.ds(start, width)]
        pack_refs[k][...] = jnp.concatenate([part, routing], axis=1).astype(BF16)


def across(column, eye):
    return jnp.sum(jnp.where(eye, column, 0.0), axis=0, keepdims=True)


def gate_kernel(groups, *refs):
    pack_refs = refs[:groups]
    w_ref = refs[groups]
    message_refs = refs[groups + 1 : 2 * groups + 1]
    placed_ref, scale_ref, full_ref = refs[2 * groups + 1 :]
    first = lax.axis_index("seq") * w_ref.shape[0]
    me = lax.axis_index("req")
    packs = [ref[...].astype(F32) for ref in pack_refs]
    row_count = packs[0].shape[0]
    tokens = groups * row_count
    width = w_ref.shape[1]
    mixed = jnp.concatenate([pack[:, :width] for pack in packs], axis=0).astype(BF16)
    routing = jnp.concatenate([pack[:, width:] for pack in packs], axis=0)
    chosen = routing[:, :TOP]
    gates = routing[:, TOP : 2 * TOP] + (
        routing[:, 2 * TOP : 3 * TOP] + routing[:, 3 * TOP : 4 * TOP]
    )
    experts = w_ref.shape[0]
    square = (tokens, tokens)
    eye = iota(square, 0) == iota(square, 1)
    earlier = (iota(square, 0) < iota(square, 1)) & (
        iota(square, 0) // row_count == iota(square, 1) // row_count
    )
    slots = groups * CAP
    shape = (slots, tokens)
    home = (iota(shape, 1) // row_count) ^ me
    slot = iota(shape, 0)
    same_group = slot // CAP == home
    ordinal_of_slot = (slot % CAP).astype(F32)
    placed, scales = [], []
    for e in range(experts):
        match = chosen == (first + e).astype(F32)
        routed = jnp.max(jnp.where(match, 1.0, 0.0), axis=1, keepdims=True)
        scale = jnp.sum(jnp.where(match, gates, 0.0), axis=1, keepdims=True)
        ordinal = across(routed, earlier)
        here = same_group & (across(routed, eye) > 0.5) & (ordinal_of_slot == ordinal)
        placed.append(jnp.where(here, 1.0, 0.0))
        scales.append(jnp.sum(jnp.where(here, across(scale, eye), 0.0), axis=1, keepdims=True))
    all_placed = jnp.concatenate(placed, axis=0).astype(BF16)
    taken = jnp.dot(all_placed, mixed, preferred_element_type=F32).astype(BF16)
    for e in range(experts):
        rows = slice(e * slots, (e + 1) * slots)
        placed_ref[e] = all_placed[rows]
        scale_ref[e] = jnp.broadcast_to(scales[e], scale_ref.shape[1:])
        full_ref[e] = jnp.dot(taken[rows], w_ref[e], preferred_element_type=F32).astype(BF16)
    for k in range(groups):
        message_refs[k][...] = full_ref[me ^ k]


def down_kernel(groups, *refs):
    message_refs = refs[:groups]
    down_ref, placed_ref, scale_ref = refs[groups : groups + 3]
    out_refs = refs[groups + 3 :]
    me = lax.axis_index("req")
    gate_up = message_refs[0][...].astype(F32)
    for ref in message_refs[1:]:
        gate_up = gate_up + ref[...].astype(F32)
    gate, up = gate_up[:, :FFE], gate_up[:, FFE:]
    hidden = (gate / (1.0 + jnp.exp(-gate)) * up).astype(BF16)
    placed, scale = placed_ref[me], scale_ref[me][:, :1]
    width = down_ref.shape[2]
    row_count = out_refs[0].shape[0]
    for k in range(groups):
        produced = jnp.dot(hidden, down_ref[k], preferred_element_type=F32)
        total = lax.dot_general(
            placed,
            (produced * scale).astype(BF16),
            (((0,), (0,)), ((), ())),
            preferred_element_type=F32,
        )
        for j in range(groups):
            out_refs[j][:, k * width : (k + 1) * width] = total[
                j * row_count : (j + 1) * row_count
            ].astype(BF16)


def spread_kernel(groups, *refs):
    total = refs[0][...].astype(F32)
    for ref in refs[1:groups]:
        total = total + ref[...].astype(F32)
    out_ref = refs[groups]
    width = out_ref.shape[2]
    for s in range(out_ref.shape[0]):
        out_ref[s] = total[:, s * width : (s + 1) * width].astype(BF16)


def final_kernel(resid_ref, arrived_ref, out_ref):
    total = resid_ref[...]
    for s in range(arrived_ref.shape[0]):
        total = total + arrived_ref[s].astype(F32)
    for r in range(out_ref.shape[0]):
        out_ref[r] = total[r * NSTEP : (r + 1) * NSTEP].astype(BF16)


def staged(
    x_in,
    attn_gain,
    moe_gain,
    w_qkv,
    w_o,
    cache_k,
    cache_v,
    page_map,
    lengths,
    routes,
    route_weights,
    w_gate_up,
    w_down,
):
    requests = x_in.shape[0]
    row_count = requests * NSTEP
    members, groups = lax.axis_size("seq"), lax.axis_size("req")
    chips = members // 2
    heads = w_qkv.shape[1] // HD
    width = w_o.shape[1]

    own_heads, x, live, routing, gain = kernel_call(
        project_kernel,
        [
            jax.ShapeDtypeStruct((heads, row_count, 2 * HD), BF16),
            jax.ShapeDtypeStruct((row_count, D), F32),
            jax.ShapeDtypeStruct((requests, cache_k.shape[1]), F32),
            jax.ShapeDtypeStruct((row_count, STAT), F32),
            jax.ShapeDtypeStruct((1, D), F32),
        ],
        [VMEM] * 4 + [SMEM] * 2 + [VMEM] * 2,
    )(x_in, attn_gain, moe_gain, w_qkv.T, lengths, page_map, routes, route_weights)
    def gathered(own, *first):
        near = [swap(own, "seq", 2 * k) for k in range(chips - 1, 0, -1)]
        near = [own] + near[::-1]
        near[1] = after(near[1], *first) if first else near[1]
        return near, [swap(piece, "seq", 1) for piece in near]

    near, far = gathered(own_heads)
    down = lax.all_to_all(w_down, "req", 0, 0, tiled=True)
    part_shape = jax.ShapeDtypeStruct((GROUP * row_count, WIDE), BF16)
    head_scratch = [
        pltpu.VMEM((2, chips, heads, row_count, 2 * HD), BF16),
        pltpu.VMEM((GROUP, row_count, KVD), F32),
        pltpu.VMEM((GROUP * row_count, WIDE), F32),
    ]
    part = kernel_call(
        lambda *refs: attend_kernel(chips, *refs),
        part_shape,
        [VMEM] * (2 * chips + 3),
        head_scratch,
    )(*near, *far, live, cache_k, cache_v)
    fresh = kernel_call(
        lambda *refs: fresh_kernel(chips, *refs),
        part_shape,
        [VMEM] * (2 * chips),
        head_scratch,
        cost=0.5,
    )(*near, *far)
    near, far = gathered(part, fresh)
    share, resid = kernel_call(
        lambda *refs: merge_kernel(members + 1, *refs),
        [jax.ShapeDtypeStruct((row_count, width), F32)] * 2,
        [VMEM] * (members + 3),
    )(*near, *far, fresh, x, w_o.T)
    near, far = gathered(share)
    packs = kernel_call(
        lambda *refs: mix_kernel(chips, groups, *refs),
        [jax.ShapeDtypeStruct((row_count, 2 * width + STAT), BF16)] * groups,
        [VMEM] * (2 * chips + 3),
        [pltpu.VMEM((2, chips, row_count, width), F32), pltpu.VMEM((row_count, D), F32)],
    )(*near, *far, x, gain, routing)

    def exchanged(pieces):
        return [pieces[0]] + [swap(pieces[k], "req", k) for k in range(1, groups)]

    experts = w_gate_up.shape[0]
    slots = groups * CAP
    *messages, placed, scale = kernel_call(
        lambda *refs: gate_kernel(groups, *refs),
        [jax.ShapeDtypeStruct((slots, 2 * FFE), BF16)] * groups
        + [
            jax.ShapeDtypeStruct((experts, slots, groups * row_count), BF16),
            jax.ShapeDtypeStruct((experts, slots, STAT), F32),
        ],
        [VMEM] * (groups + 1),
        [pltpu.VMEM((experts, slots, 2 * FFE), BF16)],
    )(*exchanged(packs), w_gate_up)
    outs = kernel_call(
        lambda *refs: down_kernel(groups, *refs),
        [jax.ShapeDtypeStruct((row_count, D), BF16)] * groups,
        [VMEM] * (groups + 3),
    )(*exchanged(messages), down, placed, scale)
    spread = kernel_call(
        lambda *refs: spread_kernel(groups, *refs),
        jax.ShapeDtypeStruct((members, row_count, width), BF16),
        [VMEM] * groups,
    )(*exchanged(outs))
    arrived = lax.all_to_all(spread, "seq", 0, 0, tiled=True)
    return kernel_call(
        final_kernel, jax.ShapeDtypeStruct((requests, NSTEP, width), BF16), [VMEM] * 2
    )(resid, arrived)


def local(*args):
    w_qkv, w_o, w_gate_up = args[3], args[4], args[11]
    members, groups = lax.axis_size("seq"), lax.axis_size("req")
    fits = (
        members == 2 * groups
        and groups & (groups - 1) == 0
        and w_qkv.shape[1] % HD == 0
        and w_gate_up.shape[0] == groups
        and (2 * w_o.shape[1]) % STAT == 0
    )
    return staged(*args) if fits else plain(*args)


def solution(mesh):
    in_specs = (
        P("req", None, None),
        P(),
        P(),
        P(None, "seq"),
        P(None, "seq"),
        P("req", "seq", None),
        P("req", "seq", None),
        P("req", "seq"),
        P("req"),
        P("req", None, None),
        P("req", None, None),
        P("seq", "req", None),
        P("seq", None, "req"),
    )
    out_specs = P("req", None, "seq")
    return jax.shard_map(local, mesh=mesh, in_specs=in_specs, out_specs=out_specs, check_vma=False)
```

```python
import math

import jax
import jax.numpy as jnp
from jax import lax
from jax.experimental import pallas as pl
from jax.experimental.pallas import tpu as pltpu
from jax.sharding import PartitionSpec as P

D = 1536
HEADS = 24
KVH = 8
HD = 64
FFE = 512
TOP = 8
NSTEP = 4
PAGE = 16
ATT = 1536
KVD = 512
GROUP = 3
CAP = 12


EPS = 1e-05
NEG = -1e30


def combined_all(value, axis, join):
    pieces = jax.tree.map(lambda part: lax.all_gather(part, axis), value)
    head = jax.tree.map(lambda part: part[0], pieces)
    tail = jax.tree.map(lambda part: part[1:], pieces)
    so_far, _ = lax.scan(lambda so_far, piece: (join(so_far, piece), None), head, tail)
    return so_far


def normalize(values, gain):
    power = jnp.mean(values * values, axis=-1, keepdims=True)
    return values * lax.rsqrt(power + EPS) * gain


def rotate(values, position):
    half = values.shape[-1] // 2
    rates = jnp.exp(
        jnp.arange(half, dtype=jnp.float32) * (-2.0 * math.log(10000.0) / values.shape[-1])
    )
    angle = position[..., None, None] * rates
    cosine = jnp.cos(angle)
    sine = jnp.sin(angle)
    first_half = values[..., :half]
    second_half = values[..., half:]
    return jnp.concatenate(
        [first_half * cosine - second_half * sine, second_half * cosine + first_half * sine],
        axis=-1,
    )


def softmax_join(left, right):
    left_top, left_total, left_sums = left
    right_top, right_total, right_sums = right
    highest = jnp.maximum(left_top, right_top)
    left_factor = jnp.exp(left_top - highest)
    right_factor = jnp.exp(right_top - highest)
    row_count, head_count = highest.shape
    left_part = left_sums.reshape(row_count, head_count, -1) * left_factor[:, :, None]
    right_part = right_sums.reshape(row_count, head_count, -1) * right_factor[:, :, None]
    joined = (left_part + right_part).reshape(row_count, -1)
    return (highest, left_total * left_factor + right_total * right_factor, joined)


def project_with(left, piece):
    return jnp.dot(left, piece, preferred_element_type=jnp.float32)


def plain(
    x_in,
    attn_gain,
    moe_gain,
    w_qkv,
    w_o,
    cache_k,
    cache_v,
    page_map,
    lengths,
    routes,
    route_weights,
    w_gate_up,
    w_down,
):
    local_requests = x_in.shape[0]
    row_count = local_requests * NSTEP
    inputs = x_in.astype(jnp.float32).reshape(row_count, D)
    normed = normalize(inputs, attn_gain).astype(jnp.bfloat16)
    projected = project_with(normed, lax.all_gather(w_qkv, "seq", axis=1, tiled=True))
    queries = projected[:, :ATT].reshape(local_requests, NSTEP, HEADS, HD)
    keys_new = projected[:, ATT : ATT + KVD].reshape(local_requests, NSTEP, KVH, HD)
    values_new = (
        projected[:, ATT + KVD :].reshape(local_requests, NSTEP, KVH, HD).astype(jnp.bfloat16)
    )
    position = (lengths[:, None] + jnp.arange(NSTEP, dtype=jnp.int32)[None, :]).astype(jnp.float32)
    queries = (
        rotate(queries, position)
        .astype(jnp.bfloat16)
        .reshape(local_requests, NSTEP, KVH, GROUP, HD)
    )
    keys_new = rotate(keys_new, position).astype(jnp.bfloat16)
    scale = HD ** (-0.5)
    slot_count = cache_k.shape[1]
    cached_keys = cache_k.reshape(local_requests, slot_count, KVH, HD)
    cached_values = cache_v.reshape(local_requests, slot_count, KVH, HD)
    slot_position = (
        page_map[:, :, None] * PAGE + jnp.arange(PAGE, dtype=jnp.int32)[None, None, :]
    ).reshape(local_requests, slot_count)
    live = (slot_position < lengths[:, None])[:, None, None, None, :]
    scores = (
        jnp.einsum("rskgd,rtkd->rskgt", queries, cached_keys, preferred_element_type=jnp.float32)
        * scale
    )
    scores = jnp.where(live, scores, NEG)
    local_top = jnp.max(scores, axis=-1)
    exp_scores = jnp.where(live, jnp.exp(scores - local_top[..., None]), 0.0)
    local_total = jnp.sum(exp_scores, axis=-1).reshape(row_count, HEADS)
    local_sums = jnp.einsum(
        "rskgt,rtkd->rskgd",
        exp_scores.astype(jnp.bfloat16),
        cached_values,
        preferred_element_type=jnp.float32,
    ).reshape(row_count, ATT)
    local_top = local_top.reshape(row_count, HEADS)
    cache_top, cache_total, cache_sums = combined_all(
        (local_top, local_total, local_sums), "seq", softmax_join
    )
    causal = (
        jnp.arange(NSTEP, dtype=jnp.int32)[:, None] >= jnp.arange(NSTEP, dtype=jnp.int32)[None, :]
    )[None, :, None, None, :]
    fresh = (
        jnp.einsum("rskgd,rukd->rskgu", queries, keys_new, preferred_element_type=jnp.float32)
        * scale
    )
    fresh = jnp.where(causal, fresh, NEG).reshape(row_count, HEADS, NSTEP)
    highest = jnp.maximum(cache_top, jnp.max(fresh, axis=-1))
    fresh_exp = jnp.exp(fresh - highest[:, :, None])
    carried = jnp.exp(cache_top - highest)
    denominator = cache_total * carried + jnp.sum(fresh_exp, axis=-1)
    fresh_probs = fresh_exp.reshape(local_requests, NSTEP, KVH, GROUP, NSTEP).astype(jnp.bfloat16)
    fresh_sums = jnp.einsum(
        "rskgu,rukd->rskgd", fresh_probs, values_new, preferred_element_type=jnp.float32
    ).reshape(row_count, HEADS, HD)
    numerator = cache_sums.reshape(row_count, HEADS, HD) * carried[:, :, None] + fresh_sums
    attended = (numerator / denominator[:, :, None]).reshape(row_count, ATT).astype(jnp.bfloat16)
    attn_mixed = project_with(attended, lax.all_gather(w_o, "seq", axis=1, tiled=True))
    resid = inputs + attn_mixed
    mixed_in = normalize(resid, moe_gain).astype(jnp.bfloat16)
    local_experts = w_gate_up.shape[0]
    groups = lax.axis_size("req")
    owned = lax.axis_index("seq") * local_experts + jnp.arange(local_experts, dtype=jnp.int32)
    chosen = routes.reshape(row_count, TOP)
    gates = route_weights.reshape(row_count, TOP)
    matches = chosen[None, :, :] == owned[:, None, None]
    routed = jnp.any(matches, axis=-1)
    route_scale = jnp.sum(jnp.where(matches, gates[None, :, :], 0.0), axis=-1)
    ordinal = jnp.cumsum(routed.astype(jnp.int32), axis=1) - 1
    placed = routed[:, :, None] & (
        ordinal[:, :, None] == jnp.arange(CAP, dtype=jnp.int32)[None, None, :]
    )
    outgoing = jnp.einsum(
        "erc,rd->ecd", placed.astype(jnp.bfloat16), mixed_in, preferred_element_type=jnp.float32
    ).astype(jnp.bfloat16)
    arrived = lax.all_to_all(outgoing[:, None], "req", split_axis=3, concat_axis=1, tiled=True)
    slice_width = arrived.shape[3]
    arrived = arrived.reshape(local_experts, groups * CAP, slice_width)
    partial_values = jnp.einsum(
        "end,edf->enf", arrived, w_gate_up, preferred_element_type=jnp.float32
    )
    gate_up = lax.psum(partial_values, "req")
    hidden = (jax.nn.silu(gate_up[..., :FFE]) * gate_up[..., FFE:]).astype(jnp.bfloat16)
    produced = jnp.einsum("enf,efd->end", hidden, w_down, preferred_element_type=jnp.float32)
    returned = lax.all_to_all(
        produced.reshape(local_experts, groups, CAP, slice_width),
        "req",
        split_axis=1,
        concat_axis=3,
        tiled=True,
    )[:, 0]
    weighted = placed.astype(jnp.float32) * route_scale[:, :, None]
    expert_total = jnp.einsum("erc,ecd->rd", weighted, returned, precision=lax.Precision.HIGHEST)
    own_share = lax.psum_scatter(expert_total, "seq", scatter_dimension=1, tiled=True)
    share_width = own_share.shape[1]
    resid_share = lax.dynamic_slice_in_dim(
        resid, lax.axis_index("seq") * share_width, share_width, 1
    )
    return (
        (resid_share + own_share).astype(jnp.bfloat16).reshape(local_requests, NSTEP, share_width)
    )


F32 = jnp.float32
BF16 = jnp.bfloat16
STAT = 128
WIDE = KVD + STAT
VMEM = pl.BlockSpec(memory_space=pltpu.VMEM)
HBM = pl.BlockSpec(memory_space=pltpu.HBM)


def kernel_call(body, out_shape, in_specs, scratch=(), out_specs=None, vmem_mib=8, cost=0.5):
    return pl.pallas_call(
        body,
        out_shape=out_shape,
        in_specs=in_specs,
        out_specs=out_specs or ([VMEM] * len(out_shape) if isinstance(out_shape, list) else VMEM),
        scratch_shapes=list(scratch),
        compiler_params=pltpu.CompilerParams(vmem_limit_bytes=vmem_mib * 2**20),
        cost_estimate=pl.CostEstimate(
            flops=int(cost * 1e9), bytes_accessed=int(cost * 3e6), transcendentals=0
        ),
    )


def iota(shape, dim):
    return lax.broadcasted_iota(jnp.int32, shape, dim)


def split3(value):
    high = value.astype(BF16).astype(F32)
    rest = value - high
    middle = rest.astype(BF16).astype(F32)
    return high, middle, rest - middle


def rows_of(ref):
    return jnp.concatenate([ref[r].astype(F32) for r in range(ref.shape[0])], axis=0)


def dot_nt(left, right):
    return lax.dot_general(left, right, (((1,), (1,)), ((), ())), preferred_element_type=F32)


def swap(value, axis, mask):
    pairs = [(i, i ^ mask) for i in range(lax.axis_size(axis))]
    return lax.ppermute(value, axis, pairs)


def after(value, *others):
    return lax.optimization_barrier((value, *others))[0]


def project_kernel(*refs):
    x_hbm, attn_hbm, moe_hbm, w_hbm, lengths_hbm, pages_hbm, routes_hbm, weights_hbm = refs[:8]
    heads_ref, x_ref, live_ref, routing_ref, gain_ref = refs[8:13]
    x_in, attn_gain, moe_gain, w_in, lengths, pages, routes, weights, sem = refs[13:]
    loads = [
        pltpu.make_async_copy(source, target, sem.at[i])
        for i, (source, target) in enumerate(
            [
                (lengths_hbm, lengths),
                (x_hbm, x_in),
                (attn_hbm, attn_gain),
                (w_hbm, w_in),
                (pages_hbm, pages),
                (routes_hbm, routes),
                (weights_hbm, weights),
                (moe_hbm, moe_gain),
            ]
        )
    ]
    for load in loads:
        load.start()
    requests = x_in.shape[0]
    row_count = requests * NSTEP
    shape = (row_count, STAT)
    loads[0].wait()
    row, lane = iota(shape, 0), iota(shape, 1)
    position = row % NSTEP
    for r in range(requests):
        position = position + jnp.where(row // NSTEP == r, lengths[r], 0)
    rates = jnp.exp((lane % (HD // 2)).astype(F32) * (-2.0 * math.log(10000.0) / HD))
    angle = position.astype(F32) * rates
    cosine = jnp.cos(angle)
    sine = jnp.where(lane % HD < HD // 2, -jnp.sin(angle), jnp.sin(angle))
    loads[1].wait()
    x = rows_of(x_in)
    x_ref[...] = x
    power = jnp.mean(x * x, axis=-1, keepdims=True)
    loads[2].wait()
    normed = (x * lax.rsqrt(power + EPS) * attn_gain[...].reshape(1, D)).astype(BF16)
    loads[3].wait()
    projected = dot_nt(normed, w_in[...])
    heads = w_in.shape[0] // HD
    first = lax.axis_index("seq") * heads
    for i in range(heads):
        one = projected[:, i * HD : (i + 1) * HD]
        both = jnp.concatenate([one, one], axis=1)
        turned = both * cosine + pltpu.roll(both, HD // 2, 1) * sine
        heads_ref[i] = jnp.where(first + i < HEADS + KVH, turned, both).astype(BF16)
    for load in loads[4:]:
        load.wait()
    slots = live_ref.shape[1]
    slot = iota((1, slots), 1)
    for r in range(requests):
        page = jnp.zeros((1, slots), jnp.int32)
        for j in range(slots // PAGE):
            page = jnp.where(slot // PAGE == j, pages[r, j], page)
        live = page * PAGE + slot % PAGE < lengths[r]
        live_ref[r : r + 1, :] = jnp.where(live, 1.0, 0.0)
    high, middle, low = split3(rows_of(weights))
    routing_ref[...] = jnp.concatenate(
        [rows_of(routes), high, middle, low, jnp.zeros((row_count, STAT - 4 * TOP), F32)], axis=1
    )
    gain_ref[...] = moe_gain[...].reshape(1, D)


def in_chip_order(near, far):
    first = lax.axis_index("seq") % 2 == 0
    return jnp.where(
        first, jnp.concatenate([near, far], axis=1), jnp.concatenate([far, near], axis=1)
    )


def gather_pieces(near_refs, far_refs, all_ref):
    core = lax.axis_index("seq") % 2
    for k in range(len(near_refs)):
        all_ref[core, k] = near_refs[k][...]
        all_ref[1 - core, k] = far_refs[k][...]


def paired(head, left, right):
    a = head(left)
    return jnp.where(iota(a.shape, 1) < HD, a, head(right))


def expanded(q_ref, r):
    rows = [q_ref[g, r * NSTEP : (r + 1) * NSTEP, :] for g in range(GROUP)]
    base = jnp.concatenate(rows + [jnp.zeros((NSTEP, KVD), F32)], axis=0)
    owner = iota(base.shape, 1) // HD
    return jnp.concatenate(
        [jnp.where(owner == k, base, 0.0) for k in range(KVH)], axis=0
    ).astype(BF16)


def attend_part(query, keys, values, live):
    scores = jnp.where(live, dot_nt(query, keys) * (HD ** (-0.5)), NEG)
    top = jnp.max(scores, axis=1, keepdims=True)
    exp_scores = jnp.where(live, jnp.exp(scores - top), 0.0)
    total = jnp.sum(exp_scores, axis=1, keepdims=True)
    return top, total, jnp.dot(exp_scores.astype(BF16), values, preferred_element_type=F32)


def place_rows(part_ref, r, row_count, top, total, sums):
    block = (GROUP + 1) * NSTEP
    owner = iota((block, KVD), 1) // HD
    lane = iota((block, STAT), 1)
    own_sums = jnp.zeros((block, KVD), F32)
    stats = jnp.zeros((block, STAT), F32)
    for k in range(KVH):
        rows = slice(k * block, (k + 1) * block)
        own_sums = jnp.where(owner == k, sums[rows], own_sums)
        value = jnp.where(lane < 3 * KVH, top[rows], total[rows])
        stats = jnp.where(lane % KVH == k, value, stats)
    high, middle, low = split3(stats)
    part = (lane // KVH) % 3
    stats = jnp.where(part == 0, high, jnp.where(part == 1, middle, low))
    for g in range(GROUP):
        rows = slice(g * row_count + r * NSTEP, g * row_count + (r + 1) * NSTEP)
        part_ref[rows, :KVD] = own_sums[g * NSTEP : (g + 1) * NSTEP]
        part_ref[rows, KVD:] = stats[g * NSTEP : (g + 1) * NSTEP]


def head_of(all_ref):
    chip = lax.axis_index("seq") // 2
    heads = all_ref.shape[2]

    def head(h):
        owner = h // heads
        return all_ref[owner % 2, chip ^ (owner // 2), h % heads].astype(F32)

    return head


def query_rows(head, q_ref):
    for g in range(GROUP):
        for m in range(KVH // 2):
            q_ref[g, :, m * STAT : (m + 1) * STAT] = paired(
                head, GROUP * 2 * m + g, GROUP * (2 * m + 1) + g
            )


def attend_kernel(chips, *refs):
    near_refs, far_refs = refs[:chips], refs[chips : 2 * chips]
    live_ref, k_ref, v_ref, out_ref, all_ref, q_ref, part_ref = refs[2 * chips :]
    requests = k_ref.shape[0]
    gather_pieces(near_refs, far_refs, all_ref)
    query_rows(head_of(all_ref), q_ref)
    for r in range(requests):
        live = live_ref[r : r + 1, :] > 0.5
        place_rows(
            part_ref,
            r,
            requests * NSTEP,
            *attend_part(expanded(q_ref, r), k_ref[r], v_ref[r], live),
        )
    out_ref[...] = part_ref[...].astype(BF16)


def fresh_kernel(chips, *refs):
    near_refs, far_refs = refs[:chips], refs[chips : 2 * chips]
    out_ref, all_ref, q_ref, part_ref = refs[2 * chips :]
    gather_pieces(near_refs, far_refs, all_ref)
    head = head_of(all_ref)
    query_rows(head, q_ref)
    row_count = q_ref.shape[1]
    pad = jnp.zeros((STAT - row_count, KVD), F32)

    def new_rows(first):
        pieces = [paired(head, first + 2 * m, first + 2 * m + 1) for m in range(KVH // 2)]
        return jnp.concatenate([jnp.concatenate(pieces, axis=1), pad], axis=0).astype(BF16)

    keys, values = new_rows(HEADS), new_rows(HEADS + KVH)
    shape = ((GROUP + 1) * NSTEP * KVH, STAT)
    slot, step = iota(shape, 1), iota(shape, 0) % NSTEP
    for r in range(row_count // NSTEP):
        live = (slot // NSTEP == r) & (slot % NSTEP <= step)
        place_rows(
            part_ref, r, row_count, *attend_part(expanded(q_ref, r), keys, values, live)
        )
    out_ref[...] = part_ref[...].astype(BF16)


def merge_kernel(count, *refs):
    part_refs = refs[:count]
    x_ref, gain_ref, routing_ref, near_w, far_w, out_ref, resid_ref = refs[count:]
    parts = [ref[...].astype(F32) for ref in part_refs]
    tops, totals = [], []
    for part in parts:
        stats = part[:, KVD:]
        full = stats + (
            pltpu.roll(stats, STAT - KVH, 1) + pltpu.roll(stats, STAT - 2 * KVH, 1)
        )
        tops.append(full)
        totals.append(pltpu.roll(full, STAT - 3 * KVH, 1))
    highest = tops[0]
    for top in tops[1:]:
        highest = jnp.maximum(highest, top)
    factors = [jnp.exp(top - highest) for top in tops]
    denominator = factors[0] * totals[0]
    for factor, total in zip(factors[1:], totals[1:]):
        denominator = denominator + factor * total
    inverse = 1.0 / denominator
    row_total = parts[0].shape[0]
    row_count = row_total // GROUP
    left = iota((row_total, STAT), 1) < HD
    columns = []
    for m in range(KVH // 2):
        value = jnp.zeros((row_total, STAT), F32)
        for part, factor in zip(parts, factors):
            spread = jnp.where(left, factor[:, 2 * m : 2 * m + 1], factor[:, 2 * m + 1 : 2 * m + 2])
            value = value + spread * part[:, m * STAT : (m + 1) * STAT]
        spread = jnp.where(left, inverse[:, 2 * m : 2 * m + 1], inverse[:, 2 * m + 1 : 2 * m + 2])
        columns.append(value * spread)

    def head(h, side):
        k, g = h // GROUP, h % GROUP
        rows = columns[k // 2][g * row_count : (g + 1) * row_count]
        return rows if k % 2 == side else pltpu.roll(rows, HD, 1)

    left = iota((row_count, STAT), 1) < HD
    attended = jnp.concatenate(
        [jnp.where(left, head(2 * n, 0), head(2 * n + 1, 1)) for n in range(HEADS // 2)], axis=1
    ).astype(BF16)
    share = in_chip_order(dot_nt(attended, near_w[...]), dot_nt(attended, far_w[...]))
    width = near_w.shape[0]
    member = lax.axis_index("seq")
    both = pl.ds(pl.multiple_of((member // 2) * (2 * width), STAT), 2 * width)
    resid = x_ref[:, both] + share
    resid_ref[...] = jnp.where(member % 2 == 0, resid[:, :width], resid[:, width:])
    stats = routing_ref[...]
    lane = iota(stats.shape, 1)
    for i, value in enumerate(split3(jnp.sum(resid * resid, axis=1, keepdims=True))):
        stats = jnp.where(lane == 4 * TOP + i, value, stats)
    out_ref[:, : 2 * width] = (resid * gain_ref[:, both]).astype(BF16)
    out_ref[:, 2 * width :] = stats.astype(BF16)


def across(column, eye):
    return jnp.sum(jnp.where(eye, column, 0.0), axis=0, keepdims=True)


def gate_kernel(groups, *refs):
    piece_refs, w_ref = refs[:groups], refs[groups]
    message_refs = refs[groups + 1 : 2 * groups + 1]
    placed_ref, scale_ref, full_ref = refs[2 * groups + 1 :]
    member, me = lax.axis_index("seq"), lax.axis_index("req")
    width = w_ref.shape[1]
    row_count = piece_refs[0].shape[0]
    tokens = groups * row_count
    pieces = jnp.concatenate([ref[...].astype(F32) for ref in piece_refs], axis=0)
    mixed, routing = pieces[:, :width].astype(BF16), pieces[:, width:]
    power = routing[:, 4 * TOP : 4 * TOP + 1] + (
        routing[:, 4 * TOP + 1 : 4 * TOP + 2] + routing[:, 4 * TOP + 2 : 4 * TOP + 3]
    )
    chosen = routing[:, :TOP]
    gates = routing[:, TOP : 2 * TOP] + (
        routing[:, 2 * TOP : 3 * TOP] + routing[:, 3 * TOP : 4 * TOP]
    )
    experts = w_ref.shape[0]
    square = (tokens, tokens)
    eye = iota(square, 0) == iota(square, 1)
    earlier = (iota(square, 0) < iota(square, 1)) & (
        iota(square, 0) // row_count == iota(square, 1) // row_count
    )
    slots = groups * CAP
    shape = (slots, tokens)
    home = (iota(shape, 1) // row_count) ^ (member // 2)
    slot = iota(shape, 0)
    same_group = slot // CAP == home
    ordinal_of_slot = (slot % CAP).astype(F32)
    placed, scales, powers = [], [], []
    power_row = across(power, eye)
    for e in range(experts):
        match = chosen == (member * experts + e).astype(F32)
        routed = jnp.max(jnp.where(match, 1.0, 0.0), axis=1, keepdims=True)
        scale = jnp.sum(jnp.where(match, gates, 0.0), axis=1, keepdims=True)
        ordinal = across(routed, earlier)
        here = same_group & (across(routed, eye) > 0.5) & (ordinal_of_slot == ordinal)
        placed.append(jnp.where(here, 1.0, 0.0))
        scales.append(jnp.sum(jnp.where(here, across(scale, eye), 0.0), axis=1, keepdims=True))
        powers.append(jnp.sum(jnp.where(here, power_row, 0.0), axis=1, keepdims=True))
    lane = iota((slots, STAT), 1)
    all_placed = jnp.concatenate(placed, axis=0).astype(BF16)
    taken = jnp.dot(all_placed, mixed, preferred_element_type=F32).astype(BF16)
    for e in range(experts):
        rows = slice(e * slots, (e + 1) * slots)
        placed_ref[e] = all_placed[rows]
        scale_ref[e] = jnp.broadcast_to(scales[e], scale_ref.shape[1:])
        full_ref[e, :, : 2 * FFE] = jnp.dot(
            taken[rows], w_ref[e], preferred_element_type=F32
        ).astype(BF16)
        high, middle, low = split3(powers[e])
        full_ref[e, :, 2 * FFE :] = jnp.where(
            lane == 0, high, jnp.where(lane == 1, middle, jnp.where(lane == 2, low, 0.0))
        ).astype(BF16)
    for k in range(groups):
        message_refs[k][...] = full_ref[me ^ k]


def hidden_kernel(*refs):
    gate_up = refs[0][...].astype(F32)
    for ref in refs[1:-1]:
        gate_up = gate_up + ref[...].astype(F32)
    power = gate_up[:, 2 * FFE : 2 * FFE + 1] + (
        gate_up[:, 2 * FFE + 1 : 2 * FFE + 2] + gate_up[:, 2 * FFE + 2 : 2 * FFE + 3]
    )
    gate_up = gate_up[:, : 2 * FFE] * lax.rsqrt(power / D + EPS)
    gate, up = gate_up[:, :FFE], gate_up[:, FFE:]
    refs[-1][...] = (gate / (1.0 + jnp.exp(-gate)) * up).astype(BF16)


def down_kernel(groups, *refs):
    hidden_refs = refs[:groups]
    w_ref, placed_ref, scale_ref, send_ref, keep_ref = refs[groups:]
    me, core = lax.axis_index("req"), lax.axis_index("seq") % 2
    total = jnp.zeros((placed_ref.shape[2], w_ref.shape[2]), F32)
    for k, hidden_ref in enumerate(hidden_refs):
        expert = me ^ k
        produced = jnp.dot(hidden_ref[...], w_ref[expert], preferred_element_type=F32)
        total = total + lax.dot_general(
            placed_ref[expert],
            (produced * scale_ref[expert][:, :1]).astype(BF16),
            (((0,), (0,)), ((), ())),
            preferred_element_type=F32,
        )
    width = w_ref.shape[2] // 2
    left, right = total[:, :width], total[:, width:]
    send_ref[...] = jnp.where(core == 0, left, right).astype(BF16)
    keep_ref[...] = jnp.where(core == 0, right, left)


def spread_kernel(keep_ref, arrived_ref, *out_refs):
    total = keep_ref[...] + arrived_ref[...].astype(F32)
    row_count = out_refs[0].shape[0]
    for k, out_ref in enumerate(out_refs):
        out_ref[...] = total[k * row_count : (k + 1) * row_count].astype(BF16)


def final_kernel(resid_ref, *refs):
    arrived_refs, out_ref = refs[:-1], refs[-1]
    total = resid_ref[...]
    for ref in arrived_refs:
        total = total + ref[...].astype(F32)
    for r in range(out_ref.shape[0]):
        out_ref[r] = total[r * NSTEP : (r + 1) * NSTEP].astype(BF16)


def staged(
    x_in,
    attn_gain,
    moe_gain,
    w_qkv,
    w_o,
    cache_k,
    cache_v,
    page_map,
    lengths,
    routes,
    route_weights,
    w_gate_up,
    w_down,
):
    requests = x_in.shape[0]
    row_count = requests * NSTEP
    members, groups = lax.axis_size("seq"), lax.axis_size("req")
    chips = members // 2
    heads = w_qkv.shape[1] // HD
    width = w_o.shape[1]

    own_heads, x, live, routing, gain = kernel_call(
        project_kernel,
        [
            jax.ShapeDtypeStruct((heads, row_count, 2 * HD), BF16),
            jax.ShapeDtypeStruct((row_count, D), F32),
            jax.ShapeDtypeStruct((requests, cache_k.shape[1]), F32),
            jax.ShapeDtypeStruct((row_count, STAT), F32),
            jax.ShapeDtypeStruct((1, D), F32),
        ],
        [HBM] * 8,
        [
            pltpu.VMEM(x_in.shape, BF16),
            pltpu.VMEM((D,), F32),
            pltpu.VMEM((D,), F32),
            pltpu.VMEM((w_qkv.shape[1], D), BF16),
            pltpu.SMEM(lengths.shape, jnp.int32),
            pltpu.SMEM(page_map.shape, jnp.int32),
            pltpu.VMEM(routes.shape, jnp.int32),
            pltpu.VMEM(route_weights.shape, F32),
            pltpu.SemaphoreType.DMA((8,)),
        ],
        vmem_mib=60,
        cost=5.0,
    )(x_in, attn_gain, moe_gain, w_qkv.T, lengths, page_map, routes, route_weights)
    def gathered(own, *first):
        near = [swap(own, "seq", 2 * k) for k in range(chips - 1, 0, -1)]
        near = [own] + near[::-1]
        near[1] = after(near[1], *first) if first else near[1]
        return near, [swap(piece, "seq", 1) for piece in near]

    near, far = gathered(own_heads)
    def gathered(own, *first):
        near = [swap(own, "seq", 2 * k) for k in range(chips - 1, 0, -1)]
        near = [own] + near[::-1]
        near[1] = after(near[1], *first) if first else near[1]
        return near, [swap(piece, "seq", 1) for piece in near]

    near, far = gathered(own_heads)
    def gathered(own, *first):
        near = [swap(own, "seq", 2 * k) for k in range(chips - 1, 0, -1)]
        near = [own] + near[::-1]
        near[1] = after(near[1], *first) if first else near[1]
        return near, [swap(piece, "seq", 1) for piece in near]

    near, far = gathered(own_heads)
    down = lax.all_to_all(w_down, "req", 0, 0, tiled=True)
    part_shape = jax.ShapeDtypeStruct((GROUP * row_count, WIDE), BF16)
    head_scratch = [
        pltpu.VMEM((2, chips, heads, row_count, 2 * HD), BF16),
        pltpu.VMEM((GROUP, row_count, KVD), F32),
        pltpu.VMEM((GROUP * row_count, WIDE), F32),
    ]
    part = kernel_call(
        lambda *refs: attend_kernel(chips, *refs),
        part_shape,
        [VMEM] * (2 * chips + 3),
        head_scratch,
    )(*near, *far, live, cache_k, cache_v)
    fresh = kernel_call(
        lambda *refs: fresh_kernel(chips, *refs),
        part_shape,
        [VMEM] * (2 * chips),
        head_scratch,
        cost=0.5,
    )(*near, *far)
    near, far = gathered(part, fresh)
    packed, resid = kernel_call(
        lambda *refs: merge_kernel(members + 1, *refs),
        [
            jax.ShapeDtypeStruct((row_count, 2 * width + STAT), BF16),
            jax.ShapeDtypeStruct((row_count, width), F32),
        ],
        [VMEM] * (members + 6),
    )(*near, *far, fresh, x, gain, routing, w_o.T, swap(w_o.T, "seq", 1))

    def crossing(mask):
        return [
            ((2 * p + c) * groups + q, (2 * (q ^ mask) + 1 - c) * groups + p)
            for p in range(chips)
            for c in range(2)
            for q in range(groups)
        ]

    place = ("seq", "req")
    pieces = [lax.ppermute(packed, place, crossing(k)) for k in range(groups)]
    experts = w_gate_up.shape[0]
    slots = groups * CAP
    *messages, placed, scale = kernel_call(
        lambda *refs: gate_kernel(groups, *refs),
        [jax.ShapeDtypeStruct((slots, 2 * FFE + STAT), BF16)] * groups
        + [
            jax.ShapeDtypeStruct((experts, slots, groups * row_count), BF16),
            jax.ShapeDtypeStruct((experts, slots, STAT), F32),
        ],
        [VMEM] * (groups + 1),
        [pltpu.VMEM((experts, slots, 2 * FFE + STAT), BF16)],
    )(*pieces, w_gate_up)
    sums = [messages[0]] + [swap(messages[k], "req", k) for k in (3, 1, 2)]
    hidden = kernel_call(
        hidden_kernel, jax.ShapeDtypeStruct((slots, FFE), BF16), [VMEM] * groups
    )(*sums)
    hiddens = [hidden] + [swap(hidden, "req", k) for k in range(1, groups)]
    send, keep = kernel_call(
        lambda *refs: down_kernel(groups, *refs),
        [
            jax.ShapeDtypeStruct((groups * row_count, width), BF16),
            jax.ShapeDtypeStruct((groups * row_count, width), F32),
        ],
        [VMEM] * (groups + 3),
    )(*hiddens, w_down, placed, scale)
    outs = kernel_call(
        spread_kernel, [jax.ShapeDtypeStruct((row_count, width), BF16)] * groups, [VMEM] * 2
    )(keep, swap(send, "seq", 1))
    arrived = [
        lax.ppermute(out, place, [(target, source) for source, target in crossing(k)])
        for k, out in enumerate(outs)
    ]
    return kernel_call(
        final_kernel,
        jax.ShapeDtypeStruct((requests, NSTEP, width), BF16),
        [VMEM] * (groups + 1),
    )(resid, *arrived)


def local(*args):
    w_qkv, w_o, w_gate_up = args[3], args[4], args[11]
    members, groups = lax.axis_size("seq"), lax.axis_size("req")
    fits = (
        members == 8
        and groups == 4
        and w_qkv.shape[1] % HD == 0
        and w_gate_up.shape[0] == groups
        and (2 * w_o.shape[1]) % STAT == 0
    )
    return staged(*args) if fits else plain(*args)


def solution(mesh):
    in_specs = (
        P("req", None, None),
        P(),
        P(),
        P(None, "seq"),
        P(None, "seq"),
        P("req", "seq", None),
        P("req", "seq", None),
        P("req", "seq"),
        P("req"),
        P("req", None, None),
        P("req", None, None),
        P("seq", "req", None),
        P("seq", None, "req"),
    )
    out_specs = P("req", None, "seq")
    return jax.shard_map(local, mesh=mesh, in_specs=in_specs, out_specs=out_specs, check_vma=False)
```

```python
import math

import jax
import jax.numpy as jnp
from jax import lax
from jax.experimental import pallas as pl
from jax.experimental.pallas import tpu as pltpu
from jax.sharding import PartitionSpec as P

D = 1536
HEADS = 24
KVH = 8
HD = 64
FFE = 512
TOP = 8
NSTEP = 4
PAGE = 16
ATT = 1536
KVD = 512
GROUP = 3
CAP = 12


EPS = 1e-05
NEG = -1e30


def combined_all(value, axis, join):
    pieces = jax.tree.map(lambda part: lax.all_gather(part, axis), value)
    head = jax.tree.map(lambda part: part[0], pieces)
    tail = jax.tree.map(lambda part: part[1:], pieces)
    so_far, _ = lax.scan(lambda so_far, piece: (join(so_far, piece), None), head, tail)
    return so_far


def normalize(values, gain):
    power = jnp.mean(values * values, axis=-1, keepdims=True)
    return values * lax.rsqrt(power + EPS) * gain


def rotate(values, position):
    half = values.shape[-1] // 2
    rates = jnp.exp(
        jnp.arange(half, dtype=jnp.float32) * (-2.0 * math.log(10000.0) / values.shape[-1])
    )
    angle = position[..., None, None] * rates
    cosine = jnp.cos(angle)
    sine = jnp.sin(angle)
    first_half = values[..., :half]
    second_half = values[..., half:]
    return jnp.concatenate(
        [first_half * cosine - second_half * sine, second_half * cosine + first_half * sine],
        axis=-1,
    )


def softmax_join(left, right):
    left_top, left_total, left_sums = left
    right_top, right_total, right_sums = right
    highest = jnp.maximum(left_top, right_top)
    left_factor = jnp.exp(left_top - highest)
    right_factor = jnp.exp(right_top - highest)
    row_count, head_count = highest.shape
    left_part = left_sums.reshape(row_count, head_count, -1) * left_factor[:, :, None]
    right_part = right_sums.reshape(row_count, head_count, -1) * right_factor[:, :, None]
    joined = (left_part + right_part).reshape(row_count, -1)
    return (highest, left_total * left_factor + right_total * right_factor, joined)


def project_with(left, piece):
    return jnp.dot(left, piece, preferred_element_type=jnp.float32)


def plain(
    x_in,
    attn_gain,
    moe_gain,
    w_qkv,
    w_o,
    cache_k,
    cache_v,
    page_map,
    lengths,
    routes,
    route_weights,
    w_gate_up,
    w_down,
):
    local_requests = x_in.shape[0]
    row_count = local_requests * NSTEP
    inputs = x_in.astype(jnp.float32).reshape(row_count, D)
    normed = normalize(inputs, attn_gain).astype(jnp.bfloat16)
    projected = project_with(normed, lax.all_gather(w_qkv, "seq", axis=1, tiled=True))
    queries = projected[:, :ATT].reshape(local_requests, NSTEP, HEADS, HD)
    keys_new = projected[:, ATT : ATT + KVD].reshape(local_requests, NSTEP, KVH, HD)
    values_new = (
        projected[:, ATT + KVD :].reshape(local_requests, NSTEP, KVH, HD).astype(jnp.bfloat16)
    )
    position = (lengths[:, None] + jnp.arange(NSTEP, dtype=jnp.int32)[None, :]).astype(jnp.float32)
    queries = (
        rotate(queries, position)
        .astype(jnp.bfloat16)
        .reshape(local_requests, NSTEP, KVH, GROUP, HD)
    )
    keys_new = rotate(keys_new, position).astype(jnp.bfloat16)
    scale = HD ** (-0.5)
    slot_count = cache_k.shape[1]
    cached_keys = cache_k.reshape(local_requests, slot_count, KVH, HD)
    cached_values = cache_v.reshape(local_requests, slot_count, KVH, HD)
    slot_position = (
        page_map[:, :, None] * PAGE + jnp.arange(PAGE, dtype=jnp.int32)[None, None, :]
    ).reshape(local_requests, slot_count)
    live = (slot_position < lengths[:, None])[:, None, None, None, :]
    scores = (
        jnp.einsum("rskgd,rtkd->rskgt", queries, cached_keys, preferred_element_type=jnp.float32)
        * scale
    )
    scores = jnp.where(live, scores, NEG)
    local_top = jnp.max(scores, axis=-1)
    exp_scores = jnp.where(live, jnp.exp(scores - local_top[..., None]), 0.0)
    local_total = jnp.sum(exp_scores, axis=-1).reshape(row_count, HEADS)
    local_sums = jnp.einsum(
        "rskgt,rtkd->rskgd",
        exp_scores.astype(jnp.bfloat16),
        cached_values,
        preferred_element_type=jnp.float32,
    ).reshape(row_count, ATT)
    local_top = local_top.reshape(row_count, HEADS)
    cache_top, cache_total, cache_sums = combined_all(
        (local_top, local_total, local_sums), "seq", softmax_join
    )
    causal = (
        jnp.arange(NSTEP, dtype=jnp.int32)[:, None] >= jnp.arange(NSTEP, dtype=jnp.int32)[None, :]
    )[None, :, None, None, :]
    fresh = (
        jnp.einsum("rskgd,rukd->rskgu", queries, keys_new, preferred_element_type=jnp.float32)
        * scale
    )
    fresh = jnp.where(causal, fresh, NEG).reshape(row_count, HEADS, NSTEP)
    highest = jnp.maximum(cache_top, jnp.max(fresh, axis=-1))
    fresh_exp = jnp.exp(fresh - highest[:, :, None])
    carried = jnp.exp(cache_top - highest)
    denominator = cache_total * carried + jnp.sum(fresh_exp, axis=-1)
    fresh_probs = fresh_exp.reshape(local_requests, NSTEP, KVH, GROUP, NSTEP).astype(jnp.bfloat16)
    fresh_sums = jnp.einsum(
        "rskgu,rukd->rskgd", fresh_probs, values_new, preferred_element_type=jnp.float32
    ).reshape(row_count, HEADS, HD)
    numerator = cache_sums.reshape(row_count, HEADS, HD) * carried[:, :, None] + fresh_sums
    attended = (numerator / denominator[:, :, None]).reshape(row_count, ATT).astype(jnp.bfloat16)
    attn_mixed = project_with(attended, lax.all_gather(w_o, "seq", axis=1, tiled=True))
    resid = inputs + attn_mixed
    mixed_in = normalize(resid, moe_gain).astype(jnp.bfloat16)
    local_experts = w_gate_up.shape[0]
    groups = lax.axis_size("req")
    owned = lax.axis_index("seq") * local_experts + jnp.arange(local_experts, dtype=jnp.int32)
    chosen = routes.reshape(row_count, TOP)
    gates = route_weights.reshape(row_count, TOP)
    matches = chosen[None, :, :] == owned[:, None, None]
    routed = jnp.any(matches, axis=-1)
    route_scale = jnp.sum(jnp.where(matches, gates[None, :, :], 0.0), axis=-1)
    ordinal = jnp.cumsum(routed.astype(jnp.int32), axis=1) - 1
    placed = routed[:, :, None] & (
        ordinal[:, :, None] == jnp.arange(CAP, dtype=jnp.int32)[None, None, :]
    )
    outgoing = jnp.einsum(
        "erc,rd->ecd", placed.astype(jnp.bfloat16), mixed_in, preferred_element_type=jnp.float32
    ).astype(jnp.bfloat16)
    arrived = lax.all_to_all(outgoing[:, None], "req", split_axis=3, concat_axis=1, tiled=True)
    slice_width = arrived.shape[3]
    arrived = arrived.reshape(local_experts, groups * CAP, slice_width)
    partial_values = jnp.einsum(
        "end,edf->enf", arrived, w_gate_up, preferred_element_type=jnp.float32
    )
    gate_up = lax.psum(partial_values, "req")
    hidden = (jax.nn.silu(gate_up[..., :FFE]) * gate_up[..., FFE:]).astype(jnp.bfloat16)
    produced = jnp.einsum("enf,efd->end", hidden, w_down, preferred_element_type=jnp.float32)
    returned = lax.all_to_all(
        produced.reshape(local_experts, groups, CAP, slice_width),
        "req",
        split_axis=1,
        concat_axis=3,
        tiled=True,
    )[:, 0]
    weighted = placed.astype(jnp.float32) * route_scale[:, :, None]
    expert_total = jnp.einsum("erc,ecd->rd", weighted, returned, precision=lax.Precision.HIGHEST)
    own_share = lax.psum_scatter(expert_total, "seq", scatter_dimension=1, tiled=True)
    share_width = own_share.shape[1]
    resid_share = lax.dynamic_slice_in_dim(
        resid, lax.axis_index("seq") * share_width, share_width, 1
    )
    return (
        (resid_share + own_share).astype(jnp.bfloat16).reshape(local_requests, NSTEP, share_width)
    )


F32 = jnp.float32
BF16 = jnp.bfloat16
STAT = 128
WIDE = KVD + STAT
VMEM = pl.BlockSpec(memory_space=pltpu.VMEM)
SMEM = pl.BlockSpec(memory_space=pltpu.SMEM)
HBM = pl.BlockSpec(memory_space=pltpu.HBM)


def kernel_call(body, out_shape, in_specs, scratch=(), out_specs=None, vmem_mib=8, cost=0.5):
    return pl.pallas_call(
        body,
        out_shape=out_shape,
        in_specs=in_specs,
        out_specs=out_specs or ([VMEM] * len(out_shape) if isinstance(out_shape, list) else VMEM),
        scratch_shapes=list(scratch),
        compiler_params=pltpu.CompilerParams(vmem_limit_bytes=vmem_mib * 2**20),
        cost_estimate=pl.CostEstimate(
            flops=int(cost * 1e9), bytes_accessed=int(cost * 3e6), transcendentals=0
        ),
    )


def iota(shape, dim):
    return lax.broadcasted_iota(jnp.int32, shape, dim)


def split3(value):
    high = value.astype(BF16).astype(F32)
    rest = value - high
    middle = rest.astype(BF16).astype(F32)
    return high, middle, rest - middle


def rows_of(ref):
    return jnp.concatenate([ref[r].astype(F32) for r in range(ref.shape[0])], axis=0)


def dot_nt(left, right):
    return lax.dot_general(left, right, (((1,), (1,)), ((), ())), preferred_element_type=F32)


def swap(value, axis, mask):
    pairs = [(i, i ^ mask) for i in range(lax.axis_size(axis))]
    return lax.ppermute(value, axis, pairs)


def after(value, *others):
    return lax.optimization_barrier((value, *others))[0]


def project_kernel(*refs):
    x_hbm, attn_hbm, w_hbm, lengths_hbm, heads_ref, x_ref = refs[:6]
    x_in, attn_gain, w_in, lengths, sem = refs[6:]
    loads = [
        pltpu.make_async_copy(source, target, sem.at[i])
        for i, (source, target) in enumerate(
            [(lengths_hbm, lengths), (x_hbm, x_in), (attn_hbm, attn_gain), (w_hbm, w_in)]
        )
    ]
    for load in loads:
        load.start()
    requests = x_in.shape[0]
    row_count = requests * NSTEP
    shape = (row_count, STAT)
    loads[0].wait()
    row, lane = iota(shape, 0), iota(shape, 1)
    position = row % NSTEP
    for r in range(requests):
        position = position + jnp.where(row // NSTEP == r, lengths[r], 0)
    rates = jnp.exp((lane % (HD // 2)).astype(F32) * (-2.0 * math.log(10000.0) / HD))
    angle = position.astype(F32) * rates
    cosine = jnp.cos(angle)
    sine = jnp.where(lane % HD < HD // 2, -jnp.sin(angle), jnp.sin(angle))
    loads[1].wait()
    x = rows_of(x_in)
    x_ref[...] = x
    power = jnp.mean(x * x, axis=-1, keepdims=True)
    loads[2].wait()
    normed = (x * lax.rsqrt(power + EPS) * attn_gain[...].reshape(1, D)).astype(BF16)
    loads[3].wait()
    projected = dot_nt(normed, w_in[...])
    heads = w_in.shape[0] // HD
    first = lax.axis_index("seq") * heads
    for i in range(heads):
        one = projected[:, i * HD : (i + 1) * HD]
        both = jnp.concatenate([one, one], axis=1)
        turned = both * cosine + pltpu.roll(both, HD // 2, 1) * sine
        heads_ref[i] = jnp.where(first + i < HEADS + KVH, turned, both).astype(BF16)


def prepare_kernel(heads_in, pages, lengths, routes, weights, moe_gain, *out_refs):
    heads_ref, live_ref, routing_ref, gain_ref = out_refs
    heads_ref[...] = heads_in[...]
    slots = live_ref.shape[1]
    slot = iota((1, slots), 1)
    for r in range(live_ref.shape[0]):
        page = jnp.zeros((1, slots), jnp.int32)
        for j in range(slots // PAGE):
            page = jnp.where(slot // PAGE == j, pages[r, j], page)
        live = page * PAGE + slot % PAGE < lengths[r]
        live_ref[r : r + 1, :] = jnp.where(live, 1.0, 0.0)
    row_count = routing_ref.shape[0]
    high, middle, low = split3(rows_of(weights))
    routing_ref[...] = jnp.concatenate(
        [rows_of(routes), high, middle, low, jnp.zeros((row_count, STAT - 4 * TOP), F32)], axis=1
    )
    gain_ref[...] = moe_gain[...].reshape(1, D)


def in_chip_order(near, far):
    first = lax.axis_index("seq") % 2 == 0
    return jnp.where(
        first, jnp.concatenate([near, far], axis=1), jnp.concatenate([far, near], axis=1)
    )


def gather_pieces(near_refs, far_refs, all_ref):
    core = lax.axis_index("seq") % 2
    for k in range(len(near_refs)):
        all_ref[core, k] = near_refs[k][...]
        all_ref[1 - core, k] = far_refs[k][...]


def paired(head, left, right):
    a = head(left)
    return jnp.where(iota(a.shape, 1) < HD, a, head(right))


def expanded(q_ref, r):
    rows = [q_ref[g, r * NSTEP : (r + 1) * NSTEP, :] for g in range(GROUP)]
    base = jnp.concatenate(rows + [jnp.zeros((NSTEP, KVD), F32)], axis=0)
    owner = iota(base.shape, 1) // HD
    return jnp.concatenate(
        [jnp.where(owner == k, base, 0.0) for k in range(KVH)], axis=0
    ).astype(BF16)


def attend_part(query, keys, values, live):
    scores = jnp.where(live, dot_nt(query, keys) * (HD ** (-0.5)), NEG)
    top = jnp.max(scores, axis=1, keepdims=True)
    exp_scores = jnp.where(live, jnp.exp(scores - top), 0.0)
    total = jnp.sum(exp_scores, axis=1, keepdims=True)
    return top, total, jnp.dot(exp_scores.astype(BF16), values, preferred_element_type=F32)


def place_rows(part_ref, r, row_count, top, total, sums):
    block = (GROUP + 1) * NSTEP
    owner = iota((block, KVD), 1) // HD
    lane = iota((block, STAT), 1)
    own_sums = jnp.zeros((block, KVD), F32)
    stats = jnp.zeros((block, STAT), F32)
    for k in range(KVH):
        rows = slice(k * block, (k + 1) * block)
        own_sums = jnp.where(owner == k, sums[rows], own_sums)
        value = jnp.where(lane < 3 * KVH, top[rows], total[rows])
        stats = jnp.where(lane % KVH == k, value, stats)
    high, middle, low = split3(stats)
    part = (lane // KVH) % 3
    stats = jnp.where(part == 0, high, jnp.where(part == 1, middle, low))
    for g in range(GROUP):
        rows = slice(g * row_count + r * NSTEP, g * row_count + (r + 1) * NSTEP)
        part_ref[rows, :KVD] = own_sums[g * NSTEP : (g + 1) * NSTEP]
        part_ref[rows, KVD:] = stats[g * NSTEP : (g + 1) * NSTEP]


def head_of(all_ref):
    chip = lax.axis_index("seq") // 2
    heads = all_ref.shape[2]

    def head(h):
        owner = h // heads
        return all_ref[owner % 2, chip ^ (owner // 2), h % heads].astype(F32)

    return head


def query_rows(head, q_ref):
    for g in range(GROUP):
        for m in range(KVH // 2):
            q_ref[g, :, m * STAT : (m + 1) * STAT] = paired(
                head, GROUP * 2 * m + g, GROUP * (2 * m + 1) + g
            )


def attend_kernel(chips, *refs):
    near_refs, far_refs = refs[:chips], refs[chips : 2 * chips]
    live_ref, k_ref, v_ref, out_ref, all_ref, q_ref, part_ref = refs[2 * chips :]
    requests = k_ref.shape[0]
    gather_pieces(near_refs, far_refs, all_ref)
    query_rows(head_of(all_ref), q_ref)
    for r in range(requests):
        live = live_ref[r : r + 1, :] > 0.5
        place_rows(
            part_ref,
            r,
            requests * NSTEP,
            *attend_part(expanded(q_ref, r), k_ref[r], v_ref[r], live),
        )
    out_ref[...] = part_ref[...].astype(BF16)


def fresh_kernel(chips, *refs):
    near_refs, far_refs = refs[:chips], refs[chips : 2 * chips]
    out_ref, all_ref, q_ref, part_ref = refs[2 * chips :]
    gather_pieces(near_refs, far_refs, all_ref)
    head = head_of(all_ref)
    query_rows(head, q_ref)
    row_count = q_ref.shape[1]
    pad = jnp.zeros((STAT - row_count, KVD), F32)

    def new_rows(first):
        pieces = [paired(head, first + 2 * m, first + 2 * m + 1) for m in range(KVH // 2)]
        return jnp.concatenate([jnp.concatenate(pieces, axis=1), pad], axis=0).astype(BF16)

    keys, values = new_rows(HEADS), new_rows(HEADS + KVH)
    shape = ((GROUP + 1) * NSTEP * KVH, STAT)
    slot, step = iota(shape, 1), iota(shape, 0) % NSTEP
    for r in range(row_count // NSTEP):
        live = (slot // NSTEP == r) & (slot % NSTEP <= step)
        place_rows(
            part_ref, r, row_count, *attend_part(expanded(q_ref, r), keys, values, live)
        )
    out_ref[...] = part_ref[...].astype(BF16)


def merge_kernel(count, *refs):
    part_refs = refs[:count]
    x_ref, gain_ref, routing_ref, near_w, far_w, out_ref, resid_ref = refs[count:]
    parts = [ref[...].astype(F32) for ref in part_refs]
    tops, totals = [], []
    for part in parts:
        stats = part[:, KVD:]
        full = stats + (
            pltpu.roll(stats, STAT - KVH, 1) + pltpu.roll(stats, STAT - 2 * KVH, 1)
        )
        tops.append(full)
        totals.append(pltpu.roll(full, STAT - 3 * KVH, 1))
    highest = tops[0]
    for top in tops[1:]:
        highest = jnp.maximum(highest, top)
    factors = [jnp.exp(top - highest) for top in tops]
    denominator = factors[0] * totals[0]
    for factor, total in zip(factors[1:], totals[1:]):
        denominator = denominator + factor * total
    inverse = 1.0 / denominator
    row_total = parts[0].shape[0]
    row_count = row_total // GROUP
    left = iota((row_total, STAT), 1) < HD
    columns = []
    for m in range(KVH // 2):
        value = jnp.zeros((row_total, STAT), F32)
        for part, factor in zip(parts, factors):
            spread = jnp.where(left, factor[:, 2 * m : 2 * m + 1], factor[:, 2 * m + 1 : 2 * m + 2])
            value = value + spread * part[:, m * STAT : (m + 1) * STAT]
        spread = jnp.where(left, inverse[:, 2 * m : 2 * m + 1], inverse[:, 2 * m + 1 : 2 * m + 2])
        columns.append(value * spread)

    def head(h, side):
        k, g = h // GROUP, h % GROUP
        rows = columns[k // 2][g * row_count : (g + 1) * row_count]
        return rows if k % 2 == side else pltpu.roll(rows, HD, 1)

    left = iota((row_count, STAT), 1) < HD
    attended = jnp.concatenate(
        [jnp.where(left, head(2 * n, 0), head(2 * n + 1, 1)) for n in range(HEADS // 2)], axis=1
    ).astype(BF16)
    share = in_chip_order(dot_nt(attended, near_w[...]), dot_nt(attended, far_w[...]))
    width = near_w.shape[0]
    member = lax.axis_index("seq")
    both = pl.ds(pl.multiple_of((member // 2) * (2 * width), STAT), 2 * width)
    resid = x_ref[:, both] + share
    resid_ref[...] = jnp.where(member % 2 == 0, resid[:, :width], resid[:, width:])
    stats = routing_ref[...]
    lane = iota(stats.shape, 1)
    for i, value in enumerate(split3(jnp.sum(resid * resid, axis=1, keepdims=True))):
        stats = jnp.where(lane == 4 * TOP + i, value, stats)
    out_ref[:, : 2 * width] = (resid * gain_ref[:, both]).astype(BF16)
    out_ref[:, 2 * width :] = stats.astype(BF16)


def across(column, eye):
    return jnp.sum(jnp.where(eye, column, 0.0), axis=0, keepdims=True)


def gate_kernel(groups, *refs):
    near_refs, far_refs, w_ref = refs[: groups // 2], refs[groups // 2 : groups], refs[groups]
    message_refs = refs[groups + 1 : 2 * groups + 1]
    placed_ref, scale_ref, full_ref = refs[2 * groups + 1 :]
    member, me = lax.axis_index("seq"), lax.axis_index("req")
    width = w_ref.shape[1]
    row_count = near_refs[0].shape[0]
    tokens = groups * row_count
    near = jnp.concatenate([ref[...].astype(F32) for ref in near_refs], axis=0)
    far = jnp.concatenate([ref[...].astype(F32) for ref in far_refs], axis=0)
    first = member % 2 == 0
    pieces = jnp.concatenate([jnp.where(first, far, near), jnp.where(first, near, far)], axis=0)
    mixed, routing = pieces[:, :width].astype(BF16), pieces[:, width:]
    power = routing[:, 4 * TOP : 4 * TOP + 1] + (
        routing[:, 4 * TOP + 1 : 4 * TOP + 2] + routing[:, 4 * TOP + 2 : 4 * TOP + 3]
    )
    chosen = routing[:, :TOP]
    gates = routing[:, TOP : 2 * TOP] + (
        routing[:, 2 * TOP : 3 * TOP] + routing[:, 3 * TOP : 4 * TOP]
    )
    experts = w_ref.shape[0]
    square = (tokens, tokens)
    eye = iota(square, 0) == iota(square, 1)
    earlier = (iota(square, 0) < iota(square, 1)) & (
        iota(square, 0) // row_count == iota(square, 1) // row_count
    )
    slots = groups * CAP
    shape = (slots, tokens)
    home = (iota(shape, 1) // row_count) ^ (member // 2)
    slot = iota(shape, 0)
    same_group = slot // CAP == home
    ordinal_of_slot = (slot % CAP).astype(F32)
    placed, scales, powers = [], [], []
    power_row = across(power, eye)
    for e in range(experts):
        match = chosen == (member * experts + e).astype(F32)
        routed = jnp.max(jnp.where(match, 1.0, 0.0), axis=1, keepdims=True)
        scale = jnp.sum(jnp.where(match, gates, 0.0), axis=1, keepdims=True)
        ordinal = across(routed, earlier)
        here = same_group & (across(routed, eye) > 0.5) & (ordinal_of_slot == ordinal)
        placed.append(jnp.where(here, 1.0, 0.0))
        scales.append(jnp.sum(jnp.where(here, across(scale, eye), 0.0), axis=1, keepdims=True))
        powers.append(jnp.sum(jnp.where(here, power_row, 0.0), axis=1, keepdims=True))
    lane = iota((slots, STAT), 1)
    all_placed = jnp.concatenate(placed, axis=0).astype(BF16)
    taken = jnp.dot(all_placed, mixed, preferred_element_type=F32).astype(BF16)
    for e in range(experts):
        rows = slice(e * slots, (e + 1) * slots)
        placed_ref[e] = all_placed[rows]
        scale_ref[e] = jnp.broadcast_to(scales[e], scale_ref.shape[1:])
        full_ref[e, :, : 2 * FFE] = jnp.dot(
            taken[rows], w_ref[e], preferred_element_type=F32
        ).astype(BF16)
        high, middle, low = split3(powers[e])
        full_ref[e, :, 2 * FFE :] = jnp.where(
            lane == 0, high, jnp.where(lane == 1, middle, jnp.where(lane == 2, low, 0.0))
        ).astype(BF16)
    for k in range(groups):
        message_refs[k][...] = full_ref[me ^ k]


def hidden_kernel(*refs):
    gate_up = refs[0][...].astype(F32)
    for ref in refs[1:-1]:
        gate_up = gate_up + ref[...].astype(F32)
    power = gate_up[:, 2 * FFE : 2 * FFE + 1] + (
        gate_up[:, 2 * FFE + 1 : 2 * FFE + 2] + gate_up[:, 2 * FFE + 2 : 2 * FFE + 3]
    )
    gate_up = gate_up[:, : 2 * FFE] * lax.rsqrt(power / D + EPS)
    gate, up = gate_up[:, :FFE], gate_up[:, FFE:]
    refs[-1][...] = (gate / (1.0 + jnp.exp(-gate)) * up).astype(BF16)


def down_kernel(groups, *refs):
    hidden_refs = refs[:groups]
    w_ref, placed_ref, scale_ref, send_ref, keep_ref = refs[groups:]
    me, core = lax.axis_index("req"), lax.axis_index("seq") % 2
    total = jnp.zeros((placed_ref.shape[2], w_ref.shape[2]), F32)
    for k, hidden_ref in enumerate(hidden_refs):
        expert = me ^ k
        produced = jnp.dot(hidden_ref[...], w_ref[expert], preferred_element_type=F32)
        total = total + lax.dot_general(
            placed_ref[expert],
            (produced * scale_ref[expert][:, :1]).astype(BF16),
            (((0,), (0,)), ((), ())),
            preferred_element_type=F32,
        )
    half = total.shape[0] // 2
    low, high = total[:half], total[half:]
    send_ref[...] = jnp.where(core == 0, high, low).astype(BF16)
    keep_ref[...] = jnp.where(core == 0, low, high)


def spread_kernel(keep_ref, arrived_ref, *out_refs):
    total = keep_ref[...] + arrived_ref[...].astype(F32)
    row_count = out_refs[0].shape[0]
    for k, out_ref in enumerate(out_refs):
        out_ref[...] = total[k * row_count : (k + 1) * row_count].astype(BF16)


def halve_kernel(resid_ref, *refs):
    arrived_refs, send_ref, keep_ref = refs[:-2], refs[-2], refs[-1]
    total = arrived_refs[0][...].astype(F32)
    for ref in arrived_refs[1:]:
        total = total + ref[...].astype(F32)
    width = total.shape[1] // 2
    left, right = total[:, :width], total[:, width:]
    first = lax.axis_index("seq") % 2 == 0
    send_ref[...] = jnp.where(first, right, left)
    keep_ref[...] = resid_ref[...] + jnp.where(first, left, right)


def final_kernel(keep_ref, arrived_ref, out_ref):
    total = keep_ref[...] + arrived_ref[...]
    for r in range(out_ref.shape[0]):
        out_ref[r] = total[r * NSTEP : (r + 1) * NSTEP].astype(BF16)


def staged(
    x_in,
    attn_gain,
    moe_gain,
    w_qkv,
    w_o,
    cache_k,
    cache_v,
    page_map,
    lengths,
    routes,
    route_weights,
    w_gate_up,
    w_down,
):
    requests = x_in.shape[0]
    row_count = requests * NSTEP
    members, groups = lax.axis_size("seq"), lax.axis_size("req")
    chips = members // 2
    heads = w_qkv.shape[1] // HD
    width = w_o.shape[1]

    heads_shape = jax.ShapeDtypeStruct((heads, row_count, 2 * HD), BF16)
    own_heads, x = kernel_call(
        project_kernel,
        [heads_shape, jax.ShapeDtypeStruct((row_count, D), F32)],
        [HBM] * 4,
        [
            pltpu.VMEM(x_in.shape, BF16),
            pltpu.VMEM((D,), F32),
            pltpu.VMEM((w_qkv.shape[1], D), BF16),
            pltpu.SMEM(lengths.shape, jnp.int32),
            pltpu.SemaphoreType.DMA((4,)),
        ],
        vmem_mib=60,
        cost=5.0,
    )(x_in, attn_gain, w_qkv.T, lengths)

    def gathered(own):
        return [own] + [swap(own, "seq", 2 * k) for k in range(1, chips)]

    near = gathered(own_heads)
    first = near[1]
    near[0], live, routing, gain = kernel_call(
        prepare_kernel,
        [
            heads_shape,
            jax.ShapeDtypeStruct((requests, cache_k.shape[1]), F32),
            jax.ShapeDtypeStruct((row_count, STAT), F32),
            jax.ShapeDtypeStruct((1, D), F32),
        ],
        [VMEM] + [SMEM] * 2 + [VMEM] * 3,
    )(after(own_heads, near[1]), page_map, lengths, routes, route_weights, moe_gain)
    near[1] = after(near[1], live)
    far = [swap(piece, "seq", 1) for piece in [after(own_heads, first)] + near[1:]]
    part_shape = jax.ShapeDtypeStruct((GROUP * row_count, WIDE), BF16)
    head_scratch = [
        pltpu.VMEM((2, chips, heads, row_count, 2 * HD), BF16),
        pltpu.VMEM((GROUP, row_count, KVD), F32),
        pltpu.VMEM((GROUP * row_count, WIDE), F32),
    ]
    part = kernel_call(
        lambda *refs: attend_kernel(chips, *refs),
        part_shape,
        [VMEM] * (2 * chips + 3),
        head_scratch,
    )(*near, *far, live, cache_k, cache_v)
    fresh = kernel_call(
        lambda *refs: fresh_kernel(chips, *refs),
        part_shape,
        [VMEM] * (2 * chips),
        head_scratch,
    )(*near, *far)
    near = gathered(part)
    near[1] = after(near[1], fresh)
    far = [swap(piece, "seq", 1) for piece in [part] + near[1:]]
    packed, resid = kernel_call(
        lambda *refs: merge_kernel(members + 1, *refs),
        [
            jax.ShapeDtypeStruct((row_count, 2 * width + STAT), BF16),
            jax.ShapeDtypeStruct((row_count, width), F32),
        ],
        [VMEM] * (members + 6),
    )(*near, *far, fresh, x, gain, routing, w_o.T, swap(w_o.T, "seq", 1))

    everyone = [(p, c, q) for p in range(chips) for c in range(2) for q in range(groups)]

    def crossing(j):
        return [
            ((2 * p + c) * groups + q, (2 * (q ^ (2 * c + j)) + 1 - c) * groups + p)
            for p, c, q in everyone
        ]

    def returning(j):
        return [
            ((2 * p + c) * groups + q, (2 * q + 1 - c) * groups + (p ^ (2 * c + j)))
            for p, c, q in everyone
        ]

    place = ("seq", "req")
    near = [lax.ppermute(packed, place, crossing(j)) for j in range(groups // 2)]
    far = [swap(piece, "seq", 1) for piece in near]
    experts = w_gate_up.shape[0]
    slots = groups * CAP
    *messages, placed, scale = kernel_call(
        lambda *refs: gate_kernel(groups, *refs),
        [jax.ShapeDtypeStruct((slots, 2 * FFE + STAT), BF16)] * groups
        + [
            jax.ShapeDtypeStruct((experts, slots, groups * row_count), BF16),
            jax.ShapeDtypeStruct((experts, slots, STAT), F32),
        ],
        [VMEM] * (groups + 1),
        [pltpu.VMEM((experts, slots, 2 * FFE + STAT), BF16)],
    )(*near, *far, w_gate_up)
    sums = [messages[0]] + [swap(messages[k], "req", k) for k in (3, 1, 2)]
    hidden = kernel_call(
        hidden_kernel, jax.ShapeDtypeStruct((slots, FFE), BF16), [VMEM] * groups
    )(*sums)
    hiddens = [hidden] + [swap(hidden, "req", k) for k in range(1, groups)]
    half = (groups * row_count // 2, 2 * width)
    send, keep = kernel_call(
        lambda *refs: down_kernel(groups, *refs),
        [jax.ShapeDtypeStruct(half, BF16), jax.ShapeDtypeStruct(half, F32)],
        [VMEM] * (groups + 3),
    )(*hiddens, w_down, placed, scale)
    outs = kernel_call(
        spread_kernel,
        [jax.ShapeDtypeStruct((row_count, 2 * width), BF16)] * (groups // 2),
        [VMEM] * 2,
    )(keep, swap(send, "seq", 1))
    arrived = [lax.ppermute(out, place, returning(j)) for j, out in enumerate(outs)]
    send, keep = kernel_call(
        halve_kernel,
        [jax.ShapeDtypeStruct((row_count, width), F32)] * 2,
        [VMEM] * (1 + groups // 2),
    )(resid, *arrived)
    return kernel_call(
        final_kernel, jax.ShapeDtypeStruct((requests, NSTEP, width), BF16), [VMEM] * 2
    )(keep, swap(send, "seq", 1))


def local(*args):
    w_qkv, w_o, w_gate_up = args[3], args[4], args[11]
    members, groups = lax.axis_size("seq"), lax.axis_size("req")
    fits = (
        members == 8
        and groups == 4
        and w_qkv.shape[1] % HD == 0
        and w_gate_up.shape[0] == groups
        and (2 * w_o.shape[1]) % STAT == 0
    )
    return staged(*args) if fits else plain(*args)


def solution(mesh):
    in_specs = (
        P("req", None, None),
        P(),
        P(),
        P(None, "seq"),
        P(None, "seq"),
        P("req", "seq", None),
        P("req", "seq", None),
        P("req", "seq"),
        P("req"),
        P("req", None, None),
        P("req", None, None),
        P("seq", "req", None),
        P("seq", None, "req"),
    )
    out_specs = P("req", None, "seq")
    return jax.shard_map(local, mesh=mesh, in_specs=in_specs, out_specs=out_specs, check_vma=False)
```

```python
import math

import jax
import jax.numpy as jnp
from jax import lax
from jax.experimental import pallas as pl
from jax.experimental.pallas import tpu as pltpu
from jax.sharding import PartitionSpec as P

D = 1536
HEADS = 24
KVH = 8
HD = 64
FFE = 512
TOP = 8
NSTEP = 4
PAGE = 16
ATT = 1536
KVD = 512
GROUP = 3
CAP = 12
MASKS = ((3, 2), (1, 0))


EPS = 1e-05
NEG = -1e30


def combined_all(value, axis, join):
    pieces = jax.tree.map(lambda part: lax.all_gather(part, axis), value)
    head = jax.tree.map(lambda part: part[0], pieces)
    tail = jax.tree.map(lambda part: part[1:], pieces)
    so_far, _ = lax.scan(lambda so_far, piece: (join(so_far, piece), None), head, tail)
    return so_far


def normalize(values, gain):
    power = jnp.mean(values * values, axis=-1, keepdims=True)
    return values * lax.rsqrt(power + EPS) * gain


def rotate(values, position):
    half = values.shape[-1] // 2
    rates = jnp.exp(
        jnp.arange(half, dtype=jnp.float32) * (-2.0 * math.log(10000.0) / values.shape[-1])
    )
    angle = position[..., None, None] * rates
    cosine = jnp.cos(angle)
    sine = jnp.sin(angle)
    first_half = values[..., :half]
    second_half = values[..., half:]
    return jnp.concatenate(
        [first_half * cosine - second_half * sine, second_half * cosine + first_half * sine],
        axis=-1,
    )


def softmax_join(left, right):
    left_top, left_total, left_sums = left
    right_top, right_total, right_sums = right
    highest = jnp.maximum(left_top, right_top)
    left_factor = jnp.exp(left_top - highest)
    right_factor = jnp.exp(right_top - highest)
    row_count, head_count = highest.shape
    left_part = left_sums.reshape(row_count, head_count, -1) * left_factor[:, :, None]
    right_part = right_sums.reshape(row_count, head_count, -1) * right_factor[:, :, None]
    joined = (left_part + right_part).reshape(row_count, -1)
    return (highest, left_total * left_factor + right_total * right_factor, joined)


def project_with(left, piece):
    return jnp.dot(left, piece, preferred_element_type=jnp.float32)


def plain(
    x_in,
    attn_gain,
    moe_gain,
    w_qkv,
    w_o,
    cache_k,
    cache_v,
    page_map,
    lengths,
    routes,
    route_weights,
    w_gate_up,
    w_down,
):
    local_requests = x_in.shape[0]
    row_count = local_requests * NSTEP
    inputs = x_in.astype(jnp.float32).reshape(row_count, D)
    normed = normalize(inputs, attn_gain).astype(jnp.bfloat16)
    projected = project_with(normed, lax.all_gather(w_qkv, "seq", axis=1, tiled=True))
    queries = projected[:, :ATT].reshape(local_requests, NSTEP, HEADS, HD)
    keys_new = projected[:, ATT : ATT + KVD].reshape(local_requests, NSTEP, KVH, HD)
    values_new = (
        projected[:, ATT + KVD :].reshape(local_requests, NSTEP, KVH, HD).astype(jnp.bfloat16)
    )
    position = (lengths[:, None] + jnp.arange(NSTEP, dtype=jnp.int32)[None, :]).astype(jnp.float32)
    queries = (
        rotate(queries, position)
        .astype(jnp.bfloat16)
        .reshape(local_requests, NSTEP, KVH, GROUP, HD)
    )
    keys_new = rotate(keys_new, position).astype(jnp.bfloat16)
    scale = HD ** (-0.5)
    slot_count = cache_k.shape[1]
    cached_keys = cache_k.reshape(local_requests, slot_count, KVH, HD)
    cached_values = cache_v.reshape(local_requests, slot_count, KVH, HD)
    slot_position = (
        page_map[:, :, None] * PAGE + jnp.arange(PAGE, dtype=jnp.int32)[None, None, :]
    ).reshape(local_requests, slot_count)
    live = (slot_position < lengths[:, None])[:, None, None, None, :]
    scores = (
        jnp.einsum("rskgd,rtkd->rskgt", queries, cached_keys, preferred_element_type=jnp.float32)
        * scale
    )
    scores = jnp.where(live, scores, NEG)
    local_top = jnp.max(scores, axis=-1)
    exp_scores = jnp.where(live, jnp.exp(scores - local_top[..., None]), 0.0)
    local_total = jnp.sum(exp_scores, axis=-1).reshape(row_count, HEADS)
    local_sums = jnp.einsum(
        "rskgt,rtkd->rskgd",
        exp_scores.astype(jnp.bfloat16),
        cached_values,
        preferred_element_type=jnp.float32,
    ).reshape(row_count, ATT)
    local_top = local_top.reshape(row_count, HEADS)
    cache_top, cache_total, cache_sums = combined_all(
        (local_top, local_total, local_sums), "seq", softmax_join
    )
    causal = (
        jnp.arange(NSTEP, dtype=jnp.int32)[:, None] >= jnp.arange(NSTEP, dtype=jnp.int32)[None, :]
    )[None, :, None, None, :]
    fresh = (
        jnp.einsum("rskgd,rukd->rskgu", queries, keys_new, preferred_element_type=jnp.float32)
        * scale
    )
    fresh = jnp.where(causal, fresh, NEG).reshape(row_count, HEADS, NSTEP)
    highest = jnp.maximum(cache_top, jnp.max(fresh, axis=-1))
    fresh_exp = jnp.exp(fresh - highest[:, :, None])
    carried = jnp.exp(cache_top - highest)
    denominator = cache_total * carried + jnp.sum(fresh_exp, axis=-1)
    fresh_probs = fresh_exp.reshape(local_requests, NSTEP, KVH, GROUP, NSTEP).astype(jnp.bfloat16)
    fresh_sums = jnp.einsum(
        "rskgu,rukd->rskgd", fresh_probs, values_new, preferred_element_type=jnp.float32
    ).reshape(row_count, HEADS, HD)
    numerator = cache_sums.reshape(row_count, HEADS, HD) * carried[:, :, None] + fresh_sums
    attended = (numerator / denominator[:, :, None]).reshape(row_count, ATT).astype(jnp.bfloat16)
    attn_mixed = project_with(attended, lax.all_gather(w_o, "seq", axis=1, tiled=True))
    resid = inputs + attn_mixed
    mixed_in = normalize(resid, moe_gain).astype(jnp.bfloat16)
    local_experts = w_gate_up.shape[0]
    groups = lax.axis_size("req")
    owned = lax.axis_index("seq") * local_experts + jnp.arange(local_experts, dtype=jnp.int32)
    chosen = routes.reshape(row_count, TOP)
    gates = route_weights.reshape(row_count, TOP)
    matches = chosen[None, :, :] == owned[:, None, None]
    routed = jnp.any(matches, axis=-1)
    route_scale = jnp.sum(jnp.where(matches, gates[None, :, :], 0.0), axis=-1)
    ordinal = jnp.cumsum(routed.astype(jnp.int32), axis=1) - 1
    placed = routed[:, :, None] & (
        ordinal[:, :, None] == jnp.arange(CAP, dtype=jnp.int32)[None, None, :]
    )
    outgoing = jnp.einsum(
        "erc,rd->ecd", placed.astype(jnp.bfloat16), mixed_in, preferred_element_type=jnp.float32
    ).astype(jnp.bfloat16)
    arrived = lax.all_to_all(outgoing[:, None], "req", split_axis=3, concat_axis=1, tiled=True)
    slice_width = arrived.shape[3]
    arrived = arrived.reshape(local_experts, groups * CAP, slice_width)
    partial_values = jnp.einsum(
        "end,edf->enf", arrived, w_gate_up, preferred_element_type=jnp.float32
    )
    gate_up = lax.psum(partial_values, "req")
    hidden = (jax.nn.silu(gate_up[..., :FFE]) * gate_up[..., FFE:]).astype(jnp.bfloat16)
    produced = jnp.einsum("enf,efd->end", hidden, w_down, preferred_element_type=jnp.float32)
    returned = lax.all_to_all(
        produced.reshape(local_experts, groups, CAP, slice_width),
        "req",
        split_axis=1,
        concat_axis=3,
        tiled=True,
    )[:, 0]
    weighted = placed.astype(jnp.float32) * route_scale[:, :, None]
    expert_total = jnp.einsum("erc,ecd->rd", weighted, returned, precision=lax.Precision.HIGHEST)
    own_share = lax.psum_scatter(expert_total, "seq", scatter_dimension=1, tiled=True)
    share_width = own_share.shape[1]
    resid_share = lax.dynamic_slice_in_dim(
        resid, lax.axis_index("seq") * share_width, share_width, 1
    )
    return (
        (resid_share + own_share).astype(jnp.bfloat16).reshape(local_requests, NSTEP, share_width)
    )


F32 = jnp.float32
BF16 = jnp.bfloat16
STAT = 128
WIDE = KVD + STAT
VMEM = pl.BlockSpec(memory_space=pltpu.VMEM)
SMEM = pl.BlockSpec(memory_space=pltpu.SMEM)
HBM = pl.BlockSpec(memory_space=pltpu.HBM)


def kernel_call(body, out_shape, in_specs, scratch=(), out_specs=None, vmem_mib=8, cost=0.5):
    return pl.pallas_call(
        body,
        out_shape=out_shape,
        in_specs=in_specs,
        out_specs=out_specs or ([VMEM] * len(out_shape) if isinstance(out_shape, list) else VMEM),
        scratch_shapes=list(scratch),
        compiler_params=pltpu.CompilerParams(vmem_limit_bytes=vmem_mib * 2**20),
        cost_estimate=pl.CostEstimate(
            flops=int(cost * 1e9), bytes_accessed=int(cost * 3e6), transcendentals=0
        ),
    )


def iota(shape, dim):
    return lax.broadcasted_iota(jnp.int32, shape, dim)


def split3(value):
    high = value.astype(BF16).astype(F32)
    rest = value - high
    middle = rest.astype(BF16).astype(F32)
    return high, middle, rest - middle


def rows_of(ref):
    return jnp.concatenate([ref[r].astype(F32) for r in range(ref.shape[0])], axis=0)


def dot_nt(left, right):
    return lax.dot_general(left, right, (((1,), (1,)), ((), ())), preferred_element_type=F32)


def swap(value, axis, mask):
    pairs = [(i, i ^ mask) for i in range(lax.axis_size(axis))]
    return lax.ppermute(value, axis, pairs)


def after(value, *others):
    return lax.optimization_barrier((value, *others))[0]


def project_kernel(*refs):
    x_hbm, attn_hbm, w_hbm, lengths_hbm, heads_ref, x_ref = refs[:6]
    x_in, attn_gain, w_in, lengths, sem = refs[6:]
    loads = [
        pltpu.make_async_copy(source, target, sem.at[i])
        for i, (source, target) in enumerate(
            [(lengths_hbm, lengths), (x_hbm, x_in), (attn_hbm, attn_gain), (w_hbm, w_in)]
        )
    ]
    for load in loads:
        load.start()
    requests = x_in.shape[0]
    row_count = requests * NSTEP
    shape = (row_count, STAT)
    loads[0].wait()
    row, lane = iota(shape, 0), iota(shape, 1)
    position = row % NSTEP
    for r in range(requests):
        position = position + jnp.where(row // NSTEP == r, lengths[r], 0)
    rates = jnp.exp((lane % (HD // 2)).astype(F32) * (-2.0 * math.log(10000.0) / HD))
    angle = position.astype(F32) * rates
    cosine = jnp.cos(angle)
    sine = jnp.where(lane % HD < HD // 2, -jnp.sin(angle), jnp.sin(angle))
    loads[1].wait()
    x = rows_of(x_in)
    width = x_ref.shape[1]
    own = pl.ds(pl.multiple_of((lax.axis_index("seq") // 2) * width, STAT), width)
    x_ref[...] = jnp.concatenate([x_in[r, :, own].astype(F32) for r in range(requests)], axis=0)
    power = jnp.mean(x * x, axis=-1, keepdims=True)
    loads[2].wait()
    normed = (x * lax.rsqrt(power + EPS) * attn_gain[...].reshape(1, D)).astype(BF16)
    loads[3].wait()
    projected = dot_nt(normed, w_in[...])
    heads = w_in.shape[0] // HD
    first = lax.axis_index("seq") * heads
    for i in range(heads):
        one = projected[:, i * HD : (i + 1) * HD]
        both = jnp.concatenate([one, one], axis=1)
        turned = both * cosine + pltpu.roll(both, HD // 2, 1) * sine
        heads_ref[i] = jnp.where(first + i < HEADS + KVH, turned, both).astype(BF16)


def prepare_kernel(heads_in, pages, lengths, routes, weights, moe_gain, *out_refs):
    heads_ref, live_ref, routing_ref, gain_ref = out_refs
    heads_ref[...] = heads_in[...]
    slots = live_ref.shape[1]
    slot = iota((1, slots), 1)
    for r in range(live_ref.shape[0]):
        page = jnp.zeros((1, slots), jnp.int32)
        for j in range(slots // PAGE):
            page = jnp.where(slot // PAGE == j, pages[r, j], page)
        live = page * PAGE + slot % PAGE < lengths[r]
        live_ref[r : r + 1, :] = jnp.where(live, 1.0, 0.0)
    row_count = routing_ref.shape[0]
    high, middle, low = split3(rows_of(weights))
    routing_ref[...] = jnp.concatenate(
        [rows_of(routes), high, middle, low, jnp.zeros((row_count, STAT - 4 * TOP), F32)], axis=1
    )
    gain_ref[...] = moe_gain[...].reshape(1, D)


def in_chip_order(near, far):
    first = lax.axis_index("seq") % 2 == 0
    return jnp.where(
        first, jnp.concatenate([near, far], axis=1), jnp.concatenate([far, near], axis=1)
    )


def gather_pieces(near_refs, far_refs, all_ref):
    core = lax.axis_index("seq") % 2
    for k in range(len(near_refs)):
        all_ref[core, k] = near_refs[k][...]
        all_ref[1 - core, k] = far_refs[k][...]


def paired(head, left, right):
    a = head(left)
    return jnp.where(iota(a.shape, 1) < HD, a, head(right))


def expanded(q_ref, r):
    rows = [q_ref[g, r * NSTEP : (r + 1) * NSTEP, :] for g in range(GROUP)]
    base = jnp.concatenate(rows + [jnp.zeros((NSTEP, KVD), F32)], axis=0)
    owner = iota(base.shape, 1) // HD
    return jnp.concatenate(
        [jnp.where(owner == k, base, 0.0) for k in range(KVH)], axis=0
    ).astype(BF16)


def attend_part(query, keys, values, live):
    scores = jnp.where(live, dot_nt(query, keys) * (HD ** (-0.5)), NEG)
    top = jnp.max(scores, axis=1, keepdims=True)
    exp_scores = jnp.where(live, jnp.exp(scores - top), 0.0)
    total = jnp.sum(exp_scores, axis=1, keepdims=True)
    return top, total, jnp.dot(exp_scores.astype(BF16), values, preferred_element_type=F32)


def place_rows(part_ref, r, row_count, top, total, sums):
    block = (GROUP + 1) * NSTEP
    owner = iota((block, KVD), 1) // HD
    lane = iota((block, STAT), 1)
    own_sums = jnp.zeros((block, KVD), F32)
    stats = jnp.zeros((block, STAT), F32)
    for k in range(KVH):
        rows = slice(k * block, (k + 1) * block)
        own_sums = jnp.where(owner == k, sums[rows], own_sums)
        value = jnp.where(lane < 3 * KVH, top[rows], total[rows])
        stats = jnp.where(lane % KVH == k, value, stats)
    high, middle, low = split3(stats)
    part = (lane // KVH) % 3
    stats = jnp.where(part == 0, high, jnp.where(part == 1, middle, low))
    for g in range(GROUP):
        rows = slice(g * row_count + r * NSTEP, g * row_count + (r + 1) * NSTEP)
        part_ref[rows, :KVD] = own_sums[g * NSTEP : (g + 1) * NSTEP]
        part_ref[rows, KVD:] = stats[g * NSTEP : (g + 1) * NSTEP]


def head_of(all_ref):
    chip = lax.axis_index("seq") // 2
    heads = all_ref.shape[2]

    def head(h):
        owner = h // heads
        return all_ref[owner % 2, chip ^ (owner // 2), h % heads].astype(F32)

    return head


def query_rows(head, q_ref):
    for g in range(GROUP):
        for m in range(KVH // 2):
            q_ref[g, :, m * STAT : (m + 1) * STAT] = paired(
                head, GROUP * 2 * m + g, GROUP * (2 * m + 1) + g
            )


def attend_kernel(chips, *refs):
    near_refs, far_refs = refs[:chips], refs[chips : 2 * chips]
    live_ref, k_ref, v_ref, out_ref, all_ref, q_ref, part_ref = refs[2 * chips :]
    requests = k_ref.shape[0]
    gather_pieces(near_refs, far_refs, all_ref)
    query_rows(head_of(all_ref), q_ref)
    for r in range(requests):
        live = live_ref[r : r + 1, :] > 0.5
        place_rows(
            part_ref,
            r,
            requests * NSTEP,
            *attend_part(expanded(q_ref, r), k_ref[r], v_ref[r], live),
        )
    out_ref[...] = part_ref[...].astype(BF16)


def fresh_kernel(chips, *refs):
    near_refs, far_refs = refs[:chips], refs[chips : 2 * chips]
    out_ref, all_ref, q_ref, part_ref = refs[2 * chips :]
    gather_pieces(near_refs, far_refs, all_ref)
    head = head_of(all_ref)
    query_rows(head, q_ref)
    row_count = q_ref.shape[1]
    pad = jnp.zeros((STAT - row_count, KVD), F32)

    def new_rows(first):
        pieces = [paired(head, first + 2 * m, first + 2 * m + 1) for m in range(KVH // 2)]
        return jnp.concatenate([jnp.concatenate(pieces, axis=1), pad], axis=0).astype(BF16)

    keys, values = new_rows(HEADS), new_rows(HEADS + KVH)
    shape = ((GROUP + 1) * NSTEP * KVH, STAT)
    slot, step = iota(shape, 1), iota(shape, 0) % NSTEP
    for r in range(row_count // NSTEP):
        live = (slot // NSTEP == r) & (slot % NSTEP <= step)
        place_rows(
            part_ref, r, row_count, *attend_part(expanded(q_ref, r), keys, values, live)
        )
    out_ref[...] = part_ref[...].astype(BF16)


def merge_kernel(count, *refs):
    part_refs = refs[:count]
    x_ref, gain_ref, routing_ref, near_w, far_w, out_ref, resid_ref = refs[count:]
    parts = [ref[...].astype(F32) for ref in part_refs]
    tops, totals = [], []
    for part in parts:
        stats = part[:, KVD:]
        full = stats + (
            pltpu.roll(stats, STAT - KVH, 1) + pltpu.roll(stats, STAT - 2 * KVH, 1)
        )
        tops.append(full)
        totals.append(pltpu.roll(full, STAT - 3 * KVH, 1))
    highest = tops[0]
    for top in tops[1:]:
        highest = jnp.maximum(highest, top)
    factors = [jnp.exp(top - highest) for top in tops]
    denominator = factors[0] * totals[0]
    for factor, total in zip(factors[1:], totals[1:]):
        denominator = denominator + factor * total
    inverse = 1.0 / denominator
    row_total = parts[0].shape[0]
    row_count = row_total // GROUP
    owner = iota((STAT, KVD), 1) // HD == iota((STAT, KVD), 0)
    spread = jnp.where(owner, 1.0, 0.0).astype(BF16)
    valid = iota((row_total, STAT), 1) < KVH
    merged = jnp.zeros((row_total, KVD), F32)
    for part, factor in zip(parts, factors):
        weight = jnp.where(valid, factor * inverse, 0.0).astype(BF16)
        merged = merged + jnp.dot(weight, spread, preferred_element_type=F32) * part[:, :KVD]
    columns = [merged[:, m * STAT : (m + 1) * STAT] for m in range(KVH // 2)]

    def head(h, side):
        k, g = h // GROUP, h % GROUP
        rows = columns[k // 2][g * row_count : (g + 1) * row_count]
        return rows if k % 2 == side else pltpu.roll(rows, HD, 1)

    left = iota((row_count, STAT), 1) < HD
    attended = jnp.concatenate(
        [jnp.where(left, head(2 * n, 0), head(2 * n + 1, 1)) for n in range(HEADS // 2)], axis=1
    ).astype(BF16)
    share = in_chip_order(dot_nt(attended, near_w[...]), dot_nt(attended, far_w[...]))
    width = near_w.shape[0]
    member = lax.axis_index("seq")
    both = pl.ds(pl.multiple_of((member // 2) * (2 * width), STAT), 2 * width)
    resid = x_ref[...] + share
    resid_ref[...] = jnp.where(member % 2 == 0, resid[:, :width], resid[:, width:])
    stats = routing_ref[...]
    lane = iota(stats.shape, 1)
    for i, value in enumerate(split3(jnp.sum(resid * resid, axis=1, keepdims=True))):
        stats = jnp.where(lane == 4 * TOP + i, value, stats)
    out_ref[:, : 2 * width] = (resid * gain_ref[:, both]).astype(BF16)
    out_ref[:, 2 * width :] = stats.astype(BF16)


def across(column, eye):
    return jnp.sum(jnp.where(eye, column, 0.0), axis=0, keepdims=True)


def gate_kernel(groups, *refs):
    near_refs, far_refs, w_ref = refs[: groups // 2], refs[groups // 2 : groups], refs[groups]
    message_refs = refs[groups + 1 : 2 * groups + 1]
    placed_ref, scale_ref, full_ref = refs[2 * groups + 1 :]
    member, me = lax.axis_index("seq"), lax.axis_index("req")
    width = w_ref.shape[1]
    row_count = near_refs[0].shape[0]
    tokens = groups * row_count
    near = jnp.concatenate([ref[...].astype(F32) for ref in near_refs], axis=0)
    far = jnp.concatenate([ref[...].astype(F32) for ref in far_refs], axis=0)
    first = member % 2 == 0
    pieces = jnp.concatenate([jnp.where(first, far, near), jnp.where(first, near, far)], axis=0)
    mixed, routing = pieces[:, :width].astype(BF16), pieces[:, width:]
    power = routing[:, 4 * TOP : 4 * TOP + 1] + (
        routing[:, 4 * TOP + 1 : 4 * TOP + 2] + routing[:, 4 * TOP + 2 : 4 * TOP + 3]
    )
    chosen = routing[:, :TOP]
    gates = routing[:, TOP : 2 * TOP] + (
        routing[:, 2 * TOP : 3 * TOP] + routing[:, 3 * TOP : 4 * TOP]
    )
    experts = w_ref.shape[0]
    square = (tokens, tokens)
    eye = iota(square, 0) == iota(square, 1)
    earlier = (iota(square, 0) < iota(square, 1)) & (
        iota(square, 0) // row_count == iota(square, 1) // row_count
    )
    slots = groups * CAP
    shape = (slots, tokens)
    block = iota(shape, 1) // row_count
    home = jnp.zeros(shape, jnp.int32)
    for b, mask in enumerate((3, 2, 1, 0)):
        home = jnp.where(block == b, mask ^ (member // 2), home)
    slot = iota(shape, 0)
    same_group = slot // CAP == home
    ordinal_of_slot = (slot % CAP).astype(F32)
    placed, scales = [], []
    row = iota((16, tokens), 0)
    power_rows = jnp.zeros((16, tokens), F32)
    for i, part in enumerate(split3(across(power, eye))):
        power_rows = jnp.where(row == i, part, power_rows)
    power_rows = power_rows.astype(BF16)
    for e in range(experts):
        match = chosen == (member * experts + e).astype(F32)
        routed = jnp.max(jnp.where(match, 1.0, 0.0), axis=1, keepdims=True)
        scale = jnp.sum(jnp.where(match, gates, 0.0), axis=1, keepdims=True)
        ordinal = across(routed, earlier)
        here = same_group & (across(routed, eye) > 0.5) & (ordinal_of_slot == ordinal)
        placed.append(jnp.where(here, 1.0, 0.0))
        scales.append(jnp.sum(jnp.where(here, across(scale, eye), 0.0), axis=1, keepdims=True))
    all_placed = jnp.concatenate(placed, axis=0).astype(BF16)
    taken = jnp.dot(all_placed, mixed, preferred_element_type=F32).astype(BF16)
    for e in range(experts):
        rows = slice(e * slots, (e + 1) * slots)
        placed_ref[e] = all_placed[rows]
        scale_ref[e] = jnp.broadcast_to(scales[e], scale_ref.shape[1:])
        gate_up = jnp.dot(taken[rows], w_ref[e], preferred_element_type=F32).astype(BF16)
        for j in range(2 * FFE // STAT):
            full_ref[e, j * slots : (j + 1) * slots, :] = gate_up[:, j * STAT : (j + 1) * STAT]
        slot_power = dot_nt(power_rows, placed_ref[e])
        full_ref[e, 2 * FFE // STAT * slots :, :] = jnp.concatenate(
            [slot_power, jnp.zeros((16, STAT - slots), F32)], axis=1
        ).astype(BF16)
    for k in range(groups):
        message_refs[k][...] = full_ref[me ^ k]


def hidden_kernel(*refs):
    out_ref = refs[-1]
    gate_up = refs[0][...].astype(F32)
    for ref in refs[1:-1]:
        gate_up = gate_up + ref[...].astype(F32)
    slots = out_ref.shape[0]
    chunks = FFE // STAT
    stats = gate_up[2 * chunks * slots :, :slots]
    power = stats[0:1] + (stats[1:2] + stats[2:3])
    eye = iota((slots, slots), 0) == iota((slots, slots), 1)
    power = jnp.sum(jnp.where(eye, power, 0.0), axis=1, keepdims=True)
    scale = lax.rsqrt(power / D + EPS)
    for j in range(chunks):
        gate = gate_up[j * slots : (j + 1) * slots] * scale
        up = gate_up[(chunks + j) * slots : (chunks + j + 1) * slots] * scale
        out_ref[:, j * STAT : (j + 1) * STAT] = (gate / (1.0 + jnp.exp(-gate)) * up).astype(BF16)


def down_kernel(groups, *refs):
    hidden_refs = refs[:groups]
    w_ref, placed_ref, scale_ref, send_ref, keep_ref = refs[groups:]
    me, core = lax.axis_index("req"), lax.axis_index("seq") % 2
    total = jnp.zeros((placed_ref.shape[2], w_ref.shape[2]), F32)
    for k, hidden_ref in enumerate(hidden_refs):
        expert = me ^ k
        produced = jnp.dot(hidden_ref[...], w_ref[expert], preferred_element_type=F32)
        total = total + lax.dot_general(
            placed_ref[expert],
            (produced * scale_ref[expert][:, :1]).astype(BF16),
            (((0,), (0,)), ((), ())),
            preferred_element_type=F32,
        )
    half = total.shape[0] // 2
    low, high = total[:half], total[half:]
    send_ref[...] = jnp.where(core == 0, high, low).astype(BF16)
    keep_ref[...] = jnp.where(core == 0, low, high)


def spread_kernel(keep_ref, arrived_ref, *out_refs):
    total = keep_ref[...] + arrived_ref[...].astype(F32)
    row_count = out_refs[0].shape[0]
    for k, out_ref in enumerate(out_refs):
        out_ref[...] = total[k * row_count : (k + 1) * row_count].astype(BF16)


def halve_kernel(resid_ref, *refs):
    arrived_refs, send_ref, keep_ref = refs[:-2], refs[-2], refs[-1]
    total = arrived_refs[0][...].astype(F32)
    for ref in arrived_refs[1:]:
        total = total + ref[...].astype(F32)
    width = total.shape[1] // 2
    left, right = total[:, :width], total[:, width:]
    first = lax.axis_index("seq") % 2 == 0
    send_ref[...] = jnp.where(first, right, left)
    keep_ref[...] = resid_ref[...] + jnp.where(first, left, right)


def final_kernel(keep_ref, arrived_ref, out_ref):
    total = keep_ref[...] + arrived_ref[...]
    for r in range(out_ref.shape[0]):
        out_ref[r] = total[r * NSTEP : (r + 1) * NSTEP].astype(BF16)


def staged(
    x_in,
    attn_gain,
    moe_gain,
    w_qkv,
    w_o,
    cache_k,
    cache_v,
    page_map,
    lengths,
    routes,
    route_weights,
    w_gate_up,
    w_down,
):
    requests = x_in.shape[0]
    row_count = requests * NSTEP
    members, groups = lax.axis_size("seq"), lax.axis_size("req")
    chips = members // 2
    heads = w_qkv.shape[1] // HD
    width = w_o.shape[1]

    heads_shape = jax.ShapeDtypeStruct((heads, row_count, 2 * HD), BF16)
    own_heads, x = kernel_call(
        project_kernel,
        [heads_shape, jax.ShapeDtypeStruct((row_count, 2 * width), F32)],
        [HBM] * 4,
        [
            pltpu.VMEM(x_in.shape, BF16),
            pltpu.VMEM((D,), F32),
            pltpu.VMEM((w_qkv.shape[1], D), BF16),
            pltpu.SMEM(lengths.shape, jnp.int32),
            pltpu.SemaphoreType.DMA((4,)),
        ],
        vmem_mib=60,
        cost=5.0,
    )(x_in, attn_gain, w_qkv.T, lengths)

    def gathered(own):
        return [own] + [swap(own, "seq", 2 * k) for k in range(1, chips)]

    near = gathered(own_heads)
    first = near[1]
    near[0], live, routing, gain = kernel_call(
        prepare_kernel,
        [
            heads_shape,
            jax.ShapeDtypeStruct((requests, cache_k.shape[1]), F32),
            jax.ShapeDtypeStruct((row_count, STAT), F32),
            jax.ShapeDtypeStruct((1, D), F32),
        ],
        [VMEM] + [SMEM] * 2 + [VMEM] * 3,
    )(after(own_heads, near[1]), page_map, lengths, routes, route_weights, moe_gain)
    near[1] = after(near[1], live)
    far = [swap(piece, "seq", 1) for piece in [after(own_heads, first)] + near[1:]]
    part_shape = jax.ShapeDtypeStruct((GROUP * row_count, WIDE), BF16)
    head_scratch = [
        pltpu.VMEM((2, chips, heads, row_count, 2 * HD), BF16),
        pltpu.VMEM((GROUP, row_count, KVD), F32),
        pltpu.VMEM((GROUP * row_count, WIDE), F32),
    ]
    part = kernel_call(
        lambda *refs: attend_kernel(chips, *refs),
        part_shape,
        [VMEM] * (2 * chips + 3),
        head_scratch,
    )(*near, *far, live, cache_k, cache_v)
    fresh = kernel_call(
        lambda *refs: fresh_kernel(chips, *refs),
        part_shape,
        [VMEM] * (2 * chips),
        head_scratch,
    )(*near, *far)
    near = gathered(part)
    near[1] = after(near[1], fresh)
    far = [swap(piece, "seq", 1) for piece in [part] + near[1:]]
    packed, resid = kernel_call(
        lambda *refs: merge_kernel(members + 1, *refs),
        [
            jax.ShapeDtypeStruct((row_count, 2 * width + STAT), BF16),
            jax.ShapeDtypeStruct((row_count, width), F32),
        ],
        [VMEM] * (members + 6),
    )(*near, *far, fresh, x, gain, routing, w_o.T, swap(w_o.T, "seq", 1))

    everyone = [(p, c, q) for p in range(chips) for c in range(2) for q in range(groups)]

    def crossing(j):
        return [
            ((2 * p + c) * groups + q, (2 * (q ^ MASKS[c][j]) + 1 - c) * groups + p)
            for p, c, q in everyone
        ]

    def returning(j):
        return [
            ((2 * p + c) * groups + q, (2 * q + 1 - c) * groups + (p ^ MASKS[c][j]))
            for p, c, q in everyone
        ]

    place = ("seq", "req")
    near = [lax.ppermute(packed, place, crossing(j)) for j in range(groups // 2)]
    far = [swap(piece, "seq", 1) for piece in near]
    experts = w_gate_up.shape[0]
    slots = groups * CAP
    message = jax.ShapeDtypeStruct((2 * FFE // STAT * slots + 16, STAT), BF16)
    *messages, placed, scale = kernel_call(
        lambda *refs: gate_kernel(groups, *refs),
        [message] * groups
        + [
            jax.ShapeDtypeStruct((experts, slots, groups * row_count), BF16),
            jax.ShapeDtypeStruct((experts, slots, STAT), F32),
        ],
        [VMEM] * (groups + 1),
        [pltpu.VMEM((experts, *message.shape), BF16)],
    )(*near, *far, w_gate_up)
    sums = [messages[0]] + [swap(messages[k], "req", k) for k in (3, 1, 2)]
    hidden = kernel_call(
        hidden_kernel, jax.ShapeDtypeStruct((slots, FFE), BF16), [VMEM] * groups
    )(*sums)
    hiddens = [hidden] + [swap(hidden, "req", k) for k in range(1, groups)]
    half = (groups * row_count // 2, 2 * width)
    send, keep = kernel_call(
        lambda *refs: down_kernel(groups, *refs),
        [jax.ShapeDtypeStruct(half, BF16), jax.ShapeDtypeStruct(half, F32)],
        [VMEM] * (groups + 3),
    )(*hiddens, w_down, placed, scale)
    outs = kernel_call(
        spread_kernel,
        [jax.ShapeDtypeStruct((row_count, 2 * width), BF16)] * (groups // 2),
        [VMEM] * 2,
    )(keep, swap(send, "seq", 1))
    arrived = [lax.ppermute(out, place, returning(j)) for j, out in enumerate(outs)]
    send, keep = kernel_call(
        halve_kernel,
        [jax.ShapeDtypeStruct((row_count, width), F32)] * 2,
        [VMEM] * (1 + groups // 2),
    )(resid, *arrived)
    return kernel_call(
        final_kernel, jax.ShapeDtypeStruct((requests, NSTEP, width), BF16), [VMEM] * 2
    )(keep, swap(send, "seq", 1))


def local(*args):
    w_qkv, w_o, w_gate_up = args[3], args[4], args[11]
    members, groups = lax.axis_size("seq"), lax.axis_size("req")
    fits = (
        members == 8
        and groups == 4
        and w_qkv.shape[1] % HD == 0
        and w_gate_up.shape[0] == groups
        and (2 * w_o.shape[1]) % STAT == 0
    )
    return staged(*args) if fits else plain(*args)


def solution(mesh):
    in_specs = (
        P("req", None, None),
        P(),
        P(),
        P(None, "seq"),
        P(None, "seq"),
        P("req", "seq", None),
        P("req", "seq", None),
        P("req", "seq"),
        P("req"),
        P("req", None, None),
        P("req", None, None),
        P("seq", "req", None),
        P("seq", None, "req"),
    )
    out_specs = P("req", None, "seq")
    return jax.shard_map(local, mesh=mesh, in_specs=in_specs, out_specs=out_specs, check_vma=False)
```

```python
import math

import jax
import jax.numpy as jnp
from jax import lax
from jax.experimental import pallas as pl
from jax.experimental.pallas import tpu as pltpu
from jax.sharding import PartitionSpec as P

D = 1536
HEADS = 24
KVH = 8
HD = 64
FFE = 512
TOP = 8
NSTEP = 4
PAGE = 16
ATT = 1536
KVD = 512
GROUP = 3
CAP = 12
MASKS = ((3, 2), (1, 0))


EPS = 1e-05
NEG = -1e30


def combined_all(value, axis, join):
    pieces = jax.tree.map(lambda part: lax.all_gather(part, axis), value)
    head = jax.tree.map(lambda part: part[0], pieces)
    tail = jax.tree.map(lambda part: part[1:], pieces)
    so_far, _ = lax.scan(lambda so_far, piece: (join(so_far, piece), None), head, tail)
    return so_far


def normalize(values, gain):
    power = jnp.mean(values * values, axis=-1, keepdims=True)
    return values * lax.rsqrt(power + EPS) * gain


def rotate(values, position):
    half = values.shape[-1] // 2
    rates = jnp.exp(
        jnp.arange(half, dtype=jnp.float32) * (-2.0 * math.log(10000.0) / values.shape[-1])
    )
    angle = position[..., None, None] * rates
    cosine = jnp.cos(angle)
    sine = jnp.sin(angle)
    first_half = values[..., :half]
    second_half = values[..., half:]
    return jnp.concatenate(
        [first_half * cosine - second_half * sine, second_half * cosine + first_half * sine],
        axis=-1,
    )


def softmax_join(left, right):
    left_top, left_total, left_sums = left
    right_top, right_total, right_sums = right
    highest = jnp.maximum(left_top, right_top)
    left_factor = jnp.exp(left_top - highest)
    right_factor = jnp.exp(right_top - highest)
    row_count, head_count = highest.shape
    left_part = left_sums.reshape(row_count, head_count, -1) * left_factor[:, :, None]
    right_part = right_sums.reshape(row_count, head_count, -1) * right_factor[:, :, None]
    joined = (left_part + right_part).reshape(row_count, -1)
    return (highest, left_total * left_factor + right_total * right_factor, joined)


def project_with(left, piece):
    return jnp.dot(left, piece, preferred_element_type=jnp.float32)


def plain(
    x_in,
    attn_gain,
    moe_gain,
    w_qkv,
    w_o,
    cache_k,
    cache_v,
    page_map,
    lengths,
    routes,
    route_weights,
    w_gate_up,
    w_down,
):
    local_requests = x_in.shape[0]
    row_count = local_requests * NSTEP
    inputs = x_in.astype(jnp.float32).reshape(row_count, D)
    normed = normalize(inputs, attn_gain).astype(jnp.bfloat16)
    projected = project_with(normed, lax.all_gather(w_qkv, "seq", axis=1, tiled=True))
    queries = projected[:, :ATT].reshape(local_requests, NSTEP, HEADS, HD)
    keys_new = projected[:, ATT : ATT + KVD].reshape(local_requests, NSTEP, KVH, HD)
    values_new = (
        projected[:, ATT + KVD :].reshape(local_requests, NSTEP, KVH, HD).astype(jnp.bfloat16)
    )
    position = (lengths[:, None] + jnp.arange(NSTEP, dtype=jnp.int32)[None, :]).astype(jnp.float32)
    queries = (
        rotate(queries, position)
        .astype(jnp.bfloat16)
        .reshape(local_requests, NSTEP, KVH, GROUP, HD)
    )
    keys_new = rotate(keys_new, position).astype(jnp.bfloat16)
    scale = HD ** (-0.5)
    slot_count = cache_k.shape[1]
    cached_keys = cache_k.reshape(local_requests, slot_count, KVH, HD)
    cached_values = cache_v.reshape(local_requests, slot_count, KVH, HD)
    slot_position = (
        page_map[:, :, None] * PAGE + jnp.arange(PAGE, dtype=jnp.int32)[None, None, :]
    ).reshape(local_requests, slot_count)
    live = (slot_position < lengths[:, None])[:, None, None, None, :]
    scores = (
        jnp.einsum("rskgd,rtkd->rskgt", queries, cached_keys, preferred_element_type=jnp.float32)
        * scale
    )
    scores = jnp.where(live, scores, NEG)
    local_top = jnp.max(scores, axis=-1)
    exp_scores = jnp.where(live, jnp.exp(scores - local_top[..., None]), 0.0)
    local_total = jnp.sum(exp_scores, axis=-1).reshape(row_count, HEADS)
    local_sums = jnp.einsum(
        "rskgt,rtkd->rskgd",
        exp_scores.astype(jnp.bfloat16),
        cached_values,
        preferred_element_type=jnp.float32,
    ).reshape(row_count, ATT)
    local_top = local_top.reshape(row_count, HEADS)
    cache_top, cache_total, cache_sums = combined_all(
        (local_top, local_total, local_sums), "seq", softmax_join
    )
    causal = (
        jnp.arange(NSTEP, dtype=jnp.int32)[:, None] >= jnp.arange(NSTEP, dtype=jnp.int32)[None, :]
    )[None, :, None, None, :]
    fresh = (
        jnp.einsum("rskgd,rukd->rskgu", queries, keys_new, preferred_element_type=jnp.float32)
        * scale
    )
    fresh = jnp.where(causal, fresh, NEG).reshape(row_count, HEADS, NSTEP)
    highest = jnp.maximum(cache_top, jnp.max(fresh, axis=-1))
    fresh_exp = jnp.exp(fresh - highest[:, :, None])
    carried = jnp.exp(cache_top - highest)
    denominator = cache_total * carried + jnp.sum(fresh_exp, axis=-1)
    fresh_probs = fresh_exp.reshape(local_requests, NSTEP, KVH, GROUP, NSTEP).astype(jnp.bfloat16)
    fresh_sums = jnp.einsum(
        "rskgu,rukd->rskgd", fresh_probs, values_new, preferred_element_type=jnp.float32
    ).reshape(row_count, HEADS, HD)
    numerator = cache_sums.reshape(row_count, HEADS, HD) * carried[:, :, None] + fresh_sums
    attended = (numerator / denominator[:, :, None]).reshape(row_count, ATT).astype(jnp.bfloat16)
    attn_mixed = project_with(attended, lax.all_gather(w_o, "seq", axis=1, tiled=True))
    resid = inputs + attn_mixed
    mixed_in = normalize(resid, moe_gain).astype(jnp.bfloat16)
    local_experts = w_gate_up.shape[0]
    groups = lax.axis_size("req")
    owned = lax.axis_index("seq") * local_experts + jnp.arange(local_experts, dtype=jnp.int32)
    chosen = routes.reshape(row_count, TOP)
    gates = route_weights.reshape(row_count, TOP)
    matches = chosen[None, :, :] == owned[:, None, None]
    routed = jnp.any(matches, axis=-1)
    route_scale = jnp.sum(jnp.where(matches, gates[None, :, :], 0.0), axis=-1)
    ordinal = jnp.cumsum(routed.astype(jnp.int32), axis=1) - 1
    placed = routed[:, :, None] & (
        ordinal[:, :, None] == jnp.arange(CAP, dtype=jnp.int32)[None, None, :]
    )
    outgoing = jnp.einsum(
        "erc,rd->ecd", placed.astype(jnp.bfloat16), mixed_in, preferred_element_type=jnp.float32
    ).astype(jnp.bfloat16)
    arrived = lax.all_to_all(outgoing[:, None], "req", split_axis=3, concat_axis=1, tiled=True)
    slice_width = arrived.shape[3]
    arrived = arrived.reshape(local_experts, groups * CAP, slice_width)
    partial_values = jnp.einsum(
        "end,edf->enf", arrived, w_gate_up, preferred_element_type=jnp.float32
    )
    gate_up = lax.psum(partial_values, "req")
    hidden = (jax.nn.silu(gate_up[..., :FFE]) * gate_up[..., FFE:]).astype(jnp.bfloat16)
    produced = jnp.einsum("enf,efd->end", hidden, w_down, preferred_element_type=jnp.float32)
    returned = lax.all_to_all(
        produced.reshape(local_experts, groups, CAP, slice_width),
        "req",
        split_axis=1,
        concat_axis=3,
        tiled=True,
    )[:, 0]
    weighted = placed.astype(jnp.float32) * route_scale[:, :, None]
    expert_total = jnp.einsum("erc,ecd->rd", weighted, returned, precision=lax.Precision.HIGHEST)
    own_share = lax.psum_scatter(expert_total, "seq", scatter_dimension=1, tiled=True)
    share_width = own_share.shape[1]
    resid_share = lax.dynamic_slice_in_dim(
        resid, lax.axis_index("seq") * share_width, share_width, 1
    )
    return (
        (resid_share + own_share).astype(jnp.bfloat16).reshape(local_requests, NSTEP, share_width)
    )


F32 = jnp.float32
BF16 = jnp.bfloat16
STAT = 128
WIDE = KVD + STAT
VMEM = pl.BlockSpec(memory_space=pltpu.VMEM)
SMEM = pl.BlockSpec(memory_space=pltpu.SMEM)
HBM = pl.BlockSpec(memory_space=pltpu.HBM)


def kernel_call(body, out_shape, in_specs, scratch=(), out_specs=None, vmem_mib=8, cost=2.0):
    return pl.pallas_call(
        body,
        out_shape=out_shape,
        in_specs=in_specs,
        out_specs=out_specs or ([VMEM] * len(out_shape) if isinstance(out_shape, list) else VMEM),
        scratch_shapes=list(scratch),
        compiler_params=pltpu.CompilerParams(vmem_limit_bytes=vmem_mib * 2**20),
        cost_estimate=pl.CostEstimate(
            flops=int(cost * 1e9), bytes_accessed=int(cost * 3e6), transcendentals=0
        ),
    )


def iota(shape, dim):
    return lax.broadcasted_iota(jnp.int32, shape, dim)


def split3(value):
    high = value.astype(BF16).astype(F32)
    rest = value - high
    middle = rest.astype(BF16).astype(F32)
    return high, middle, rest - middle


def rows_of(ref):
    return jnp.concatenate([ref[r].astype(F32) for r in range(ref.shape[0])], axis=0)


def dot_nt(left, right):
    return lax.dot_general(left, right, (((1,), (1,)), ((), ())), preferred_element_type=F32)


def swap(value, axis, mask):
    pairs = [(i, i ^ mask) for i in range(lax.axis_size(axis))]
    return lax.ppermute(value, axis, pairs)


def after(value, *others):
    return lax.optimization_barrier((value, *others))[0]


def project_kernel(*refs):
    x_hbm, attn_hbm, w_hbm, lengths_hbm, heads_ref, x_ref = refs[:6]
    x_in, attn_gain, w_in, lengths, sem = refs[6:]
    loads = [
        pltpu.make_async_copy(source, target, sem.at[i])
        for i, (source, target) in enumerate(
            [(lengths_hbm, lengths), (x_hbm, x_in), (attn_hbm, attn_gain), (w_hbm, w_in)]
        )
    ]
    for load in loads:
        load.start()
    requests = x_in.shape[0]
    row_count = requests * NSTEP
    shape = (row_count, STAT)
    loads[0].wait()
    row, lane = iota(shape, 0), iota(shape, 1)
    position = row % NSTEP
    for r in range(requests):
        position = position + jnp.where(row // NSTEP == r, lengths[r], 0)
    rates = jnp.exp((lane % (HD // 2)).astype(F32) * (-2.0 * math.log(10000.0) / HD))
    angle = position.astype(F32) * rates
    cosine = jnp.cos(angle)
    sine = jnp.where(lane % HD < HD // 2, -jnp.sin(angle), jnp.sin(angle))
    loads[1].wait()
    x = rows_of(x_in)
    width = x_ref.shape[1]
    own = pl.ds(pl.multiple_of((lax.axis_index("seq") // 2) * width, STAT), width)
    x_ref[...] = jnp.concatenate([x_in[r, :, own].astype(F32) for r in range(requests)], axis=0)
    power = jnp.mean(x * x, axis=-1, keepdims=True)
    loads[2].wait()
    normed = (x * lax.rsqrt(power + EPS) * attn_gain[...].reshape(1, D)).astype(BF16)
    loads[3].wait()
    projected = dot_nt(normed, w_in[...])
    heads = w_in.shape[0] // HD
    first = lax.axis_index("seq") * heads
    for i in range(heads):
        one = projected[:, i * HD : (i + 1) * HD]
        both = jnp.concatenate([one, one], axis=1)
        turned = both * cosine + pltpu.roll(both, HD // 2, 1) * sine
        heads_ref[i] = jnp.where(first + i < HEADS + KVH, turned, both).astype(BF16)


def prepare_kernel(heads_in, pages, lengths, routes, weights, moe_gain, *out_refs):
    heads_ref, live_ref, routing_ref, gain_ref = out_refs
    heads_ref[...] = heads_in[...]
    slots = live_ref.shape[1]
    slot = iota((1, slots), 1)
    for r in range(live_ref.shape[0]):
        page = jnp.zeros((1, slots), jnp.int32)
        for j in range(slots // PAGE):
            page = jnp.where(slot // PAGE == j, pages[r, j], page)
        live = page * PAGE + slot % PAGE < lengths[r]
        live_ref[r : r + 1, :] = jnp.where(live, 1.0, 0.0)
    row_count = routing_ref.shape[0]
    high, middle, low = split3(rows_of(weights))
    routing_ref[...] = jnp.concatenate(
        [rows_of(routes), high, middle, low, jnp.zeros((row_count, STAT - 4 * TOP), F32)], axis=1
    )
    gain_ref[...] = moe_gain[...].reshape(1, D)


def in_chip_order(near, far):
    first = lax.axis_index("seq") % 2 == 0
    return jnp.where(
        first, jnp.concatenate([near, far], axis=1), jnp.concatenate([far, near], axis=1)
    )


def gather_pieces(near_refs, far_refs, all_ref):
    core = lax.axis_index("seq") % 2
    for k in range(len(near_refs)):
        all_ref[core, k] = near_refs[k][...]
        all_ref[1 - core, k] = far_refs[k][...]


def paired(head, left, right):
    a = head(left)
    return jnp.where(iota(a.shape, 1) < HD, a, head(right))


def expanded(q_ref, r):
    rows = [q_ref[g, r * NSTEP : (r + 1) * NSTEP, :] for g in range(GROUP)]
    base = jnp.concatenate(rows + [jnp.zeros((NSTEP, KVD), F32)], axis=0)
    owner = iota(base.shape, 1) // HD
    return jnp.concatenate(
        [jnp.where(owner == k, base, 0.0) for k in range(KVH)], axis=0
    ).astype(BF16)


def attend_part(query, keys, values, live):
    scores = jnp.where(live, dot_nt(query, keys) * (HD ** (-0.5)), NEG)
    top = jnp.max(scores, axis=1, keepdims=True)
    exp_scores = jnp.where(live, jnp.exp(scores - top), 0.0)
    total = jnp.sum(exp_scores, axis=1, keepdims=True)
    return top, total, jnp.dot(exp_scores.astype(BF16), values, preferred_element_type=F32)


def place_rows(part_ref, r, row_count, top, total, sums):
    block = (GROUP + 1) * NSTEP
    owner = iota((block, KVD), 1) // HD
    lane = iota((block, STAT), 1)
    own_sums = jnp.zeros((block, KVD), F32)
    stats = jnp.zeros((block, STAT), F32)
    for k in range(KVH):
        rows = slice(k * block, (k + 1) * block)
        own_sums = jnp.where(owner == k, sums[rows], own_sums)
        value = jnp.where(lane < 3 * KVH, top[rows], total[rows])
        stats = jnp.where(lane % KVH == k, value, stats)
    high, middle, low = split3(stats)
    part = (lane // KVH) % 3
    stats = jnp.where(part == 0, high, jnp.where(part == 1, middle, low))
    for g in range(GROUP):
        rows = slice(g * row_count + r * NSTEP, g * row_count + (r + 1) * NSTEP)
        part_ref[rows, :KVD] = own_sums[g * NSTEP : (g + 1) * NSTEP]
        part_ref[rows, KVD:] = stats[g * NSTEP : (g + 1) * NSTEP]


def head_of(all_ref):
    chip = lax.axis_index("seq") // 2
    heads = all_ref.shape[2]

    def head(h):
        owner = h // heads
        return all_ref[owner % 2, chip ^ (owner // 2), h % heads].astype(F32)

    return head


def query_rows(head, q_ref):
    for g in range(GROUP):
        for m in range(KVH // 2):
            q_ref[g, :, m * STAT : (m + 1) * STAT] = paired(
                head, GROUP * 2 * m + g, GROUP * (2 * m + 1) + g
            )


def attend_kernel(chips, *refs):
    near_refs, far_refs = refs[:chips], refs[chips : 2 * chips]
    live_ref, k_ref, v_ref, out_ref, all_ref, q_ref, part_ref = refs[2 * chips :]
    requests = k_ref.shape[0]
    gather_pieces(near_refs, far_refs, all_ref)
    query_rows(head_of(all_ref), q_ref)
    for r in range(requests):
        live = live_ref[r : r + 1, :] > 0.5
        place_rows(
            part_ref,
            r,
            requests * NSTEP,
            *attend_part(expanded(q_ref, r), k_ref[r], v_ref[r], live),
        )
    out_ref[...] = part_ref[...].astype(BF16)


def fresh_kernel(chips, *refs):
    near_refs, far_refs = refs[:chips], refs[chips : 2 * chips]
    out_ref, all_ref, q_ref, part_ref = refs[2 * chips :]
    gather_pieces(near_refs, far_refs, all_ref)
    head = head_of(all_ref)
    query_rows(head, q_ref)
    row_count = q_ref.shape[1]
    pad = jnp.zeros((STAT - row_count, KVD), F32)

    def new_rows(first):
        pieces = [paired(head, first + 2 * m, first + 2 * m + 1) for m in range(KVH // 2)]
        return jnp.concatenate([jnp.concatenate(pieces, axis=1), pad], axis=0).astype(BF16)

    keys, values = new_rows(HEADS), new_rows(HEADS + KVH)
    shape = ((GROUP + 1) * NSTEP * KVH, STAT)
    slot, step = iota(shape, 1), iota(shape, 0) % NSTEP
    for r in range(row_count // NSTEP):
        live = (slot // NSTEP == r) & (slot % NSTEP <= step)
        place_rows(
            part_ref, r, row_count, *attend_part(expanded(q_ref, r), keys, values, live)
        )
    out_ref[...] = part_ref[...].astype(BF16)


def merge_kernel(count, *refs):
    part_refs = refs[:count]
    x_ref, gain_ref, routing_ref, near_w, far_w, out_ref, resid_ref = refs[count:]
    parts = [ref[...].astype(F32) for ref in part_refs]
    tops, totals = [], []
    for part in parts:
        stats = part[:, KVD:]
        full = stats + (
            pltpu.roll(stats, STAT - KVH, 1) + pltpu.roll(stats, STAT - 2 * KVH, 1)
        )
        tops.append(full)
        totals.append(pltpu.roll(full, STAT - 3 * KVH, 1))
    highest = tops[0]
    for top in tops[1:]:
        highest = jnp.maximum(highest, top)
    factors = [jnp.exp(top - highest) for top in tops]
    denominator = factors[0] * totals[0]
    for factor, total in zip(factors[1:], totals[1:]):
        denominator = denominator + factor * total
    inverse = 1.0 / denominator
    row_total = parts[0].shape[0]
    row_count = row_total // GROUP
    owner = iota((STAT, KVD), 1) // HD == iota((STAT, KVD), 0)
    spread = jnp.where(owner, 1.0, 0.0).astype(BF16)
    valid = iota((row_total, STAT), 1) < KVH
    merged = jnp.zeros((row_total, KVD), F32)
    for part, factor in zip(parts, factors):
        weight = jnp.where(valid, factor * inverse, 0.0).astype(BF16)
        merged = merged + jnp.dot(weight, spread, preferred_element_type=F32) * part[:, :KVD]
    columns = [merged[:, m * STAT : (m + 1) * STAT] for m in range(KVH // 2)]

    def head(h, side):
        k, g = h // GROUP, h % GROUP
        rows = columns[k // 2][g * row_count : (g + 1) * row_count]
        return rows if k % 2 == side else pltpu.roll(rows, HD, 1)

    left = iota((row_count, STAT), 1) < HD
    attended = jnp.concatenate(
        [jnp.where(left, head(2 * n, 0), head(2 * n + 1, 1)) for n in range(HEADS // 2)], axis=1
    ).astype(BF16)
    share = in_chip_order(dot_nt(attended, near_w[...]), dot_nt(attended, far_w[...]))
    width = near_w.shape[0]
    member = lax.axis_index("seq")
    both = pl.ds(pl.multiple_of((member // 2) * (2 * width), STAT), 2 * width)
    resid = x_ref[...] + share
    resid_ref[...] = jnp.where(member % 2 == 0, resid[:, :width], resid[:, width:])
    stats = routing_ref[...]
    lane = iota(stats.shape, 1)
    for i, value in enumerate(split3(jnp.sum(resid * resid, axis=1, keepdims=True))):
        stats = jnp.where(lane == 4 * TOP + i, value, stats)
    out_ref[:, : 2 * width] = (resid * gain_ref[:, both]).astype(BF16)
    out_ref[:, 2 * width :] = stats.astype(BF16)


def across(column, eye):
    return jnp.sum(jnp.where(eye, column, 0.0), axis=0, keepdims=True)


def gate_kernel(groups, *refs):
    near_refs, far_refs, w_ref = refs[: groups // 2], refs[groups // 2 : groups], refs[groups]
    message_refs = refs[groups + 1 : 2 * groups + 1]
    placed_ref, scale_ref, full_ref = refs[2 * groups + 1 :]
    member, me = lax.axis_index("seq"), lax.axis_index("req")
    width = w_ref.shape[1]
    row_count = near_refs[0].shape[0]
    tokens = groups * row_count
    near = jnp.concatenate([ref[...].astype(F32) for ref in near_refs], axis=0)
    far = jnp.concatenate([ref[...].astype(F32) for ref in far_refs], axis=0)
    first = member % 2 == 0
    pieces = jnp.concatenate([jnp.where(first, far, near), jnp.where(first, near, far)], axis=0)
    mixed, routing = pieces[:, :width].astype(BF16), pieces[:, width:]
    power = routing[:, 4 * TOP : 4 * TOP + 1] + (
        routing[:, 4 * TOP + 1 : 4 * TOP + 2] + routing[:, 4 * TOP + 2 : 4 * TOP + 3]
    )
    chosen = routing[:, :TOP]
    gates = routing[:, TOP : 2 * TOP] + (
        routing[:, 2 * TOP : 3 * TOP] + routing[:, 3 * TOP : 4 * TOP]
    )
    experts = w_ref.shape[0]
    square = (tokens, tokens)
    eye = iota(square, 0) == iota(square, 1)
    earlier = (iota(square, 0) < iota(square, 1)) & (
        iota(square, 0) // row_count == iota(square, 1) // row_count
    )
    slots = groups * CAP
    shape = (slots, tokens)
    block = iota(shape, 1) // row_count
    home = jnp.zeros(shape, jnp.int32)
    for b, mask in enumerate((3, 2, 1, 0)):
        home = jnp.where(block == b, mask ^ (member // 2), home)
    slot = iota(shape, 0)
    same_group = slot // CAP == home
    ordinal_of_slot = (slot % CAP).astype(F32)
    placed, scales = [], []
    row = iota((16, tokens), 0)
    power_rows = jnp.zeros((16, tokens), F32)
    for i, part in enumerate(split3(across(power, eye))):
        power_rows = jnp.where(row == i, part, power_rows)
    power_rows = power_rows.astype(BF16)
    for e in range(experts):
        match = chosen == (member * experts + e).astype(F32)
        routed = jnp.max(jnp.where(match, 1.0, 0.0), axis=1, keepdims=True)
        scale = jnp.sum(jnp.where(match, gates, 0.0), axis=1, keepdims=True)
        ordinal = across(routed, earlier)
        here = same_group & (across(routed, eye) > 0.5) & (ordinal_of_slot == ordinal)
        placed.append(jnp.where(here, 1.0, 0.0))
        scales.append(jnp.sum(jnp.where(here, across(scale, eye), 0.0), axis=1, keepdims=True))
    all_placed = jnp.concatenate(placed, axis=0).astype(BF16)
    taken = jnp.dot(all_placed, mixed, preferred_element_type=F32).astype(BF16)
    for e in range(experts):
        rows = slice(e * slots, (e + 1) * slots)
        placed_ref[e] = all_placed[rows]
        scale_ref[e] = jnp.broadcast_to(scales[e], scale_ref.shape[1:])
        gate_up = jnp.dot(taken[rows], w_ref[e], preferred_element_type=F32).astype(BF16)
        for j in range(2 * FFE // STAT):
            full_ref[e, j * slots : (j + 1) * slots, :] = gate_up[:, j * STAT : (j + 1) * STAT]
        slot_power = dot_nt(power_rows, placed_ref[e])
        full_ref[e, 2 * FFE // STAT * slots :, :] = jnp.concatenate(
            [slot_power, jnp.zeros((16, STAT - slots), F32)], axis=1
        ).astype(BF16)
    for k in range(groups):
        message_refs[k][...] = full_ref[me ^ k]


def hidden_kernel(*refs):
    out_ref = refs[-1]
    gate_up = refs[0][...].astype(F32)
    for ref in refs[1:-1]:
        gate_up = gate_up + ref[...].astype(F32)
    slots = out_ref.shape[0]
    chunks = FFE // STAT
    stats = gate_up[2 * chunks * slots :, :slots]
    power = stats[0:1] + (stats[1:2] + stats[2:3])
    eye = iota((slots, slots), 0) == iota((slots, slots), 1)
    power = jnp.sum(jnp.where(eye, power, 0.0), axis=1, keepdims=True)
    scale = lax.rsqrt(power / D + EPS)
    for j in range(chunks):
        gate = gate_up[j * slots : (j + 1) * slots] * scale
        up = gate_up[(chunks + j) * slots : (chunks + j + 1) * slots] * scale
        out_ref[:, j * STAT : (j + 1) * STAT] = (gate / (1.0 + jnp.exp(-gate)) * up).astype(BF16)


def down_kernel(groups, *refs):
    hidden_refs = refs[:groups]
    w_ref, placed_ref, scale_ref, send_ref, keep_ref = refs[groups:]
    me, core = lax.axis_index("req"), lax.axis_index("seq") % 2
    total = jnp.zeros((placed_ref.shape[2], w_ref.shape[2]), F32)
    for k, hidden_ref in enumerate(hidden_refs):
        expert = me ^ k
        produced = jnp.dot(hidden_ref[...], w_ref[expert], preferred_element_type=F32)
        total = total + lax.dot_general(
            placed_ref[expert],
            (produced * scale_ref[expert][:, :1]).astype(BF16),
            (((0,), (0,)), ((), ())),
            preferred_element_type=F32,
        )
    half = total.shape[0] // 2
    low, high = total[:half], total[half:]
    send_ref[...] = jnp.where(core == 0, high, low).astype(BF16)
    keep_ref[...] = jnp.where(core == 0, low, high)


def spread_kernel(keep_ref, arrived_ref, *out_refs):
    total = keep_ref[...] + arrived_ref[...].astype(F32)
    row_count = out_refs[0].shape[0]
    for k, out_ref in enumerate(out_refs):
        out_ref[...] = total[k * row_count : (k + 1) * row_count].astype(BF16)


def halve_kernel(resid_ref, *refs):
    arrived_refs, send_ref, keep_ref = refs[:-2], refs[-2], refs[-1]
    total = arrived_refs[0][...].astype(F32)
    for ref in arrived_refs[1:]:
        total = total + ref[...].astype(F32)
    width = total.shape[1] // 2
    left, right = total[:, :width], total[:, width:]
    first = lax.axis_index("seq") % 2 == 0
    send_ref[...] = jnp.where(first, right, left)
    keep_ref[...] = resid_ref[...] + jnp.where(first, left, right)


def final_kernel(keep_ref, arrived_ref, out_ref):
    total = keep_ref[...] + arrived_ref[...]
    for r in range(out_ref.shape[0]):
        out_ref[r] = total[r * NSTEP : (r + 1) * NSTEP].astype(BF16)


def staged(
    x_in,
    attn_gain,
    moe_gain,
    w_qkv,
    w_o,
    cache_k,
    cache_v,
    page_map,
    lengths,
    routes,
    route_weights,
    w_gate_up,
    w_down,
):
    requests = x_in.shape[0]
    row_count = requests * NSTEP
    members, groups = lax.axis_size("seq"), lax.axis_size("req")
    chips = members // 2
    heads = w_qkv.shape[1] // HD
    width = w_o.shape[1]

    heads_shape = jax.ShapeDtypeStruct((heads, row_count, 2 * HD), BF16)
    own_heads, x = kernel_call(
        project_kernel,
        [heads_shape, jax.ShapeDtypeStruct((row_count, 2 * width), F32)],
        [HBM] * 4,
        [
            pltpu.VMEM(x_in.shape, BF16),
            pltpu.VMEM((D,), F32),
            pltpu.VMEM((w_qkv.shape[1], D), BF16),
            pltpu.SMEM(lengths.shape, jnp.int32),
            pltpu.SemaphoreType.DMA((4,)),
        ],
        vmem_mib=60,
        cost=5.0,
    )(x_in, attn_gain, w_qkv.T, lengths)

    def gathered(own):
        return [own] + [swap(own, "seq", 2 * k) for k in range(1, chips)]

    near = gathered(own_heads)
    first = near[1]
    near[0], live, routing, gain = kernel_call(
        prepare_kernel,
        [
            heads_shape,
            jax.ShapeDtypeStruct((requests, cache_k.shape[1]), F32),
            jax.ShapeDtypeStruct((row_count, STAT), F32),
            jax.ShapeDtypeStruct((1, D), F32),
        ],
        [VMEM] + [SMEM] * 2 + [VMEM] * 3,
    )(after(own_heads, near[1]), page_map, lengths, routes, route_weights, moe_gain)
    near[1] = after(near[1], live)
    far = [swap(piece, "seq", 1) for piece in [after(own_heads, first)] + near[1:]]
    part_shape = jax.ShapeDtypeStruct((GROUP * row_count, WIDE), BF16)
    head_scratch = [
        pltpu.VMEM((2, chips, heads, row_count, 2 * HD), BF16),
        pltpu.VMEM((GROUP, row_count, KVD), F32),
        pltpu.VMEM((GROUP * row_count, WIDE), F32),
    ]
    part = kernel_call(
        lambda *refs: attend_kernel(chips, *refs),
        part_shape,
        [VMEM] * (2 * chips + 3),
        head_scratch,
    )(*near, *far, live, cache_k, cache_v)
    fresh = kernel_call(
        lambda *refs: fresh_kernel(chips, *refs),
        part_shape,
        [VMEM] * (2 * chips),
        head_scratch,
    )(*near, *far)
    near = gathered(part)
    near[1] = after(near[1], fresh)
    far = [swap(piece, "seq", 1) for piece in [after(part, near[1])] + near[1:]]
    packed, resid = kernel_call(
        lambda *refs: merge_kernel(members + 1, *refs),
        [
            jax.ShapeDtypeStruct((row_count, 2 * width + STAT), BF16),
            jax.ShapeDtypeStruct((row_count, width), F32),
        ],
        [VMEM] * (members + 6),
    )(*near, *far, fresh, x, gain, routing, w_o.T, swap(w_o.T, "seq", 1))

    everyone = [(p, c, q) for p in range(chips) for c in range(2) for q in range(groups)]

    def crossing(j):
        return [
            ((2 * p + c) * groups + q, (2 * (q ^ MASKS[c][j]) + 1 - c) * groups + p)
            for p, c, q in everyone
        ]

    def returning(j):
        return [
            ((2 * p + c) * groups + q, (2 * q + 1 - c) * groups + (p ^ MASKS[c][j]))
            for p, c, q in everyone
        ]

    place = ("seq", "req")
    near = [lax.ppermute(packed, place, crossing(j)) for j in range(groups // 2)]
    far = [swap(piece, "seq", 1) for piece in near]
    experts = w_gate_up.shape[0]
    slots = groups * CAP
    message = jax.ShapeDtypeStruct((2 * FFE // STAT * slots + 16, STAT), BF16)
    *messages, placed, scale = kernel_call(
        lambda *refs: gate_kernel(groups, *refs),
        [message] * groups
        + [
            jax.ShapeDtypeStruct((experts, slots, groups * row_count), BF16),
            jax.ShapeDtypeStruct((experts, slots, STAT), F32),
        ],
        [VMEM] * (groups + 1),
        [pltpu.VMEM((experts, *message.shape), BF16)],
    )(*near, *far, w_gate_up)
    sums = [messages[0]] + [swap(messages[k], "req", k) for k in (3, 1, 2)]
    hidden = kernel_call(
        hidden_kernel, jax.ShapeDtypeStruct((slots, FFE), BF16), [VMEM] * groups
    )(*sums)
    hiddens = [hidden] + [swap(hidden, "req", k) for k in range(1, groups)]
    half = (groups * row_count // 2, 2 * width)
    send, keep = kernel_call(
        lambda *refs: down_kernel(groups, *refs),
        [jax.ShapeDtypeStruct(half, BF16), jax.ShapeDtypeStruct(half, F32)],
        [VMEM] * (groups + 3),
    )(*hiddens, w_down, placed, scale)
    outs = kernel_call(
        spread_kernel,
        [jax.ShapeDtypeStruct((row_count, 2 * width), BF16)] * (groups // 2),
        [VMEM] * 2,
    )(keep, swap(send, "seq", 1))
    arrived = [lax.ppermute(out, place, returning(j)) for j, out in enumerate(outs)]
    send, keep = kernel_call(
        halve_kernel,
        [jax.ShapeDtypeStruct((row_count, width), F32)] * 2,
        [VMEM] * (1 + groups // 2),
    )(resid, *arrived)
    return kernel_call(
        final_kernel, jax.ShapeDtypeStruct((requests, NSTEP, width), BF16), [VMEM] * 2
    )(keep, swap(send, "seq", 1))


def local(*args):
    w_qkv, w_o, w_gate_up = args[3], args[4], args[11]
    members, groups = lax.axis_size("seq"), lax.axis_size("req")
    fits = (
        members == 8
        and groups == 4
        and w_qkv.shape[1] % HD == 0
        and w_gate_up.shape[0] == groups
        and (2 * w_o.shape[1]) % STAT == 0
    )
    return staged(*args) if fits else plain(*args)


def solution(mesh):
    in_specs = (
        P("req", None, None),
        P(),
        P(),
        P(None, "seq"),
        P(None, "seq"),
        P("req", "seq", None),
        P("req", "seq", None),
        P("req", "seq"),
        P("req"),
        P("req", None, None),
        P("req", None, None),
        P("seq", "req", None),
        P("seq", None, "req"),
    )
    out_specs = P("req", None, "seq")
    return jax.shard_map(local, mesh=mesh, in_specs=in_specs, out_specs=out_specs, check_vma=False)
```

```python
import math

import jax
import jax.numpy as jnp
from jax import lax
from jax.experimental import pallas as pl
from jax.experimental.pallas import tpu as pltpu
from jax.sharding import PartitionSpec as P

D = 1536
HEADS = 24
KVH = 8
HD = 64
FFE = 512
TOP = 8
NSTEP = 4
PAGE = 16
ATT = 1536
KVD = 512
GROUP = 3
CAP = 12
MASKS = ((3, 2), (1, 0))


EPS = 1e-05
NEG = -1e30


def combined_all(value, axis, join):
    pieces = jax.tree.map(lambda part: lax.all_gather(part, axis), value)
    head = jax.tree.map(lambda part: part[0], pieces)
    tail = jax.tree.map(lambda part: part[1:], pieces)
    so_far, _ = lax.scan(lambda so_far, piece: (join(so_far, piece), None), head, tail)
    return so_far


def normalize(values, gain):
    power = jnp.mean(values * values, axis=-1, keepdims=True)
    return values * lax.rsqrt(power + EPS) * gain


def rotate(values, position):
    half = values.shape[-1] // 2
    rates = jnp.exp(
        jnp.arange(half, dtype=jnp.float32) * (-2.0 * math.log(10000.0) / values.shape[-1])
    )
    angle = position[..., None, None] * rates
    cosine = jnp.cos(angle)
    sine = jnp.sin(angle)
    first_half = values[..., :half]
    second_half = values[..., half:]
    return jnp.concatenate(
        [first_half * cosine - second_half * sine, second_half * cosine + first_half * sine],
        axis=-1,
    )


def softmax_join(left, right):
    left_top, left_total, left_sums = left
    right_top, right_total, right_sums = right
    highest = jnp.maximum(left_top, right_top)
    left_factor = jnp.exp(left_top - highest)
    right_factor = jnp.exp(right_top - highest)
    row_count, head_count = highest.shape
    left_part = left_sums.reshape(row_count, head_count, -1) * left_factor[:, :, None]
    right_part = right_sums.reshape(row_count, head_count, -1) * right_factor[:, :, None]
    joined = (left_part + right_part).reshape(row_count, -1)
    return (highest, left_total * left_factor + right_total * right_factor, joined)


def project_with(left, piece):
    return jnp.dot(left, piece, preferred_element_type=jnp.float32)


def plain(
    x_in,
    attn_gain,
    moe_gain,
    w_qkv,
    w_o,
    cache_k,
    cache_v,
    page_map,
    lengths,
    routes,
    route_weights,
    w_gate_up,
    w_down,
):
    local_requests = x_in.shape[0]
    row_count = local_requests * NSTEP
    inputs = x_in.astype(jnp.float32).reshape(row_count, D)
    normed = normalize(inputs, attn_gain).astype(jnp.bfloat16)
    projected = project_with(normed, lax.all_gather(w_qkv, "seq", axis=1, tiled=True))
    queries = projected[:, :ATT].reshape(local_requests, NSTEP, HEADS, HD)
    keys_new = projected[:, ATT : ATT + KVD].reshape(local_requests, NSTEP, KVH, HD)
    values_new = (
        projected[:, ATT + KVD :].reshape(local_requests, NSTEP, KVH, HD).astype(jnp.bfloat16)
    )
    position = (lengths[:, None] + jnp.arange(NSTEP, dtype=jnp.int32)[None, :]).astype(jnp.float32)
    queries = (
        rotate(queries, position)
        .astype(jnp.bfloat16)
        .reshape(local_requests, NSTEP, KVH, GROUP, HD)
    )
    keys_new = rotate(keys_new, position).astype(jnp.bfloat16)
    scale = HD ** (-0.5)
    slot_count = cache_k.shape[1]
    cached_keys = cache_k.reshape(local_requests, slot_count, KVH, HD)
    cached_values = cache_v.reshape(local_requests, slot_count, KVH, HD)
    slot_position = (
        page_map[:, :, None] * PAGE + jnp.arange(PAGE, dtype=jnp.int32)[None, None, :]
    ).reshape(local_requests, slot_count)
    live = (slot_position < lengths[:, None])[:, None, None, None, :]
    scores = (
        jnp.einsum("rskgd,rtkd->rskgt", queries, cached_keys, preferred_element_type=jnp.float32)
        * scale
    )
    scores = jnp.where(live, scores, NEG)
    local_top = jnp.max(scores, axis=-1)
    exp_scores = jnp.where(live, jnp.exp(scores - local_top[..., None]), 0.0)
    local_total = jnp.sum(exp_scores, axis=-1).reshape(row_count, HEADS)
    local_sums = jnp.einsum(
        "rskgt,rtkd->rskgd",
        exp_scores.astype(jnp.bfloat16),
        cached_values,
        preferred_element_type=jnp.float32,
    ).reshape(row_count, ATT)
    local_top = local_top.reshape(row_count, HEADS)
    cache_top, cache_total, cache_sums = combined_all(
        (local_top, local_total, local_sums), "seq", softmax_join
    )
    causal = (
        jnp.arange(NSTEP, dtype=jnp.int32)[:, None] >= jnp.arange(NSTEP, dtype=jnp.int32)[None, :]
    )[None, :, None, None, :]
    fresh = (
        jnp.einsum("rskgd,rukd->rskgu", queries, keys_new, preferred_element_type=jnp.float32)
        * scale
    )
    fresh = jnp.where(causal, fresh, NEG).reshape(row_count, HEADS, NSTEP)
    highest = jnp.maximum(cache_top, jnp.max(fresh, axis=-1))
    fresh_exp = jnp.exp(fresh - highest[:, :, None])
    carried = jnp.exp(cache_top - highest)
    denominator = cache_total * carried + jnp.sum(fresh_exp, axis=-1)
    fresh_probs = fresh_exp.reshape(local_requests, NSTEP, KVH, GROUP, NSTEP).astype(jnp.bfloat16)
    fresh_sums = jnp.einsum(
        "rskgu,rukd->rskgd", fresh_probs, values_new, preferred_element_type=jnp.float32
    ).reshape(row_count, HEADS, HD)
    numerator = cache_sums.reshape(row_count, HEADS, HD) * carried[:, :, None] + fresh_sums
    attended = (numerator / denominator[:, :, None]).reshape(row_count, ATT).astype(jnp.bfloat16)
    attn_mixed = project_with(attended, lax.all_gather(w_o, "seq", axis=1, tiled=True))
    resid = inputs + attn_mixed
    mixed_in = normalize(resid, moe_gain).astype(jnp.bfloat16)
    local_experts = w_gate_up.shape[0]
    groups = lax.axis_size("req")
    owned = lax.axis_index("seq") * local_experts + jnp.arange(local_experts, dtype=jnp.int32)
    chosen = routes.reshape(row_count, TOP)
    gates = route_weights.reshape(row_count, TOP)
    matches = chosen[None, :, :] == owned[:, None, None]
    routed = jnp.any(matches, axis=-1)
    route_scale = jnp.sum(jnp.where(matches, gates[None, :, :], 0.0), axis=-1)
    ordinal = jnp.cumsum(routed.astype(jnp.int32), axis=1) - 1
    placed = routed[:, :, None] & (
        ordinal[:, :, None] == jnp.arange(CAP, dtype=jnp.int32)[None, None, :]
    )
    outgoing = jnp.einsum(
        "erc,rd->ecd", placed.astype(jnp.bfloat16), mixed_in, preferred_element_type=jnp.float32
    ).astype(jnp.bfloat16)
    arrived = lax.all_to_all(outgoing[:, None], "req", split_axis=3, concat_axis=1, tiled=True)
    slice_width = arrived.shape[3]
    arrived = arrived.reshape(local_experts, groups * CAP, slice_width)
    partial_values = jnp.einsum(
        "end,edf->enf", arrived, w_gate_up, preferred_element_type=jnp.float32
    )
    gate_up = lax.psum(partial_values, "req")
    hidden = (jax.nn.silu(gate_up[..., :FFE]) * gate_up[..., FFE:]).astype(jnp.bfloat16)
    produced = jnp.einsum("enf,efd->end", hidden, w_down, preferred_element_type=jnp.float32)
    returned = lax.all_to_all(
        produced.reshape(local_experts, groups, CAP, slice_width),
        "req",
        split_axis=1,
        concat_axis=3,
        tiled=True,
    )[:, 0]
    weighted = placed.astype(jnp.float32) * route_scale[:, :, None]
    expert_total = jnp.einsum("erc,ecd->rd", weighted, returned, precision=lax.Precision.HIGHEST)
    own_share = lax.psum_scatter(expert_total, "seq", scatter_dimension=1, tiled=True)
    share_width = own_share.shape[1]
    resid_share = lax.dynamic_slice_in_dim(
        resid, lax.axis_index("seq") * share_width, share_width, 1
    )
    return (
        (resid_share + own_share).astype(jnp.bfloat16).reshape(local_requests, NSTEP, share_width)
    )


F32 = jnp.float32
BF16 = jnp.bfloat16
STAT = 128
WIDE = KVD + STAT
VMEM = pl.BlockSpec(memory_space=pltpu.VMEM)
SMEM = pl.BlockSpec(memory_space=pltpu.SMEM)
HBM = pl.BlockSpec(memory_space=pltpu.HBM)


def kernel_call(body, out_shape, in_specs, scratch=(), out_specs=None, vmem_mib=8, cost=2.0):
    return pl.pallas_call(
        body,
        out_shape=out_shape,
        in_specs=in_specs,
        out_specs=out_specs or ([VMEM] * len(out_shape) if isinstance(out_shape, list) else VMEM),
        scratch_shapes=list(scratch),
        compiler_params=pltpu.CompilerParams(vmem_limit_bytes=vmem_mib * 2**20),
        cost_estimate=pl.CostEstimate(
            flops=int(cost * 1e9), bytes_accessed=int(cost * 3e6), transcendentals=0
        ),
    )


def iota(shape, dim):
    return lax.broadcasted_iota(jnp.int32, shape, dim)


def split3(value):
    high = value.astype(BF16).astype(F32)
    rest = value - high
    middle = rest.astype(BF16).astype(F32)
    return high, middle, rest - middle


def rows_of(ref):
    return jnp.concatenate([ref[r].astype(F32) for r in range(ref.shape[0])], axis=0)


def dot_nt(left, right):
    return lax.dot_general(left, right, (((1,), (1,)), ((), ())), preferred_element_type=F32)


def swap(value, axis, mask):
    pairs = [(i, i ^ mask) for i in range(lax.axis_size(axis))]
    return lax.ppermute(value, axis, pairs)


def after(value, *others):
    return lax.optimization_barrier((value, *others))[0]


def project_kernel(*refs):
    x_hbm, attn_hbm, w_hbm, lengths_hbm, heads_ref, x_ref = refs[:6]
    x_in, attn_gain, w_in, lengths, sem = refs[6:]
    loads = [
        pltpu.make_async_copy(source, target, sem.at[i])
        for i, (source, target) in enumerate(
            [(lengths_hbm, lengths), (x_hbm, x_in), (attn_hbm, attn_gain), (w_hbm, w_in)]
        )
    ]
    for load in loads:
        load.start()
    requests = x_in.shape[0]
    row_count = requests * NSTEP
    shape = (row_count, STAT)
    loads[0].wait()
    row, lane = iota(shape, 0), iota(shape, 1)
    position = row % NSTEP
    for r in range(requests):
        position = position + jnp.where(row // NSTEP == r, lengths[r], 0)
    rates = jnp.exp((lane % (HD // 2)).astype(F32) * (-2.0 * math.log(10000.0) / HD))
    angle = position.astype(F32) * rates
    cosine = jnp.cos(angle)
    sine = jnp.where(lane % HD < HD // 2, -jnp.sin(angle), jnp.sin(angle))
    loads[1].wait()
    x = rows_of(x_in)
    width = x_ref.shape[1]
    own = pl.ds(pl.multiple_of((lax.axis_index("seq") // 2) * width, STAT), width)
    x_ref[...] = jnp.concatenate([x_in[r, :, own].astype(F32) for r in range(requests)], axis=0)
    power = jnp.mean(x * x, axis=-1, keepdims=True)
    loads[2].wait()
    normed = (x * lax.rsqrt(power + EPS) * attn_gain[...].reshape(1, D)).astype(BF16)
    loads[3].wait()
    projected = dot_nt(normed, w_in[...])
    heads = w_in.shape[0] // HD
    first = lax.axis_index("seq") * heads
    for i in range(heads):
        one = projected[:, i * HD : (i + 1) * HD]
        both = jnp.concatenate([one, one], axis=1)
        turned = both * cosine + pltpu.roll(both, HD // 2, 1) * sine
        heads_ref[i] = jnp.where(first + i < HEADS + KVH, turned, both).astype(BF16)


def prepare_kernel(heads_in, pages, lengths, routes, weights, moe_gain, *out_refs):
    heads_ref, live_ref, routing_ref, gain_ref = out_refs
    heads_ref[...] = heads_in[...]
    slots = live_ref.shape[1]
    slot = iota((1, slots), 1)
    for r in range(live_ref.shape[0]):
        page = jnp.zeros((1, slots), jnp.int32)
        for j in range(slots // PAGE):
            page = jnp.where(slot // PAGE == j, pages[r, j], page)
        live = page * PAGE + slot % PAGE < lengths[r]
        live_ref[r : r + 1, :] = jnp.where(live, 1.0, 0.0)
    row_count = routing_ref.shape[0]
    high, middle, low = split3(rows_of(weights))
    routing_ref[...] = jnp.concatenate(
        [rows_of(routes), high, middle, low, jnp.zeros((row_count, STAT - 4 * TOP), F32)], axis=1
    )
    gain_ref[...] = moe_gain[...].reshape(1, D)


def in_chip_order(near, far):
    first = lax.axis_index("seq") % 2 == 0
    return jnp.where(
        first, jnp.concatenate([near, far], axis=1), jnp.concatenate([far, near], axis=1)
    )


def gather_pieces(near_refs, far_refs, all_ref):
    core = lax.axis_index("seq") % 2
    for k in range(len(near_refs)):
        all_ref[core, k] = near_refs[k][...]
        all_ref[1 - core, k] = far_refs[k][...]


def paired(head, left, right):
    a = head(left)
    return jnp.where(iota(a.shape, 1) < HD, a, head(right))


def expanded(q_ref, r):
    rows = [q_ref[g, r * NSTEP : (r + 1) * NSTEP, :] for g in range(GROUP)]
    base = jnp.concatenate(rows + [jnp.zeros((NSTEP, KVD), F32)], axis=0)
    owner = iota(base.shape, 1) // HD
    return jnp.concatenate(
        [jnp.where(owner == k, base, 0.0) for k in range(KVH)], axis=0
    ).astype(BF16)


def attend_part(query, keys, values, live):
    scores = jnp.where(live, dot_nt(query, keys) * (HD ** (-0.5)), NEG)
    top = jnp.max(scores, axis=1, keepdims=True)
    exp_scores = jnp.where(live, jnp.exp(scores - top), 0.0)
    total = jnp.sum(exp_scores, axis=1, keepdims=True)
    return top, total, jnp.dot(exp_scores.astype(BF16), values, preferred_element_type=F32)


def place_rows(part_ref, r, row_count, top, total, sums):
    block = (GROUP + 1) * NSTEP
    owner = iota((block, KVD), 1) // HD
    lane = iota((block, STAT), 1)
    own_sums = jnp.zeros((block, KVD), F32)
    stats = jnp.zeros((block, STAT), F32)
    for k in range(KVH):
        rows = slice(k * block, (k + 1) * block)
        own_sums = jnp.where(owner == k, sums[rows], own_sums)
        value = jnp.where(lane < 3 * KVH, top[rows], total[rows])
        stats = jnp.where(lane % KVH == k, value, stats)
    high, middle, low = split3(stats)
    part = (lane // KVH) % 3
    stats = jnp.where(part == 0, high, jnp.where(part == 1, middle, low))
    for g in range(GROUP):
        rows = slice(g * row_count + r * NSTEP, g * row_count + (r + 1) * NSTEP)
        part_ref[rows, :KVD] = own_sums[g * NSTEP : (g + 1) * NSTEP]
        part_ref[rows, KVD:] = stats[g * NSTEP : (g + 1) * NSTEP]


def head_of(all_ref):
    chip = lax.axis_index("seq") // 2
    heads = all_ref.shape[2]

    def head(h):
        owner = h // heads
        return all_ref[owner % 2, chip ^ (owner // 2), h % heads].astype(F32)

    return head


def query_rows(head, q_ref):
    for g in range(GROUP):
        for m in range(KVH // 2):
            q_ref[g, :, m * STAT : (m + 1) * STAT] = paired(
                head, GROUP * 2 * m + g, GROUP * (2 * m + 1) + g
            )


def attend_kernel(chips, *refs):
    near_refs, far_refs = refs[:chips], refs[chips : 2 * chips]
    live_ref, k_ref, v_ref, out_ref, all_ref, q_ref, part_ref = refs[2 * chips :]
    requests = k_ref.shape[0]
    gather_pieces(near_refs, far_refs, all_ref)
    query_rows(head_of(all_ref), q_ref)
    for r in range(requests):
        live = live_ref[r : r + 1, :] > 0.5
        place_rows(
            part_ref,
            r,
            requests * NSTEP,
            *attend_part(expanded(q_ref, r), k_ref[r], v_ref[r], live),
        )
    out_ref[...] = part_ref[...].astype(BF16)


def fresh_kernel(chips, *refs):
    near_refs, far_refs = refs[:chips], refs[chips : 2 * chips]
    out_ref, all_ref, q_ref, part_ref = refs[2 * chips :]
    gather_pieces(near_refs, far_refs, all_ref)
    head = head_of(all_ref)
    query_rows(head, q_ref)
    row_count = q_ref.shape[1]
    pad = jnp.zeros((STAT - row_count, KVD), F32)

    def new_rows(first):
        pieces = [paired(head, first + 2 * m, first + 2 * m + 1) for m in range(KVH // 2)]
        return jnp.concatenate([jnp.concatenate(pieces, axis=1), pad], axis=0).astype(BF16)

    keys, values = new_rows(HEADS), new_rows(HEADS + KVH)
    shape = ((GROUP + 1) * NSTEP * KVH, STAT)
    slot, step = iota(shape, 1), iota(shape, 0) % NSTEP
    for r in range(row_count // NSTEP):
        live = (slot // NSTEP == r) & (slot % NSTEP <= step)
        place_rows(
            part_ref, r, row_count, *attend_part(expanded(q_ref, r), keys, values, live)
        )
    out_ref[...] = part_ref[...].astype(BF16)


def merge_kernel(count, *refs):
    part_refs = refs[:count]
    x_ref, gain_ref, routing_ref, near_w, far_w, out_ref, resid_ref = refs[count:]
    parts = [ref[...].astype(F32) for ref in part_refs]
    tops, totals = [], []
    for part in parts:
        stats = part[:, KVD:]
        full = stats + (
            pltpu.roll(stats, STAT - KVH, 1) + pltpu.roll(stats, STAT - 2 * KVH, 1)
        )
        tops.append(full)
        totals.append(pltpu.roll(full, STAT - 3 * KVH, 1))
    highest = tops[0]
    for top in tops[1:]:
        highest = jnp.maximum(highest, top)
    factors = [jnp.exp(top - highest) for top in tops]
    denominator = factors[0] * totals[0]
    for factor, total in zip(factors[1:], totals[1:]):
        denominator = denominator + factor * total
    inverse = 1.0 / denominator
    row_total = parts[0].shape[0]
    row_count = row_total // GROUP
    owner = iota((STAT, KVD), 1) // HD == iota((STAT, KVD), 0)
    spread = jnp.where(owner, 1.0, 0.0).astype(BF16)
    valid = iota((row_total, STAT), 1) < KVH
    merged = jnp.zeros((row_total, KVD), F32)
    for part, factor in zip(parts, factors):
        weight = jnp.where(valid, factor * inverse, 0.0).astype(BF16)
        merged = merged + jnp.dot(weight, spread, preferred_element_type=F32) * part[:, :KVD]
    columns = [merged[:, m * STAT : (m + 1) * STAT] for m in range(KVH // 2)]

    def head(h, side):
        k, g = h // GROUP, h % GROUP
        rows = columns[k // 2][g * row_count : (g + 1) * row_count]
        return rows if k % 2 == side else pltpu.roll(rows, HD, 1)

    left = iota((row_count, STAT), 1) < HD
    attended = jnp.concatenate(
        [jnp.where(left, head(2 * n, 0), head(2 * n + 1, 1)) for n in range(HEADS // 2)], axis=1
    ).astype(BF16)
    share = in_chip_order(dot_nt(attended, near_w[...]), dot_nt(attended, far_w[...]))
    width = near_w.shape[0]
    member = lax.axis_index("seq")
    both = pl.ds(pl.multiple_of((member // 2) * (2 * width), STAT), 2 * width)
    resid = x_ref[...] + share
    resid_ref[...] = jnp.where(member % 2 == 0, resid[:, :width], resid[:, width:])
    stats = routing_ref[...]
    lane = iota(stats.shape, 1)
    for i, value in enumerate(split3(jnp.sum(resid * resid, axis=1, keepdims=True))):
        stats = jnp.where(lane == 4 * TOP + i, value, stats)
    out_ref[:, : 2 * width] = (resid * gain_ref[:, both]).astype(BF16)
    out_ref[:, 2 * width :] = stats.astype(BF16)


def across(column, eye):
    return jnp.sum(jnp.where(eye, column, 0.0), axis=0, keepdims=True)


def gate_kernel(groups, *refs):
    near_refs, far_refs, w_ref = refs[: groups // 2], refs[groups // 2 : groups], refs[groups]
    message_refs = refs[groups + 1 : 2 * groups + 1]
    placed_ref, scale_ref, full_ref = refs[2 * groups + 1 :]
    member, me = lax.axis_index("seq"), lax.axis_index("req")
    width = w_ref.shape[1]
    row_count = near_refs[0].shape[0]
    tokens = groups * row_count
    near = jnp.concatenate([ref[...].astype(F32) for ref in near_refs], axis=0)
    far = jnp.concatenate([ref[...].astype(F32) for ref in far_refs], axis=0)
    first = member % 2 == 0
    pieces = jnp.concatenate([jnp.where(first, far, near), jnp.where(first, near, far)], axis=0)
    mixed, routing = pieces[:, :width].astype(BF16), pieces[:, width:]
    power = routing[:, 4 * TOP : 4 * TOP + 1] + (
        routing[:, 4 * TOP + 1 : 4 * TOP + 2] + routing[:, 4 * TOP + 2 : 4 * TOP + 3]
    )
    chosen = routing[:, :TOP]
    gates = routing[:, TOP : 2 * TOP] + (
        routing[:, 2 * TOP : 3 * TOP] + routing[:, 3 * TOP : 4 * TOP]
    )
    experts = w_ref.shape[0]
    square = (tokens, tokens)
    eye = iota(square, 0) == iota(square, 1)
    earlier = (iota(square, 0) < iota(square, 1)) & (
        iota(square, 0) // row_count == iota(square, 1) // row_count
    )
    slots = groups * CAP
    shape = (slots, tokens)
    block = iota(shape, 1) // row_count
    home = jnp.zeros(shape, jnp.int32)
    for b, mask in enumerate((3, 2, 1, 0)):
        home = jnp.where(block == b, mask ^ (member // 2), home)
    slot = iota(shape, 0)
    same_group = slot // CAP == home
    ordinal_of_slot = (slot % CAP).astype(F32)
    placed, scales = [], []
    row = iota((16, tokens), 0)
    power_rows = jnp.zeros((16, tokens), F32)
    for i, part in enumerate(split3(across(power, eye))):
        power_rows = jnp.where(row == i, part, power_rows)
    power_rows = power_rows.astype(BF16)
    for e in range(experts):
        match = chosen == (member * experts + e).astype(F32)
        routed = jnp.max(jnp.where(match, 1.0, 0.0), axis=1, keepdims=True)
        scale = jnp.sum(jnp.where(match, gates, 0.0), axis=1, keepdims=True)
        ordinal = across(routed, earlier)
        here = same_group & (across(routed, eye) > 0.5) & (ordinal_of_slot == ordinal)
        placed.append(jnp.where(here, 1.0, 0.0))
        scales.append(jnp.sum(jnp.where(here, across(scale, eye), 0.0), axis=1, keepdims=True))
    all_placed = jnp.concatenate(placed, axis=0).astype(BF16)
    taken = jnp.dot(all_placed, mixed, preferred_element_type=F32).astype(BF16)
    for e in range(experts):
        rows = slice(e * slots, (e + 1) * slots)
        placed_ref[e] = all_placed[rows]
        scale_ref[e] = jnp.broadcast_to(scales[e], scale_ref.shape[1:])
        gate_up = jnp.dot(taken[rows], w_ref[e], preferred_element_type=F32).astype(BF16)
        for j in range(2 * FFE // STAT):
            full_ref[e, j * slots : (j + 1) * slots, :] = gate_up[:, j * STAT : (j + 1) * STAT]
        slot_power = dot_nt(power_rows, placed_ref[e])
        full_ref[e, 2 * FFE // STAT * slots :, :] = jnp.concatenate(
            [slot_power, jnp.zeros((16, STAT - slots), F32)], axis=1
        ).astype(BF16)
    for k in range(groups):
        message_refs[k][...] = full_ref[me ^ k]


def hidden_kernel(*refs):
    out_ref = refs[-1]
    gate_up = refs[0][...].astype(F32)
    for ref in refs[1:-1]:
        gate_up = gate_up + ref[...].astype(F32)
    slots = out_ref.shape[0]
    chunks = FFE // STAT
    stats = gate_up[2 * chunks * slots :, :slots]
    power = stats[0:1] + (stats[1:2] + stats[2:3])
    eye = iota((slots, slots), 0) == iota((slots, slots), 1)
    power = jnp.sum(jnp.where(eye, power, 0.0), axis=1, keepdims=True)
    scale = lax.rsqrt(power / D + EPS)
    for j in range(chunks):
        gate = gate_up[j * slots : (j + 1) * slots] * scale
        up = gate_up[(chunks + j) * slots : (chunks + j + 1) * slots] * scale
        out_ref[:, j * STAT : (j + 1) * STAT] = (gate / (1.0 + jnp.exp(-gate)) * up).astype(BF16)


def down_kernel(groups, *refs):
    hidden_refs = refs[:groups]
    w_ref, placed_ref, scale_ref, send_ref, keep_ref = refs[groups:]
    me, core = lax.axis_index("req"), lax.axis_index("seq") % 2
    total = jnp.zeros((placed_ref.shape[2], w_ref.shape[2]), F32)
    for k, hidden_ref in enumerate(hidden_refs):
        expert = me ^ k
        produced = jnp.dot(hidden_ref[...], w_ref[expert], preferred_element_type=F32)
        total = total + lax.dot_general(
            placed_ref[expert],
            (produced * scale_ref[expert][:, :1]).astype(BF16),
            (((0,), (0,)), ((), ())),
            preferred_element_type=F32,
        )
    half = total.shape[0] // 2
    low, high = total[:half], total[half:]
    send_ref[...] = jnp.where(core == 0, high, low).astype(BF16)
    keep_ref[...] = jnp.where(core == 0, low, high)


def spread_kernel(keep_ref, arrived_ref, *out_refs):
    total = keep_ref[...] + arrived_ref[...].astype(F32)
    row_count = out_refs[0].shape[0]
    for k, out_ref in enumerate(out_refs):
        out_ref[...] = total[k * row_count : (k + 1) * row_count].astype(BF16)


def halve_kernel(resid_ref, *refs):
    arrived_refs, send_ref, keep_ref = refs[:-2], refs[-2], refs[-1]
    total = arrived_refs[0][...].astype(F32)
    for ref in arrived_refs[1:]:
        total = total + ref[...].astype(F32)
    width = total.shape[1] // 2
    left, right = total[:, :width], total[:, width:]
    first = lax.axis_index("seq") % 2 == 0
    send_ref[...] = jnp.where(first, right, left)
    keep_ref[...] = resid_ref[...] + jnp.where(first, left, right)


def final_kernel(keep_ref, arrived_ref, out_ref):
    total = keep_ref[...] + arrived_ref[...]
    for r in range(out_ref.shape[0]):
        out_ref[r] = total[r * NSTEP : (r + 1) * NSTEP].astype(BF16)


def staged(
    x_in,
    attn_gain,
    moe_gain,
    w_qkv,
    w_o,
    cache_k,
    cache_v,
    page_map,
    lengths,
    routes,
    route_weights,
    w_gate_up,
    w_down,
):
    requests = x_in.shape[0]
    row_count = requests * NSTEP
    members, groups = lax.axis_size("seq"), lax.axis_size("req")
    chips = members // 2
    heads = w_qkv.shape[1] // HD
    width = w_o.shape[1]

    heads_shape = jax.ShapeDtypeStruct((heads, row_count, 2 * HD), BF16)
    own_heads, x = kernel_call(
        project_kernel,
        [heads_shape, jax.ShapeDtypeStruct((row_count, 2 * width), F32)],
        [HBM] * 4,
        [
            pltpu.VMEM(x_in.shape, BF16),
            pltpu.VMEM((D,), F32),
            pltpu.VMEM((w_qkv.shape[1], D), BF16),
            pltpu.SMEM(lengths.shape, jnp.int32),
            pltpu.SemaphoreType.DMA((4,)),
        ],
        vmem_mib=60,
        cost=5.0,
    )(x_in, attn_gain, w_qkv.T, lengths)

    def gathered(own):
        return [own] + [swap(own, "seq", 2 * k) for k in range(1, chips)]

    near = gathered(own_heads)
    first = near[1]
    near[0], live, routing, gain = kernel_call(
        prepare_kernel,
        [
            heads_shape,
            jax.ShapeDtypeStruct((requests, cache_k.shape[1]), F32),
            jax.ShapeDtypeStruct((row_count, STAT), F32),
            jax.ShapeDtypeStruct((1, D), F32),
        ],
        [VMEM] + [SMEM] * 2 + [VMEM] * 3,
    )(after(own_heads, near[1]), page_map, lengths, routes, route_weights, moe_gain)
    near[1] = after(near[1], live)
    far = [swap(piece, "seq", 1) for piece in [after(own_heads, first)] + near[1:]]
    part_shape = jax.ShapeDtypeStruct((GROUP * row_count, WIDE), BF16)
    head_scratch = [
        pltpu.VMEM((2, chips, heads, row_count, 2 * HD), BF16),
        pltpu.VMEM((GROUP, row_count, KVD), F32),
        pltpu.VMEM((GROUP * row_count, WIDE), F32),
    ]
    part = kernel_call(
        lambda *refs: attend_kernel(chips, *refs),
        part_shape,
        [VMEM] * (2 * chips + 3),
        head_scratch,
    )(*near, *far, live, cache_k, cache_v)
    fresh = kernel_call(
        lambda *refs: fresh_kernel(chips, *refs),
        part_shape,
        [VMEM] * (2 * chips),
        head_scratch,
    )(*near, *far)
    near = gathered(part)
    near[1] = after(near[1], fresh)
    far = [swap(piece, "seq", 1) for piece in [after(part, near[1])] + near[1:]]
    packed, resid = kernel_call(
        lambda *refs: merge_kernel(members + 1, *refs),
        [
            jax.ShapeDtypeStruct((row_count, 2 * width + STAT), BF16),
            jax.ShapeDtypeStruct((row_count, width), F32),
        ],
        [VMEM] * (members + 6),
    )(*near, *far, fresh, x, gain, routing, w_o.T, swap(w_o.T, "seq", 1))

    everyone = [(p, c, q) for p in range(chips) for c in range(2) for q in range(groups)]

    def crossing(j):
        return [
            ((2 * p + c) * groups + q, (2 * (q ^ MASKS[c][j]) + 1 - c) * groups + p)
            for p, c, q in everyone
        ]

    def returning(j):
        return [
            ((2 * p + c) * groups + q, (2 * q + 1 - c) * groups + (p ^ MASKS[c][j]))
            for p, c, q in everyone
        ]

    place = ("seq", "req")
    near = [lax.ppermute(packed, place, crossing(j)) for j in range(groups // 2)]
    far = [swap(piece, "seq", 1) for piece in near]
    experts = w_gate_up.shape[0]
    slots = groups * CAP
    message = jax.ShapeDtypeStruct((2 * FFE // STAT * slots + 16, STAT), BF16)
    *messages, placed, scale = kernel_call(
        lambda *refs: gate_kernel(groups, *refs),
        [message] * groups
        + [
            jax.ShapeDtypeStruct((experts, slots, groups * row_count), BF16),
            jax.ShapeDtypeStruct((experts, slots, STAT), F32),
        ],
        [VMEM] * (groups + 1),
        [pltpu.VMEM((experts, *message.shape), BF16)],
    )(*near, *far, w_gate_up)
    sums = [messages[0]] + [swap(messages[k], "req", k) for k in (2, 1, 3)]
    hidden = kernel_call(
        hidden_kernel, jax.ShapeDtypeStruct((slots, FFE), BF16), [VMEM] * groups
    )(*sums)
    hiddens = [hidden] + [swap(hidden, "req", k) for k in range(1, groups)]
    half = (groups * row_count // 2, 2 * width)
    send, keep = kernel_call(
        lambda *refs: down_kernel(groups, *refs),
        [jax.ShapeDtypeStruct(half, BF16), jax.ShapeDtypeStruct(half, F32)],
        [VMEM] * (groups + 3),
    )(*hiddens, w_down, placed, scale)
    outs = kernel_call(
        spread_kernel,
        [jax.ShapeDtypeStruct((row_count, 2 * width), BF16)] * (groups // 2),
        [VMEM] * 2,
    )(keep, swap(send, "seq", 1))
    arrived = [lax.ppermute(out, place, returning(j)) for j, out in enumerate(outs)]
    send, keep = kernel_call(
        halve_kernel,
        [jax.ShapeDtypeStruct((row_count, width), F32)] * 2,
        [VMEM] * (1 + groups // 2),
    )(resid, *arrived)
    return kernel_call(
        final_kernel, jax.ShapeDtypeStruct((requests, NSTEP, width), BF16), [VMEM] * 2
    )(keep, swap(send, "seq", 1))


def local(*args):
    w_qkv, w_o, w_gate_up = args[3], args[4], args[11]
    members, groups = lax.axis_size("seq"), lax.axis_size("req")
    fits = (
        members == 8
        and groups == 4
        and w_qkv.shape[1] % HD == 0
        and w_gate_up.shape[0] == groups
        and (2 * w_o.shape[1]) % STAT == 0
    )
    return staged(*args) if fits else plain(*args)


def solution(mesh):
    in_specs = (
        P("req", None, None),
        P(),
        P(),
        P(None, "seq"),
        P(None, "seq"),
        P("req", "seq", None),
        P("req", "seq", None),
        P("req", "seq"),
        P("req"),
        P("req", None, None),
        P("req", None, None),
        P("seq", "req", None),
        P("seq", None, "req"),
    )
    out_specs = P("req", None, "seq")
    return jax.shard_map(local, mesh=mesh, in_specs=in_specs, out_specs=out_specs, check_vma=False)
```
